256 devices in a mesh: group: 4 (over y), vocab: 32 (over z, x), rows: 2 (over core).
Axes of the slice: x: 4, y: 4, z: 8, core: 2. Of those that a mesh axis runs over, the one named last changes fastest.
Arguments:
- teacher_logits: bfloat16 [768, 98304], P(None, ('group', 'vocab', 'rows')), may hold values from -240 to 240
- student_hidden: bfloat16 [768, 4096], P('rows'), may hold values from -70 to 70
- head_weight: bfloat16 [4096, 98304], P(None, ('group', 'vocab')), may hold values from -0.25 to 0.25
- sampled_ids: int32 [768], P('rows'), may hold values from 0 to 98303
- assignment: int32 [768], replicated, may hold values from 0 to 767, each once
- row_scale: float32 [768], P('rows'), may hold values from 64 to 640
Outputs:
- loss: float32 [1], replicated
- hidden_grad: bfloat16 [768, 4096], P('rows', ('group', 'vocab'))
- head_grad: bfloat16 [4096, 98304], P('rows', ('group', 'vocab'))
The draws below stay inside these ranges and needn't reach their ends.
Inputs may be any that keep to these rules, and one draw needn't show every extreme that they name: `assignment`: each of 0 to 767 appears once.
All inputs are finite; a program needn't handle non-finite values.
Results may differ from the reference program's by a relative error of at most 0.0015.
The reference program's roundings to bfloat16 on the way (of `grad_logits`) count: a program that leaves them out, or rounds other values in their place, can miss the bound.
Values may be sent and summed in bfloat16 or wider, within the bound.
No kernel may reach another device: no remote copies, remote signals or barrier semaphores. Data moves between devices by JAX's collectives and lax.ppermute only.
A program may use at most 128 MiB of HBM per device.

```python
import math
import jax
import jax.numpy as jnp

D = 4096
VOCAB = 98304
ROWS = 768


def draw_teacher_logits(key, part):
    key = jax.random.fold_in(key, 11)
    key_values = jax.random.fold_in(key, 0)
    values = 3.0 * jax.random.normal(key_values, (ROWS, VOCAB), jnp.float32)
    return jnp.clip(values, -15.0, 15.0).astype(jnp.bfloat16)


def draw_student_hidden(key, part):
    key = jax.random.fold_in(key, 23)
    key_values = jax.random.fold_in(key, 0)
    values = jax.random.normal(key_values, (ROWS, D), jnp.float32)
    return jnp.clip(values, -6.0, 6.0).astype(jnp.bfloat16)


def touch_ends(drawn, stream_key, smallest, top_value):
    extent = drawn.shape
    index_at = [jax.random.randint(jax.random.fold_in(stream_key, axis), (), 0, extent[axis]) for axis in range(len(extent))]
    drawn = drawn.at[tuple(index_at)].set(smallest)
    longest = extent.index(max(extent))
    index_at[longest] = (index_at[longest] + 1) % extent[longest]
    return drawn.at[tuple(index_at)].set(top_value)


def steps_of(own_key, dims, cuts, least, high):
    level = 1.0
    for axis_at, parts in cuts:
        draws = jax.random.uniform(jax.random.fold_in(jax.random.fold_in(own_key, 6), axis_at), (parts,), jnp.float32, least / len(cuts), high / len(cuts))
        level = level * jnp.repeat(jnp.exp(draws), dims[axis_at] // parts).reshape((-1,) + (1,) * (len(dims) - 1 - axis_at))
    return level


def noise(rng, extent, deviation, reach, shards=(), held_as=jnp.bfloat16):
    result = deviation * jax.random.normal(rng, extent, jnp.float32)
    if shards:
        result = result * steps_of(rng, extent, shards, -0.22, 0.18)
    return jnp.clip(result, -reach, reach).astype(held_as)


def setup_inputs(seed: int = 0) -> dict:
    keys = jax.random.split(jax.random.key(seed), 7)
    return {
        "teacher_logits": draw_teacher_logits(jax.random.fold_in(keys[6], 71), 0),
        "student_hidden": draw_student_hidden(jax.random.fold_in(keys[6], 71), 0),
        "head_weight": noise(keys[2], (D, VOCAB), (3.0 * D ** -0.5), 0.25, ((1, 128),)),
        "sampled_ids": touch_ends(jax.random.randint(keys[3], (ROWS,), 0, VOCAB), jax.random.fold_in(keys[3], 1), 0, VOCAB - 1).astype(jnp.int32),
        "assignment": jax.random.permutation(keys[4], ROWS).astype(jnp.int32),
        "row_scale": jnp.clip(jnp.exp(math.log(640.0) - 2.3025851 * jax.random.uniform(keys[5], (ROWS,), jnp.float32) ** steps_of(keys[5], (ROWS,), ((0, 2),), -0.2, 0.2)), 64.0, 640.0),
    }


CE_WEIGHT = 0.5


def reference(teacher_logits, student_hidden, head_weight, sampled_ids, assignment, row_scale):
    teacher_rows = jnp.take(teacher_logits, assignment, axis=0).astype(jnp.float32)
    logits = jnp.dot(student_hidden, head_weight, preferred_element_type=jnp.float32)
    norm_student = jax.nn.logsumexp(logits, axis=1)
    norm_teacher = jax.nn.logsumexp(teacher_rows, axis=1)
    prob_student = jnp.exp(logits - norm_student[:, None])
    prob_teacher = jnp.exp(teacher_rows - norm_teacher[:, None])
    divergence = jnp.sum(prob_teacher * (teacher_rows - logits), axis=1) - norm_teacher + norm_student
    picked = jnp.take_along_axis(logits, sampled_ids[:, None], axis=1)[:, 0]
    cross_entropy = norm_student - picked
    loss = jnp.mean(divergence + CE_WEIGHT * cross_entropy).reshape(1)
    sampled_hot = (jnp.arange(VOCAB, dtype=jnp.int32)[None, :] == sampled_ids[:, None]).astype(jnp.float32)
    grad_logits = (row_scale[:, None] * ((1.0 + CE_WEIGHT) * prob_student - prob_teacher - CE_WEIGHT * sampled_hot)).astype(jnp.bfloat16)
    hidden_grad = jnp.dot(grad_logits, head_weight.T, preferred_element_type=jnp.float32).astype(jnp.bfloat16)
    head_grad = jnp.dot(student_hidden.T, grad_logits, preferred_element_type=jnp.float32).astype(jnp.bfloat16)
    return loss, hidden_grad, head_grad
```

```python
import functools

import jax
import jax.numpy as jnp
from jax import lax
from jax.experimental import pallas as pl
from jax.experimental.pallas import tpu as pltpu
from jax.sharding import Mesh, PartitionSpec as P

CE_WEIGHT = 0.5
SEND_SCALE = 64.0
VMEM = 48 * 1024 * 1024
F32 = jnp.float32
BF16 = jnp.bfloat16
F16 = jnp.float16


def params(*semantics):
    return pltpu.CompilerParams(vmem_limit_bytes=VMEM, dimension_semantics=semantics or None)


def shift(a, axis, by):
    n = lax.axis_size(axis)
    return lax.ppermute(a, axis, [(i, (i + by) % n) for i in range(n)])


def logits_kernel(h_ref, w_ref, out_ref):
    k = pl.program_id(0)
    part = jnp.dot(h_ref[...], w_ref[...], preferred_element_type=F32)

    @pl.when(k == 0)
    def _():
        out_ref[...] = part

    @pl.when(k > 0)
    def _():
        out_ref[...] += part


def student_logits(hidden, head, steps=8):
    rows, depth = hidden.shape
    cols = head.shape[1]
    kb = depth // steps
    return pl.pallas_call(
        logits_kernel,
        out_shape=jax.ShapeDtypeStruct((rows, cols), F32),
        grid=(steps,),
        in_specs=[
            pl.BlockSpec((rows, kb), lambda k: (0, k)),
            pl.BlockSpec((kb, cols), lambda k: (k, 0)),
        ],
        out_specs=pl.BlockSpec((rows, cols), lambda k: (0, 0)),
        compiler_params=params("arbitrary"),
        cost_estimate=pl.CostEstimate(
            flops=2 * rows * depth * cols,
            bytes_accessed=2 * (rows * depth + depth * cols) + 4 * rows * cols,
            transcendentals=0,
        ),
        name="student_logits",
    )(hidden, head)


def stats_kernel(pos_ref, l_ref, own_ref, oth_ref, assign_ref, ids_ref, stats_ref, t_ref):
    rows, cols = l_ref.shape
    half = cols // 2
    total = own_ref.shape[0]
    pick = (lax.broadcasted_iota(jnp.int32, (rows, total), 1) == assign_ref[...]).astype(BF16)
    own = jnp.dot(pick, own_ref[...], preferred_element_type=F32)
    oth = jnp.dot(pick, oth_ref[...], preferred_element_type=F32)
    first = pos_ref[0] == 0
    teacher = jnp.concatenate([jnp.where(first, own, oth), jnp.where(first, oth, own)], axis=1)
    t_ref[...] = teacher.astype(BF16)
    logits = l_ref[...]
    top_s = jnp.max(logits, axis=1, keepdims=True)
    sum_s = jnp.sum(jnp.exp(logits - top_s), axis=1, keepdims=True)
    top_t = jnp.max(teacher, axis=1, keepdims=True)
    exp_t = jnp.exp(teacher - top_t)
    sum_t = jnp.sum(exp_t, axis=1, keepdims=True)
    cross = jnp.sum(exp_t * (teacher - logits), axis=1, keepdims=True)
    columns = pos_ref[1] + lax.broadcasted_iota(jnp.int32, (rows, cols), 1)
    picked = jnp.sum(jnp.where(columns == ids_ref[...], logits, 0.0), axis=1, keepdims=True)
    lane = lax.broadcasted_iota(jnp.int32, (rows, 128), 1)
    packed = jnp.zeros((rows, 128), F32)
    for at, value in enumerate((top_s, sum_s, top_t, sum_t, cross, picked)):
        packed = jnp.where(lane == at, value, packed)
    stats_ref[...] = packed.T[:8, :]


def local_stats(pos, logits, own, oth, assign, ids):
    rows, cols = logits.shape
    whole = pl.BlockSpec(memory_space=pltpu.VMEM)
    return pl.pallas_call(
        stats_kernel,
        out_shape=(
            jax.ShapeDtypeStruct((8, rows), F32),
            jax.ShapeDtypeStruct((rows, cols), BF16),
        ),
        in_specs=[pl.BlockSpec(memory_space=pltpu.SMEM)] + [whole] * 5,
        out_specs=(whole, whole),
        compiler_params=params(),
        cost_estimate=pl.CostEstimate(
            flops=2 * rows * cols * own.shape[0],
            bytes_accessed=4 * rows * cols + 4 * own.size + 2 * rows * cols,
            transcendentals=2 * rows * cols,
        ),
        name="local_stats",
    )(pos, logits, own, oth, assign, ids)


def merge(parts):
    row = lambda at: [p[at : at + 1, :] for p in parts]
    tops_s, sums_s, tops_t, sums_t, crosses, pickeds = (row(at) for at in range(6))
    top_s = functools.reduce(jnp.maximum, tops_s)
    top_t = functools.reduce(jnp.maximum, tops_t)
    scale_s = [jnp.exp(t - top_s) for t in tops_s]
    scale_t = [jnp.exp(t - top_t) for t in tops_t]
    add = lambda xs: functools.reduce(jnp.add, xs)
    return (
        top_s,
        add([a * b for a, b in zip(sums_s, scale_s)]),
        top_t,
        add([a * b for a, b in zip(sums_t, scale_t)]),
        add([a * b for a, b in zip(crosses, scale_t)]),
        add(pickeds),
    )


def merge_kernel(*refs):
    out = refs[-1]
    merged = merge([r[...] for r in refs[:-1]])
    out[...] = jnp.zeros_like(out)
    for at, value in enumerate(merged):
        out[at : at + 1, :] = value


def merge_stats(parts):
    whole = pl.BlockSpec(memory_space=pltpu.VMEM)
    return pl.pallas_call(
        merge_kernel,
        out_shape=jax.ShapeDtypeStruct(parts[0].shape, F32),
        in_specs=[whole] * len(parts),
        out_specs=whole,
        compiler_params=params(),
        name="merge_stats",
    )(*parts)


def grad_kernel(n_parts, pos_ref, l_ref, t_ref, ids_ref, scale_ref, *refs):
    parts, (g_ref, loss_ref) = refs[:n_parts], refs[n_parts:]
    rows, cols = l_ref.shape
    top_s, sum_s, top_t, sum_t, cross, picked = merge([p[...] for p in parts])
    norm_s = top_s + jnp.log(sum_s)
    norm_t = top_t + jnp.log(sum_t)
    terms = cross / sum_t - norm_t + norm_s + CE_WEIGHT * (norm_s - picked)
    loss_ref[...] = jnp.broadcast_to(jnp.sum(terms, axis=1, keepdims=True), loss_ref.shape)
    sub = lax.broadcasted_iota(jnp.int32, (128, rows), 0)
    turned = jnp.where(sub == 0, norm_s, jnp.where(sub == 1, norm_t, 0.0)).T
    norm_s, norm_t = turned[:, 0:1], turned[:, 1:2]
    columns = pos_ref[1] + lax.broadcasted_iota(jnp.int32, (rows, cols), 1)
    hot = jnp.where(columns == ids_ref[...], CE_WEIGHT, 0.0)
    prob_s = jnp.exp(l_ref[...] - norm_s)
    prob_t = jnp.exp(t_ref[...].astype(F32) - norm_t)
    g_ref[...] = (scale_ref[...] * ((1.0 + CE_WEIGHT) * prob_s - prob_t - hot)).astype(BF16)


def grad_logits(pos, logits, teacher, ids, scale, parts):
    rows, cols = logits.shape
    whole = pl.BlockSpec(memory_space=pltpu.VMEM)
    return pl.pallas_call(
        functools.partial(grad_kernel, len(parts)),
        out_shape=(
            jax.ShapeDtypeStruct((rows, cols), BF16),
            jax.ShapeDtypeStruct((8, 128), F32),
        ),
        in_specs=[pl.BlockSpec(memory_space=pltpu.SMEM)] + [whole] * (4 + len(parts)),
        out_specs=(whole, whole),
        compiler_params=params(),
        cost_estimate=pl.CostEstimate(
            flops=8 * rows * cols,
            bytes_accessed=8 * rows * cols,
            transcendentals=2 * rows * cols,
        ),
        name="grad_logits",
    )(pos, logits, teacher, ids, scale, *parts)


def hidden_kernel(nz, pos_ref, w_ref, g_ref, o1, o2, o3, o0):
    step = pl.program_id(0)
    w = w_ref[...].reshape(nz * 16, w_ref.shape[-1])
    part = lax.dot_general(w, g_ref[...], (((1,), (1,)), ((), ())), preferred_element_type=F32)
    z = pos_ref[4]

    def put(ref, value):
        for at in range(nz):
            ref[0, lax.rem(at - z + nz, nz)] = value[at * 16 : (at + 1) * 16].astype(ref.dtype)

    for k, ref in enumerate((o1, o2, o3, o0)):

        @pl.when(step // 4 == k)
        def _(ref=ref, k=k):
            put(ref, part * SEND_SCALE if k < 3 else part)


def hidden_part(pos, head6, g, first_x, half):
    ny, nz, nx, _, sub, cols = head6.shape
    rows = g.shape[0]

    def w_map(s, pos):
        far, near = (s // 4 + 1) % 4, s % 4
        dx, dy = (far, near) if first_x else (near, far)
        return ((pos[2] + dy) % ny, 0, (pos[3] + dx) % nx, half, 0, 0)

    def out_spec(k):
        return pl.BlockSpec(
            (1, nz, sub, rows), lambda s, pos: (jnp.clip(s - 4 * k, 0, 3), 0, 0, 0)
        )

    shape = (4, nz, sub, rows)
    return pl.pallas_call(
        functools.partial(hidden_kernel, nz),
        out_shape=[jax.ShapeDtypeStruct(shape, F32)] * 4,
        grid_spec=pltpu.PrefetchScalarGridSpec(
            num_scalar_prefetch=1,
            grid=(16,),
            in_specs=[
                pl.BlockSpec((1, nz, 1, 1, sub, cols), w_map),
                pl.BlockSpec((rows, cols), lambda s, pos: (0, 0)),
            ],
            out_specs=[out_spec(k) for k in range(4)],
        ),
        compiler_params=params("arbitrary"),
        cost_estimate=pl.CostEstimate(
            flops=rows * cols * ny * nz * nx * 2 * sub,
            bytes_accessed=head6.size + 8 * rows * ny * nz * nx * sub,
            transcendentals=0,
        ),
        name="hidden_part",
    )(pos, head6, g)


def head_kernel(pos_ref, own_ref, oth_ref, g_own_ref, g_oth_ref, out_ref):
    dims = (((0,), (0,)), ((), ()))
    total = lax.dot_general(own_ref[...], g_own_ref[...], dims, preferred_element_type=F32)
    total += lax.dot_general(oth_ref[...], g_oth_ref[...], dims, preferred_element_type=F32)
    out_ref[...] = total.astype(BF16)


def head_grad(pos, hidden, hidden_oth, g, g_oth, block=256):
    rows, depth = hidden.shape
    cols = g.shape[1]
    width = hidden_oth.shape[1]
    steps = width // block
    return pl.pallas_call(
        head_kernel,
        out_shape=jax.ShapeDtypeStruct((width, cols), BF16),
        grid_spec=pltpu.PrefetchScalarGridSpec(
            num_scalar_prefetch=1,
            grid=(steps,),
            in_specs=[
                pl.BlockSpec((rows, block), lambda i, pos: (0, pos[0] * steps + i)),
                pl.BlockSpec((rows, block), lambda i, pos: (0, i)),
                pl.BlockSpec((rows, cols), lambda i, pos: (0, 0)),
                pl.BlockSpec((rows, cols), lambda i, pos: (0, 0)),
            ],
            out_specs=pl.BlockSpec((block, cols), lambda i, pos: (i, 0)),
        ),
        compiler_params=params("arbitrary"),
        cost_estimate=pl.CostEstimate(
            flops=4 * rows * width * cols,
            bytes_accessed=4 * rows * width + 4 * rows * cols + 2 * width * cols,
            transcendentals=0,
        ),
        name="head_grad",
    )(pos, hidden, hidden_oth, g, g_oth)


def body(teacher, hidden, head, ids, assignment, row_scale):
    c, x, y, z = (lax.axis_index(a) for a in ("c", "x", "y", "z"))
    rows, depth = hidden.shape
    cols = head.shape[1]
    block = lax.axis_index(("y", "z", "x"))
    pos = jnp.stack([c, block * cols, y, x, z]).astype(jnp.int32)

    teacher_oth = shift(teacher, "c", 1)
    width = depth // 2
    hidden_oth = shift(lax.dynamic_slice(hidden, (0, (1 - c) * width), (rows, width)), "c", 1)
    assign = lax.dynamic_slice(assignment, (c * rows,), (rows,)).reshape(rows, 1)
    ids = ids.reshape(rows, 1)
    scale = row_scale.reshape(rows, 1)

    logits = student_logits(hidden, head)
    stats, teacher_rows = local_stats(pos, logits, teacher, teacher_oth, assign, ids)
    for axis in ("x", "y"):
        stats = merge_stats([stats] + [shift(stats, axis, d) for d in (1, 2, 3)])
    parts = [stats] + [shift(stats, "z", d) for d in range(1, 8)]
    g, loss_part = grad_logits(pos, logits, teacher_rows, ids, scale, parts)
    g_oth = shift(g, "c", 1)

    ny, nz, nx = (lax.axis_size(a) for a in ("y", "z", "x"))
    sub = depth // (ny * nz * nx) // 2
    head6 = head.reshape(ny, nz, nx, 2, sub, cols)

    def first_level(half, axis):
        *far, own = hidden_part(pos, head6, g, axis == "x", half)
        far = [shift(f.astype(F16), axis, d + 1) for d, f in enumerate(far)]
        return own, far

    own_a, far_a = first_level(0, "x")
    own_b, far_b = first_level(1, "y")
    add = lambda own, far: own + sum(f.astype(F32) for f in far) * (1.0 / SEND_SCALE)
    sum_a, sum_b = add(own_a, far_a), add(own_b, far_b)
    sum_a = sum_a[0] + sum(shift(sum_a[d], "y", d) for d in (1, 2, 3))
    sum_b = sum_b[0] + sum(shift(sum_b[d], "x", d) for d in (1, 2, 3))
    both = jnp.concatenate([sum_a, sum_b], axis=1)
    hidden_sum = both[0] + sum(shift(both[d], "z", d) for d in range(1, 8))
    hidden_grad = hidden_sum.T.astype(BF16)

    head_out = head_grad(pos, hidden, hidden_oth, g, g_oth)
    loss_all = loss_part + shift(loss_part, "c", 1)
    loss = loss_all[0, :1] / (2 * rows)
    return loss, hidden_grad, head_out


def solution(mesh):
    ny, nzx, nc = mesh.devices.shape
    nx = 4
    fine = Mesh(mesh.devices.reshape(ny, nzx // nx, nx, nc), ("y", "z", "x", "c"))
    vocab = ("y", "z", "x")
    in_specs = (
        P(None, vocab + ("c",)),
        P("c", None),
        P(None, vocab),
        P("c"),
        P(),
        P("c"),
    )
    out_specs = (P(), P("c", vocab), P("c", vocab))
    return jax.shard_map(body, mesh=fine, in_specs=in_specs, out_specs=out_specs, check_vma=False)
```

```python
import functools

import jax
import jax.numpy as jnp
from jax import lax
from jax.experimental import pallas as pl
from jax.experimental.pallas import tpu as pltpu
from jax.sharding import Mesh, PartitionSpec as P

CE_WEIGHT = 0.5
SEND_SCALE = 64.0
F32 = jnp.float32
BF16 = jnp.bfloat16
F16 = jnp.float16


WHOLE = pl.BlockSpec(memory_space=pltpu.VMEM)


def params(mib, *semantics):
    return pltpu.CompilerParams(
        vmem_limit_bytes=mib * 1024 * 1024, dimension_semantics=semantics or None
    )


def shift(a, axis, by):
    n = lax.axis_size(axis)
    return lax.ppermute(a, axis, [(i, (i + by) % n) for i in range(n)])


def logits_kernel(steps, h_ref, w_ref, out_ref, h_buf, w_buf, h_sem, w_sem):
    kb = w_buf.shape[1]

    def copies(k):
        at = pl.ds(k * kb, kb)
        return (
            pltpu.make_async_copy(h_ref.at[:, at], h_buf.at[k], h_sem.at[k]),
            pltpu.make_async_copy(w_ref.at[at], w_buf.at[k], w_sem.at[k]),
        )

    for k in range(steps):
        for copy in copies(k):
            copy.start()
    out_ref[...] = jnp.zeros_like(out_ref)

    def step(k, carry):
        for copy in copies(k):
            copy.wait()
        out_ref[...] += jnp.dot(h_buf[k], w_buf[k], preferred_element_type=F32)
        return carry

    lax.fori_loop(0, steps, step, 0)


def student_logits(hidden, head, steps=4):
    rows, depth = hidden.shape
    cols = head.shape[1]
    kb = depth // steps
    return pl.pallas_call(
        functools.partial(logits_kernel, steps),
        out_shape=jax.ShapeDtypeStruct((rows, cols), F32),
        in_specs=[pl.BlockSpec(memory_space=pl.ANY)] * 2,
        out_specs=WHOLE,
        scratch_shapes=[
            pltpu.VMEM((steps, rows, kb), BF16),
            pltpu.VMEM((steps, kb, cols), BF16),
            pltpu.SemaphoreType.DMA((steps,)),
            pltpu.SemaphoreType.DMA((steps,)),
        ],
        compiler_params=params(56),
        cost_estimate=pl.CostEstimate(
            flops=2 * rows * depth * cols,
            bytes_accessed=2 * (rows * depth + depth * cols) + 4 * rows * cols,
            transcendentals=0,
        ),
        name="student_logits",
    )(hidden, head)


def columns_of(*rows):
    n = rows[0].shape[1]
    sub = lax.broadcasted_iota(jnp.int32, (128, n), 0)
    packed = jnp.zeros((128, n), F32)
    for at, row in enumerate(rows):
        packed = jnp.where(sub == at, row.astype(F32), packed)
    turned = packed.T
    return [turned[:, at : at + 1] for at in range(len(rows))]


def stats_kernel(pos_ref, l_ref, own_ref, oth_ref, assign_ref, ids_ref, stats_ref, t_ref):
    rows, cols = l_ref.shape
    total = own_ref.shape[0]
    first = pos_ref[0] == 0
    assign = assign_ref[...]
    assign = jnp.where(first, assign[:, :rows], assign[:, rows:])
    assign, ids = columns_of(assign, ids_ref[...])
    lanes = lax.broadcasted_iota(jnp.int32, (rows, total), 1).astype(F32)
    pick = (lanes == assign).astype(BF16)
    own = jnp.dot(pick, own_ref[...], preferred_element_type=F32)
    oth = jnp.dot(pick, oth_ref[...], preferred_element_type=F32)
    teacher = jnp.concatenate([jnp.where(first, own, oth), jnp.where(first, oth, own)], axis=1)
    t_ref[...] = teacher.astype(BF16)
    logits = l_ref[...]
    top_s = jnp.max(logits, axis=1, keepdims=True)
    sum_s = jnp.sum(jnp.exp(logits - top_s), axis=1, keepdims=True)
    top_t = jnp.max(teacher, axis=1, keepdims=True)
    exp_t = jnp.exp(teacher - top_t)
    sum_t = jnp.sum(exp_t, axis=1, keepdims=True)
    cross = jnp.sum(exp_t * (teacher - logits), axis=1, keepdims=True)
    columns = pos_ref[1] + lax.broadcasted_iota(jnp.int32, (rows, cols), 1)
    hot = columns.astype(F32) == ids
    picked = jnp.sum(jnp.where(hot, logits, 0.0), axis=1, keepdims=True)
    lane = lax.broadcasted_iota(jnp.int32, (rows, 128), 1)
    packed = jnp.zeros((rows, 128), F32)
    for at, value in enumerate((top_s, sum_s, top_t, sum_t, cross, picked)):
        packed = jnp.where(lane == at, value, packed)
    stats_ref[...] = packed.T[:8, :]


def local_stats(pos, logits, own, oth, assign, ids):
    rows, cols = logits.shape
    return pl.pallas_call(
        stats_kernel,
        out_shape=(
            jax.ShapeDtypeStruct((8, rows), F32),
            jax.ShapeDtypeStruct((rows, cols), BF16),
        ),
        in_specs=[pl.BlockSpec(memory_space=pltpu.SMEM)] + [WHOLE] * 5,
        out_specs=(WHOLE, WHOLE),
        compiler_params=params(16),
        cost_estimate=pl.CostEstimate(
            flops=2 * rows * cols * own.shape[0],
            bytes_accessed=4 * rows * cols + 4 * own.size + 2 * rows * cols,
            transcendentals=2 * rows * cols,
        ),
        name="local_stats",
    )(pos, logits, own, oth, assign, ids)


def merge(refs):
    def row(at):
        return [r[:, at, :] if len(r.shape) == 3 else r[at : at + 1, :] for r in refs]

    def over(fold, reduce, values):
        return functools.reduce(fold, [reduce(v, axis=0, keepdims=True) for v in values])

    tops_s, sums_s, tops_t, sums_t, crosses, pickeds = (row(at) for at in range(6))
    top_s = over(jnp.maximum, jnp.max, tops_s)
    top_t = over(jnp.maximum, jnp.max, tops_t)
    scale_s = [jnp.exp(t - top_s) for t in tops_s]
    scale_t = [jnp.exp(t - top_t) for t in tops_t]
    total = lambda xs: over(jnp.add, jnp.sum, xs)
    times = lambda xs, ys: [a * b for a, b in zip(xs, ys)]
    return (
        top_s,
        total(times(sums_s, scale_s)),
        top_t,
        total(times(sums_t, scale_t)),
        total(times(crosses, scale_t)),
        total(pickeds),
    )


def merge_kernel(*refs):
    out = refs[-1]
    merged = merge(refs[:-1])
    out[...] = jnp.zeros_like(out)
    for at, value in enumerate(merged):
        out[at : at + 1, :] = value


def merge_stats(*parts):
    return pl.pallas_call(
        merge_kernel,
        out_shape=jax.ShapeDtypeStruct(parts[0].shape[-2:], F32),
        in_specs=[WHOLE] * len(parts),
        out_specs=WHOLE,
        compiler_params=params(16),
        name="merge_stats",
    )(*parts)


def grad_kernel(n_parts, pos_ref, l_ref, t_ref, ids_ref, scale_ref, *refs):
    parts, (g_ref, loss_ref) = refs[:n_parts], refs[n_parts:]
    rows, cols = l_ref.shape
    top_s, sum_s, top_t, sum_t, cross, picked = merge(parts)
    norm_s = top_s + jnp.log(sum_s)
    norm_t = top_t + jnp.log(sum_t)
    terms = cross / sum_t - norm_t + norm_s + CE_WEIGHT * (norm_s - picked)
    loss_ref[...] = jnp.broadcast_to(jnp.sum(terms, axis=1, keepdims=True), loss_ref.shape)
    norm_s, norm_t, ids, scale = columns_of(norm_s, norm_t, ids_ref[...], scale_ref[...])
    columns = pos_ref[1] + lax.broadcasted_iota(jnp.int32, (rows, cols), 1)
    hot = jnp.where(columns.astype(F32) == ids, CE_WEIGHT, 0.0)
    prob_s = jnp.exp(l_ref[...] - norm_s)
    prob_t = jnp.exp(t_ref[...].astype(F32) - norm_t)
    g_ref[...] = (scale * ((1.0 + CE_WEIGHT) * prob_s - prob_t - hot)).astype(BF16)


def grad_logits(pos, logits, teacher, ids, scale, parts):
    rows, cols = logits.shape
    return pl.pallas_call(
        functools.partial(grad_kernel, len(parts)),
        out_shape=(
            jax.ShapeDtypeStruct((rows, cols), BF16),
            jax.ShapeDtypeStruct((8, 128), F32),
        ),
        in_specs=[pl.BlockSpec(memory_space=pltpu.SMEM)] + [WHOLE] * (4 + len(parts)),
        out_specs=(WHOLE, WHOLE),
        compiler_params=params(16),
        cost_estimate=pl.CostEstimate(
            flops=8 * rows * cols,
            bytes_accessed=8 * rows * cols,
            transcendentals=2 * rows * cols,
        ),
        name="grad_logits",
    )(pos, logits, teacher, ids, scale, *parts)


def hidden_kernel(first_x, half, pos_ref, w_ref, g_ref, *outs):
    ny, nz, nx, _, sub, cols = w_ref.shape
    y, x, z = pos_ref[2], pos_ref[3], pos_ref[4]
    g = g_ref[...]
    first, second = (nx, ny) if first_x else (ny, nx)
    for k, out in enumerate(outs):
        far = (k + 1) % first
        if first_x:
            w = w_ref[:, :, lax.rem(x + far, nx), half]
        else:
            w = w_ref[lax.rem(y + far, ny), :, :, half]
        part = lax.dot_general(
            w.reshape(-1, cols), g, (((1,), (1,)), ((), ())), preferred_element_type=F32
        )
        if far:
            part = part * SEND_SCALE
        for a in range(second):
            for b in range(nz):
                at = (a * nz + b if first_x else b * nx + a) * sub
                near = lax.rem(a - (y if first_x else x) + second, second)
                out[near, lax.rem(b - z + nz, nz)] = part[at : at + sub]


def hidden_part(pos, head6, g, first_x, half):
    ny, nz, nx, _, sub, cols = head6.shape
    rows = g.shape[0]
    first, second = (nx, ny) if first_x else (ny, nx)
    shape = jax.ShapeDtypeStruct((second, nz, sub, rows), F32)
    return pl.pallas_call(
        functools.partial(hidden_kernel, first_x, half),
        out_shape=[shape] * first,
        in_specs=[pl.BlockSpec(memory_space=pltpu.SMEM), WHOLE, WHOLE],
        out_specs=[WHOLE] * first,
        compiler_params=params(16),
        cost_estimate=pl.CostEstimate(
            flops=rows * head6.size,
            bytes_accessed=head6.size + 4 * rows * first * second * nz * sub,
            transcendentals=0,
        ),
        name="hidden_part",
    )(pos, head6, g)


def head_kernel(pos_ref, own_ref, oth_ref, g_own_ref, g_oth_ref, out_ref):
    dims = (((0,), (0,)), ((), ()))
    total = lax.dot_general(own_ref[...], g_own_ref[...], dims, preferred_element_type=F32)
    total += lax.dot_general(oth_ref[...], g_oth_ref[...], dims, preferred_element_type=F32)
    out_ref[...] = total.astype(BF16)


def head_grad(pos, hidden, hidden_oth, g, g_oth, block=512):
    rows, depth = hidden.shape
    cols = g.shape[1]
    width = hidden_oth.shape[1]
    steps = width // block
    return pl.pallas_call(
        head_kernel,
        out_shape=jax.ShapeDtypeStruct((width, cols), BF16),
        grid_spec=pltpu.PrefetchScalarGridSpec(
            num_scalar_prefetch=1,
            grid=(steps,),
            in_specs=[
                pl.BlockSpec((rows, block), lambda i, pos: (0, pos[0] * steps + i)),
                pl.BlockSpec((rows, block), lambda i, pos: (0, i)),
                pl.BlockSpec((rows, cols), lambda i, pos: (0, 0)),
                pl.BlockSpec((rows, cols), lambda i, pos: (0, 0)),
            ],
            out_specs=pl.BlockSpec((block, cols), lambda i, pos: (i, 0)),
        ),
        compiler_params=params(24, "arbitrary"),
        cost_estimate=pl.CostEstimate(
            flops=4 * rows * width * cols,
            bytes_accessed=4 * rows * width + 4 * rows * cols + 2 * width * cols,
            transcendentals=0,
        ),
        name="head_grad",
    )(pos, hidden, hidden_oth, g, g_oth)


def body(teacher, hidden, head, ids, assignment, row_scale):
    c, x, y, z = (lax.axis_index(a) for a in ("c", "x", "y", "z"))
    rows, depth = hidden.shape
    cols = head.shape[1]
    block = lax.axis_index(("y", "z", "x"))
    pos = jnp.stack([c, block * cols, y, x, z]).astype(jnp.int32)

    teacher_oth = shift(teacher, "c", 1)
    width = depth // 2
    hidden_oth = shift(lax.dynamic_slice(hidden, (0, (1 - c) * width), (rows, width)), "c", 1)
    assign = assignment.reshape(1, -1)
    ids = ids.reshape(1, rows)
    scale = row_scale.reshape(1, rows)

    logits = student_logits(hidden, head)
    stats, teacher_rows = local_stats(pos, logits, teacher, teacher_oth, assign, ids)
    stats, hidden_oth = lax.optimization_barrier((stats, hidden_oth))
    ny, nz, nx = (lax.axis_size(a) for a in ("y", "z", "x"))
    stats = jnp.broadcast_to(stats[None], (nz * nx,) + stats.shape)
    stats = merge_stats(lax.all_to_all(stats, ("z", "x"), 0, 0, tiled=True))
    parts = [stats] + [shift(stats, "y", d) for d in range(1, ny)]
    g, loss_part = grad_logits(pos, logits, teacher_rows, ids, scale, parts)
    g_oth = shift(g, "c", 1)

    sub = depth // (ny * nz * nx) // 2
    head6 = head.reshape(ny, nz, nx, 2, sub, cols)

    def first_level(half, axis):
        *far, own = hidden_part(pos, head6, g, axis == "x", half)
        far = [shift(f.astype(F16), axis, d + 1) for d, f in enumerate(far)]
        return own, far

    own_a, far_a = first_level(0, "x")
    own_b, far_b = first_level(1, "y")
    head_out = head_grad(pos, hidden, hidden_oth, g, g_oth)
    far_a, far_b, head_out = lax.optimization_barrier((far_a, far_b, head_out))

    def add(own, far):
        return own + sum(f.astype(F32) for f in far) * (1.0 / SEND_SCALE)

    def level(chunks, axis):
        sent = [(chunks[d] * SEND_SCALE).astype(F16) for d in range(1, chunks.shape[0])]
        return add(chunks[0], [shift(f, axis, d + 1) for d, f in enumerate(sent)])

    sum_a = level(add(own_a, far_a), "y")
    sum_b = level(add(own_b, far_b), "x")
    hidden_sum = level(jnp.concatenate([sum_a, sum_b], axis=1), "z")
    hidden_grad = hidden_sum.T.astype(BF16)

    loss_all = loss_part + shift(loss_part, "c", 1)
    loss = loss_all[0, :1] / (2 * rows)
    return loss, hidden_grad, head_out


def solution(mesh):
    ny, nzx, nc = mesh.devices.shape
    nx = 4
    fine = Mesh(mesh.devices.reshape(ny, nzx // nx, nx, nc), ("y", "z", "x", "c"))
    vocab = ("y", "z", "x")
    in_specs = (
        P(None, vocab + ("c",)),
        P("c", None),
        P(None, vocab),
        P("c"),
        P(),
        P("c"),
    )
    out_specs = (P(), P("c", vocab), P("c", vocab))
    return jax.shard_map(body, mesh=fine, in_specs=in_specs, out_specs=out_specs, check_vma=False)
```

```python
import functools

import jax
import jax.numpy as jnp
from jax import lax
from jax.experimental import pallas as pl
from jax.experimental.pallas import tpu as pltpu
from jax.sharding import Mesh, PartitionSpec as P

CE_WEIGHT = 0.5
SEND_SCALE = 64.0
SPARE = 256
F32 = jnp.float32
BF16 = jnp.bfloat16
F16 = jnp.float16


WHOLE = pl.BlockSpec(memory_space=pltpu.VMEM)


def params(mib, *semantics):
    return pltpu.CompilerParams(
        vmem_limit_bytes=mib * 1024 * 1024, dimension_semantics=semantics or None
    )


def shift(a, axis, by):
    n = lax.axis_size(axis)
    return lax.ppermute(a, axis, [(i, (i + by) % n) for i in range(n)])


def logits_kernel(steps, h_ref, w_ref, out_ref, h_buf, w_buf, h_sem, w_sem):
    kb = w_buf.shape[1]

    def copies(k):
        at = pl.ds(k * kb, kb)
        return (
            pltpu.make_async_copy(h_ref.at[:, at], h_buf.at[k], h_sem.at[k]),
            pltpu.make_async_copy(w_ref.at[at], w_buf.at[k], w_sem.at[k]),
        )

    for k in range(steps):
        for copy in copies(k):
            copy.start()
    out_ref[...] = jnp.zeros_like(out_ref)

    def step(k, carry):
        for copy in copies(k):
            copy.wait()
        out_ref[...] += jnp.dot(h_buf[k], w_buf[k], preferred_element_type=F32)
        return carry

    lax.fori_loop(0, steps, step, 0)


def student_logits(hidden, head, steps=4):
    rows, depth = hidden.shape
    cols = head.shape[1]
    kb = depth // steps
    return pl.pallas_call(
        functools.partial(logits_kernel, steps),
        out_shape=jax.ShapeDtypeStruct((rows, cols), F32),
        in_specs=[pl.BlockSpec(memory_space=pl.ANY)] * 2,
        out_specs=WHOLE,
        scratch_shapes=[
            pltpu.VMEM((steps, rows, kb), BF16),
            pltpu.VMEM((steps, kb, cols), BF16),
            pltpu.SemaphoreType.DMA((steps,)),
            pltpu.SemaphoreType.DMA((steps,)),
        ],
        compiler_params=params(52),
        cost_estimate=pl.CostEstimate(
            flops=2 * rows * depth * cols,
            bytes_accessed=2 * (rows * depth + depth * cols) + 4 * rows * cols,
            transcendentals=0,
        ),
        name="student_logits",
    )(hidden, head)


def columns_of(*rows):
    n = rows[0].shape[1]
    sub = lax.broadcasted_iota(jnp.int32, (128, n), 0)
    packed = jnp.zeros((128, n), F32)
    for at, row in enumerate(rows):
        packed = jnp.where(sub == at, row.astype(F32), packed)
    turned = packed.T
    return [turned[:, at : at + 1] for at in range(len(rows))]


def stats_kernel(
    pos_ref, l_hbm, own_ref, oth_ref, assign_ref, ids_ref, stats_ref, t_ref, l_ref, l_sem
):
    rows, cols = l_ref.shape
    copy = pltpu.make_async_copy(l_hbm, l_ref, l_sem)
    copy.start()
    total = own_ref.shape[0]
    first = pos_ref[0] == 0
    assign = assign_ref[...]
    assign = jnp.where(first, assign[:, :rows], assign[:, rows:])
    assign, ids = columns_of(assign, ids_ref[...])
    lanes = lax.broadcasted_iota(jnp.int32, (rows, total), 1).astype(F32)
    pick = (lanes == assign).astype(BF16)
    own = jnp.dot(pick, own_ref[...], preferred_element_type=F32)
    oth = jnp.dot(pick, oth_ref[...], preferred_element_type=F32)
    teacher = jnp.concatenate([jnp.where(first, own, oth), jnp.where(first, oth, own)], axis=1)
    t_ref[...] = teacher.astype(BF16)
    copy.wait()
    logits = l_ref[...]
    top_s = jnp.max(logits, axis=1, keepdims=True)
    sum_s = jnp.sum(jnp.exp(logits - top_s), axis=1, keepdims=True)
    top_t = jnp.max(teacher, axis=1, keepdims=True)
    exp_t = jnp.exp(teacher - top_t)
    sum_t = jnp.sum(exp_t, axis=1, keepdims=True)
    cross = jnp.sum(exp_t * (teacher - logits), axis=1, keepdims=True)
    columns = pos_ref[1] + lax.broadcasted_iota(jnp.int32, (rows, cols), 1)
    hot = columns.astype(F32) == ids
    picked = jnp.sum(jnp.where(hot, logits, 0.0), axis=1, keepdims=True)
    lane = lax.broadcasted_iota(jnp.int32, (rows, 128), 1)
    packed = jnp.zeros((rows, 128), F32)
    for at, value in enumerate((top_s, sum_s, top_t, sum_t, cross, picked)):
        packed = jnp.where(lane == at, value, packed)
    packed = packed.T
    top_s, sum_s, top_t, sum_t, cross, picked = (packed[at : at + 1] for at in range(6))
    cross = cross / sum_t
    picked = jnp.sum(picked, axis=1, keepdims=True)
    spare = stats_ref.shape[1] - rows
    stats_ref[0:1, :rows] = top_s + jnp.log(sum_s)
    stats_ref[1:2, :rows] = top_t + jnp.log(sum_t)
    stats_ref[0:1, rows:] = cross[:, :spare]
    stats_ref[1:2, rows : 2 * rows - spare] = cross[:, spare:]
    lane = lax.broadcasted_iota(jnp.int32, (1, 2 * (spare - rows // 2)), 1)
    stats_ref[1:2, 2 * rows - spare :] = jnp.where(lane == 0, picked, 0.0)


def local_stats(pos, logits, own, oth, assign, ids):
    rows, cols = logits.shape
    return pl.pallas_call(
        stats_kernel,
        out_shape=(
            jax.ShapeDtypeStruct((2, rows + SPARE), F32),
            jax.ShapeDtypeStruct((rows, cols), BF16),
        ),
        in_specs=[pl.BlockSpec(memory_space=pltpu.SMEM), pl.BlockSpec(memory_space=pl.ANY)]
        + [WHOLE] * 4,
        out_specs=(WHOLE, WHOLE),
        scratch_shapes=[pltpu.VMEM((rows, cols), F32), pltpu.SemaphoreType.DMA],
        compiler_params=params(16),
        cost_estimate=pl.CostEstimate(
            flops=2 * rows * cols * own.shape[0],
            bytes_accessed=4 * rows * cols + 4 * own.size + 2 * rows * cols,
            transcendentals=2 * rows * cols,
        ),
        name="local_stats",
    )(pos, logits, own, oth, assign, ids)


def logsumexp(values):
    top = jnp.max(values, axis=0, keepdims=True)
    return top + jnp.log(jnp.sum(jnp.exp(values - top), axis=0, keepdims=True))


def grad_kernel(pos_ref, l_ref, t_ref, ids_ref, scale_ref, stats_ref, g_ref, loss_ref):
    rows, cols = l_ref.shape
    spare = stats_ref.shape[2] - rows
    norm_s = logsumexp(stats_ref[:, 0, :rows])
    block_t = stats_ref[:, 1, :rows]
    norm_t = logsumexp(block_t)
    share_t = jnp.exp(block_t - norm_t)
    far = 2 * rows - spare
    picked = jnp.sum(stats_ref[:, 1, far:], axis=0, keepdims=True)
    cross = jnp.concatenate([stats_ref[:, 0, rows:], stats_ref[:, 1, rows:far]], axis=1)
    cross = jnp.sum(cross * share_t, axis=0, keepdims=True)
    terms = cross - norm_t + (1.0 + CE_WEIGHT) * norm_s
    terms = jnp.sum(terms, axis=1, keepdims=True)
    terms -= CE_WEIGHT * jnp.sum(picked, axis=1, keepdims=True)
    loss_ref[...] = jnp.broadcast_to(terms, loss_ref.shape)
    norm_s, norm_t, ids, scale = columns_of(norm_s, norm_t, ids_ref[...], scale_ref[...])
    columns = pos_ref[1] + lax.broadcasted_iota(jnp.int32, (rows, cols), 1)
    hot = jnp.where(columns.astype(F32) == ids, CE_WEIGHT, 0.0)
    prob_s = jnp.exp(l_ref[...] - norm_s)
    prob_t = jnp.exp(t_ref[...].astype(F32) - norm_t)
    g_ref[...] = (scale * ((1.0 + CE_WEIGHT) * prob_s - prob_t - hot)).astype(BF16)


def grad_logits(pos, logits, teacher, ids, scale, stats):
    rows, cols = logits.shape
    return pl.pallas_call(
        grad_kernel,
        out_shape=(
            jax.ShapeDtypeStruct((rows, cols), BF16),
            jax.ShapeDtypeStruct((8, 128), F32),
        ),
        in_specs=[pl.BlockSpec(memory_space=pltpu.SMEM)] + [WHOLE] * 5,
        out_specs=(WHOLE, WHOLE),
        compiler_params=params(16),
        cost_estimate=pl.CostEstimate(
            flops=8 * rows * cols,
            bytes_accessed=8 * rows * cols,
            transcendentals=2 * rows * cols,
        ),
        name="grad_logits",
    )(pos, logits, teacher, ids, scale, stats)


def hidden_kernel(first_x, half, pos_ref, w_ref, g_ref, up, down, keep1, keep3, own):
    ny, nz, nx, _, sub, cols = w_ref.shape
    y, x = pos_ref[2], pos_ref[3]
    g = g_ref[...]
    slots = {
        1: (keep1.at[0], keep1.at[1], up.at[2], up.at[3]),
        2: (up.at[0], up.at[1], down.at[0], down.at[1]),
        3: (down.at[2], down.at[3], keep3.at[0], keep3.at[1]),
        0: tuple(own.at[near] for near in range(4)),
    }
    for far, places in slots.items():

        def block(near):
            dx, dy = (far, near) if first_x else (near, far)
            w = w_ref[lax.rem(y + dy, ny), :, lax.rem(x + dx, nx), half]
            return w.reshape(nz * sub, cols)

        w = jnp.concatenate([block(near) for near in range(4)], axis=0)
        part = lax.dot_general(
            w, g, (((1,), (1,)), ((), ())), preferred_element_type=F32
        )
        for near, place in enumerate(places):
            place[...] = part[near * nz * sub : (near + 1) * nz * sub].reshape(place.shape)


def hidden_part(pos, head6, g, first_x, half):
    ny, nz, nx, _, sub, cols = head6.shape
    rows = g.shape[0]
    shape = lambda n: jax.ShapeDtypeStruct((n, nz, sub, rows), F32)
    return pl.pallas_call(
        functools.partial(hidden_kernel, first_x, half),
        out_shape=[shape(4), shape(4), shape(2), shape(2), shape(4)],
        in_specs=[pl.BlockSpec(memory_space=pltpu.SMEM), WHOLE, WHOLE],
        out_specs=[WHOLE] * 5,
        compiler_params=params(16),
        cost_estimate=pl.CostEstimate(
            flops=rows * head6.size,
            bytes_accessed=head6.size + 2 * rows * ny * nz * nx * sub,
            transcendentals=0,
        ),
        name="hidden_part",
    )(pos, head6, g)


def head_kernel(pos_ref, own_ref, oth_ref, g_own_ref, g_oth_ref, out_ref, buf, sem):
    steps, block, _ = buf.shape
    g = jnp.concatenate([g_own_ref[...], g_oth_ref[...]], axis=0)
    copies = []
    for i in range(steps):
        at = pl.ds(pl.multiple_of(pos_ref[0] * (steps * block) + i * block, block), block)
        h = jnp.concatenate([own_ref[:, at], oth_ref[:, at]], axis=0)
        total = lax.dot_general(h, g, (((0,), (0,)), ((), ())), preferred_element_type=F32)
        buf[i] = total.astype(BF16)
        copy = pltpu.make_async_copy(buf.at[i], out_ref.at[pl.ds(i * block, block)], sem.at[i])
        copy.start()
        copies.append(copy)
    for copy in copies:
        copy.wait()


def head_grad(pos, hidden, hidden_oth, g, g_oth, steps=2):
    rows, depth = hidden.shape
    cols = g.shape[1]
    width = depth // 2
    return pl.pallas_call(
        head_kernel,
        out_shape=jax.ShapeDtypeStruct((width, cols), BF16),
        in_specs=[pl.BlockSpec(memory_space=pltpu.SMEM)] + [WHOLE] * 4,
        out_specs=pl.BlockSpec(memory_space=pl.ANY),
        scratch_shapes=[
            pltpu.VMEM((steps, width // steps, cols), BF16),
            pltpu.SemaphoreType.DMA((steps,)),
        ],
        compiler_params=params(20),
        cost_estimate=pl.CostEstimate(
            flops=4 * rows * width * cols,
            bytes_accessed=4 * rows * width + 4 * rows * cols + 2 * width * cols,
            transcendentals=0,
        ),
        name="head_grad",
    )(pos, hidden, hidden_oth, g, g_oth)


def body(teacher, hidden, head, ids, assignment, row_scale):
    c, x, y = (lax.axis_index(a) for a in ("c", "x", "y"))
    rows, depth = hidden.shape
    cols = head.shape[1]
    chips = ("y", "z", "x")
    ny, nz, nx = (lax.axis_size(a) for a in chips)
    pos = jnp.stack([c, lax.axis_index(chips) * cols, y, x]).astype(jnp.int32)
    assign = assignment.reshape(1, -1)
    ids = ids.reshape(1, rows)
    scale = row_scale.reshape(1, rows)

    teacher_oth = shift(teacher, "c", 1)
    logits = student_logits(hidden, head)
    stats, teacher_rows = local_stats(pos, logits, teacher, teacher_oth, assign, ids)
    hidden, head, stats = lax.optimization_barrier((hidden, head, stats))
    hidden_oth = shift(hidden, "c", 1)
    stats = jnp.broadcast_to(stats[None], (ny * nz * nx,) + stats.shape)
    stats = lax.all_to_all(stats, chips, 0, 0, tiled=True)
    stats, hidden_oth = lax.optimization_barrier((stats, hidden_oth))
    g, loss_part = grad_logits(pos, logits, teacher_rows, ids, scale, stats)
    g_oth = shift(g, "c", 1)

    sub = depth // (ny * nz * nx) // 2
    head6 = head.reshape(ny, nz, nx, 2, sub, cols)

    def send(value, axis, by):
        return shift((value * SEND_SCALE).astype(F16), axis, by)

    def taken(value):
        return value.astype(F32) * (1.0 / SEND_SCALE)

    def first_step(g, half, axis):
        up, down, c1, c3, c0 = hidden_part(pos, head6, g, axis == "x", half)
        up, down = ((v * SEND_SCALE).astype(F16) for v in (up, down))
        g, up, down = lax.optimization_barrier((g, up, down))
        return g, (c0, c1, c3), (shift(up, axis, 1), shift(down, axis, -1))

    def second_step(kept, got, axis):
        (c0, c1, c3), (up, down) = kept, got
        up2 = send(c1 + taken(up[:2]), axis, 1)
        down2 = send(c3 + taken(down[:2]), axis, -1)
        return c0[:2] + taken(down[2:]) + taken(up2), c0[2:] + taken(up[2:]) + taken(down2)

    g_then, kept_a, got_a = first_step(g, 0, "x")
    _, kept_b, got_b = first_step(g_then, 1, "y")
    head_out = head_grad(pos, hidden, hidden_oth, g, g_oth)
    got_a, got_b, head_out = lax.optimization_barrier((got_a, got_b, head_out))
    low_a, high_a = second_step(kept_a, got_a, "x")
    low_b, high_b = second_step(kept_b, got_b, "y")

    def second_level(low, high, axis):
        far = [send(f, axis, d) for d, f in ((2, high[0]), (1, low[1]), (3, high[1]))]
        return low[0] + sum(taken(f) for f in far)

    both = jnp.concatenate(
        [second_level(low_a, high_a, "y"), second_level(low_b, high_b, "x")], axis=1
    )
    both = lax.all_to_all((both * SEND_SCALE).astype(F16), "z", 0, 0, tiled=True)
    hidden_grad = jnp.sum(taken(both), axis=0).T.astype(BF16)

    loss_all = loss_part + shift(loss_part, "c", 1)
    loss = loss_all[0, :1] / (2 * rows)
    return loss, hidden_grad, head_out


def solution(mesh):
    ny, nzx, nc = mesh.devices.shape
    nx = 4
    fine = Mesh(mesh.devices.reshape(ny, nzx // nx, nx, nc), ("y", "z", "x", "c"))
    vocab = ("y", "z", "x")
    in_specs = (
        P(None, vocab + ("c",)),
        P("c", None),
        P(None, vocab),
        P("c"),
        P(),
        P("c"),
    )
    out_specs = (P(), P("c", vocab), P("c", vocab))
    return jax.shard_map(body, mesh=fine, in_specs=in_specs, out_specs=out_specs, check_vma=False)
```

```python
import functools

import jax
import jax.numpy as jnp
from jax import lax
from jax.experimental import pallas as pl
from jax.experimental.pallas import tpu as pltpu
from jax.sharding import Mesh, PartitionSpec as P

CE_WEIGHT = 0.5
SEND_SCALE = 64.0
SPARE = 256
F32 = jnp.float32
BF16 = jnp.bfloat16
F16 = jnp.float16


WHOLE = pl.BlockSpec(memory_space=pltpu.VMEM)


def params(mib, *semantics):
    return pltpu.CompilerParams(
        vmem_limit_bytes=mib * 1024 * 1024, dimension_semantics=semantics or None
    )


def shift(a, axis, by):
    n = lax.axis_size(axis)
    return lax.ppermute(a, axis, [(i, (i + by) % n) for i in range(n)])


def logits_kernel(steps, h_ref, w_ref, out_ref, h_buf, w_buf, h_sem, w_sem):
    kb = w_buf.shape[1]

    def copies(k):
        at = pl.ds(k * kb, kb)
        return (
            pltpu.make_async_copy(h_ref.at[:, at], h_buf.at[k], h_sem.at[k]),
            pltpu.make_async_copy(w_ref.at[at], w_buf.at[k], w_sem.at[k]),
        )

    for k in range(steps):
        for copy in copies(k):
            copy.start()
    out_ref[...] = jnp.zeros_like(out_ref)

    def step(k, carry):
        for copy in copies(k):
            copy.wait()
        out_ref[...] += jnp.dot(h_buf[k], w_buf[k], preferred_element_type=F32)
        return carry

    lax.fori_loop(0, steps, step, 0)


def student_logits(hidden, head, steps=4):
    rows, depth = hidden.shape
    cols = head.shape[1]
    kb = depth // steps
    return pl.pallas_call(
        functools.partial(logits_kernel, steps),
        out_shape=jax.ShapeDtypeStruct((rows, cols), F32),
        in_specs=[pl.BlockSpec(memory_space=pl.ANY)] * 2,
        out_specs=WHOLE,
        scratch_shapes=[
            pltpu.VMEM((steps, rows, kb), BF16),
            pltpu.VMEM((steps, kb, cols), BF16),
            pltpu.SemaphoreType.DMA((steps,)),
            pltpu.SemaphoreType.DMA((steps,)),
        ],
        compiler_params=params(52),
        cost_estimate=pl.CostEstimate(
            flops=2 * rows * depth * cols,
            bytes_accessed=2 * (rows * depth + depth * cols) + 4 * rows * cols,
            transcendentals=0,
        ),
        name="student_logits",
    )(hidden, head)


def columns_of(*rows):
    n = rows[0].shape[1]
    sub = lax.broadcasted_iota(jnp.int32, (128, n), 0)
    packed = jnp.zeros((128, n), F32)
    for at, row in enumerate(rows):
        packed = jnp.where(sub == at, row.astype(F32), packed)
    turned = packed.T
    return [turned[:, at : at + 1] for at in range(len(rows))]


def in_row(ref):
    return jnp.concatenate([ref[i : i + 1, :] for i in range(ref.shape[0])], axis=1)


def pack_stats(out_ref, lse_s, lse_t, cross, picked):
    rows = lse_s.shape[1]
    spare = out_ref.shape[1] - rows
    far = 2 * rows - spare
    out_ref[0:1, :rows] = lse_s
    out_ref[1:2, :rows] = lse_t
    out_ref[0:1, rows:] = cross[:, :spare]
    out_ref[1:2, rows:far] = cross[:, spare:]
    lane = lax.broadcasted_iota(jnp.int32, (1, out_ref.shape[1] - far), 1)
    out_ref[1:2, far:] = jnp.where(lane == 0, picked, 0.0)


def logsumexp(values):
    top = jnp.max(values, axis=0, keepdims=True)
    return top + jnp.log(jnp.sum(jnp.exp(values - top), axis=0, keepdims=True))


def merge(first, second):
    rows = first.shape[1] - SPARE
    far = 2 * rows - SPARE
    lse_s = logsumexp(first[:, :rows])
    lse_t = logsumexp(second[:, :rows])
    share_t = jnp.exp(second[:, :rows] - lse_t)
    cross = jnp.concatenate([first[:, rows:], second[:, rows:far]], axis=1)
    cross = jnp.sum(cross * share_t, axis=0, keepdims=True)
    picked = jnp.sum(second[:, far:], axis=0, keepdims=True)
    return lse_s, lse_t, cross, jnp.sum(picked, axis=1, keepdims=True)


def merge_kernel(in_ref, out_ref):
    pack_stats(out_ref, *merge(in_ref[:, 0, :], in_ref[:, 1, :]))


def merge_stats(stats):
    return pl.pallas_call(
        merge_kernel,
        out_shape=jax.ShapeDtypeStruct(stats.shape[1:], F32),
        in_specs=[WHOLE],
        out_specs=WHOLE,
        compiler_params=params(16),
        name="merge_stats",
    )(stats)


def stats_kernel(pos_ref, l_ref, own_ref, oth_ref, assign_ref, ids_ref, stats_ref, t_ref):
    rows, cols = l_ref.shape
    total = own_ref.shape[0]
    first = pos_ref[0] == 0
    assign = in_row(assign_ref)
    assign = jnp.where(first, assign[:, :rows], assign[:, rows:])
    assign, ids = columns_of(assign, in_row(ids_ref))
    lanes = lax.broadcasted_iota(jnp.int32, (rows, total), 1).astype(F32)
    pick = (lanes == assign).astype(BF16)
    own = jnp.dot(pick, own_ref[...], preferred_element_type=F32)
    oth = jnp.dot(pick, oth_ref[...], preferred_element_type=F32)
    teacher = jnp.concatenate([jnp.where(first, own, oth), jnp.where(first, oth, own)], axis=1)
    t_ref[...] = teacher.astype(BF16)
    logits = l_ref[...]
    top_s = jnp.max(logits, axis=1, keepdims=True)
    sum_s = jnp.sum(jnp.exp(logits - top_s), axis=1, keepdims=True)
    top_t = jnp.max(teacher, axis=1, keepdims=True)
    exp_t = jnp.exp(teacher - top_t)
    sum_t = jnp.sum(exp_t, axis=1, keepdims=True)
    cross = jnp.sum(exp_t * (teacher - logits), axis=1, keepdims=True)
    columns = pos_ref[1] + lax.broadcasted_iota(jnp.int32, (rows, cols), 1)
    hot = columns.astype(F32) == ids
    picked = jnp.sum(jnp.where(hot, logits, 0.0), axis=1, keepdims=True)
    lane = lax.broadcasted_iota(jnp.int32, (rows, 128), 1)
    packed = jnp.zeros((rows, 128), F32)
    for at, value in enumerate((top_s, sum_s, top_t, sum_t, cross, picked)):
        packed = jnp.where(lane == at, value, packed)
    packed = packed.T
    top_s, sum_s, top_t, sum_t, cross, picked = (packed[at : at + 1] for at in range(6))
    cross = cross / sum_t
    picked = jnp.sum(picked, axis=1, keepdims=True)
    pack_stats(stats_ref, top_s + jnp.log(sum_s), top_t + jnp.log(sum_t), cross, picked)


def local_stats(pos, logits, own, oth, assign, ids):
    rows, cols = logits.shape
    return pl.pallas_call(
        stats_kernel,
        out_shape=(
            jax.ShapeDtypeStruct((2, rows + SPARE), F32),
            jax.ShapeDtypeStruct((rows, cols), BF16),
        ),
        in_specs=[pl.BlockSpec(memory_space=pltpu.SMEM)] + [WHOLE] * 5,
        out_specs=(WHOLE, WHOLE),
        compiler_params=params(16),
        cost_estimate=pl.CostEstimate(
            flops=2 * rows * cols * own.shape[0],
            bytes_accessed=4 * rows * cols + 4 * own.size + 2 * rows * cols,
            transcendentals=2 * rows * cols,
        ),
        name="local_stats",
    )(pos, logits, own, oth, assign, ids)


def grad_kernel(pos_ref, l_ref, t_ref, ids_ref, scale_ref, s0, s1, s2, s3, g_ref, loss_ref):
    rows, cols = l_ref.shape
    parts = (s0, s1, s2, s3)
    first, second = (
        jnp.concatenate([part[at : at + 1, :] for part in parts], axis=0) for at in (0, 1)
    )
    norm_s, norm_t, cross, picked = merge(first, second)
    terms = cross - norm_t + (1.0 + CE_WEIGHT) * norm_s
    terms = jnp.sum(terms, axis=1, keepdims=True) - CE_WEIGHT * picked
    loss_ref[...] = jnp.broadcast_to(terms, loss_ref.shape)
    norm_s, norm_t, ids, scale = columns_of(norm_s, norm_t, in_row(ids_ref), in_row(scale_ref))
    columns = pos_ref[1] + lax.broadcasted_iota(jnp.int32, (rows, cols), 1)
    hot = jnp.where(columns.astype(F32) == ids, CE_WEIGHT, 0.0)
    prob_s = jnp.exp(l_ref[...] - norm_s)
    prob_t = jnp.exp(t_ref[...].astype(F32) - norm_t)
    g_ref[...] = (scale * ((1.0 + CE_WEIGHT) * prob_s - prob_t - hot)).astype(BF16)


def grad_logits(pos, logits, teacher, ids, scale, parts):
    rows, cols = logits.shape
    return pl.pallas_call(
        grad_kernel,
        out_shape=(
            jax.ShapeDtypeStruct((rows, cols), BF16),
            jax.ShapeDtypeStruct((8, 128), F32),
        ),
        in_specs=[pl.BlockSpec(memory_space=pltpu.SMEM)] + [WHOLE] * 8,
        out_specs=(WHOLE, WHOLE),
        compiler_params=params(16),
        cost_estimate=pl.CostEstimate(
            flops=8 * rows * cols,
            bytes_accessed=8 * rows * cols,
            transcendentals=2 * rows * cols,
        ),
        name="grad_logits",
    )(pos, logits, teacher, ids, scale, *parts)


def hidden_kernel(first_x, half, pos_ref, w_ref, g_ref, up, down, keep1, keep3, own):
    ny, nz, nx, _, sub, cols = w_ref.shape
    y, x = pos_ref[2], pos_ref[3]
    g = g_ref[...]
    slots = {
        1: (keep1.at[0], keep1.at[1], up.at[2], up.at[3]),
        2: (up.at[0], up.at[1], down.at[0], down.at[1]),
        3: (down.at[2], down.at[3], keep3.at[0], keep3.at[1]),
        0: tuple(own.at[near] for near in range(4)),
    }
    for far, places in slots.items():

        def block(near):
            dx, dy = (far, near) if first_x else (near, far)
            w = w_ref[lax.rem(y + dy, ny), :, lax.rem(x + dx, nx), half]
            return w.reshape(nz * sub, cols)

        w = jnp.concatenate([block(near) for near in range(4)], axis=0)
        part = lax.dot_general(
            w, g, (((1,), (1,)), ((), ())), preferred_element_type=F32
        )
        for near, place in enumerate(places):
            place[...] = part[near * nz * sub : (near + 1) * nz * sub].reshape(place.shape)


def hidden_part(pos, head6, g, first_x, half):
    ny, nz, nx, _, sub, cols = head6.shape
    rows = g.shape[0]
    shape = lambda n: jax.ShapeDtypeStruct((n, nz, sub, rows), F32)
    return pl.pallas_call(
        functools.partial(hidden_kernel, first_x, half),
        out_shape=[shape(4), shape(4), shape(2), shape(2), shape(4)],
        in_specs=[pl.BlockSpec(memory_space=pltpu.SMEM), WHOLE, WHOLE],
        out_specs=[WHOLE] * 5,
        compiler_params=params(16),
        cost_estimate=pl.CostEstimate(
            flops=rows * head6.size,
            bytes_accessed=head6.size + 2 * rows * ny * nz * nx * sub,
            transcendentals=0,
        ),
        name="hidden_part",
    )(pos, head6, g)


def head_kernel(pos_ref, own_ref, oth_ref, g_own_ref, g_oth_ref, out_ref, buf, sem):
    steps, block, _ = buf.shape
    g = jnp.concatenate([g_own_ref[...], g_oth_ref[...]], axis=0)
    copies = []
    for i in range(steps):
        at = pl.ds(pl.multiple_of(pos_ref[0] * (steps * block) + i * block, block), block)
        h = jnp.concatenate([own_ref[:, at], oth_ref[:, at]], axis=0)
        total = lax.dot_general(h, g, (((0,), (0,)), ((), ())), preferred_element_type=F32)
        buf[i] = total.astype(BF16)
        copy = pltpu.make_async_copy(buf.at[i], out_ref.at[pl.ds(i * block, block)], sem.at[i])
        copy.start()
        copies.append(copy)
    for copy in copies:
        copy.wait()


def head_grad(pos, hidden, hidden_oth, g, g_oth, steps=2):
    rows, depth = hidden.shape
    cols = g.shape[1]
    width = depth // 2
    return pl.pallas_call(
        head_kernel,
        out_shape=jax.ShapeDtypeStruct((width, cols), BF16),
        in_specs=[pl.BlockSpec(memory_space=pltpu.SMEM)] + [WHOLE] * 4,
        out_specs=pl.BlockSpec(memory_space=pl.ANY),
        scratch_shapes=[
            pltpu.VMEM((steps, width // steps, cols), BF16),
            pltpu.SemaphoreType.DMA((steps,)),
        ],
        compiler_params=params(20),
        cost_estimate=pl.CostEstimate(
            flops=4 * rows * width * cols,
            bytes_accessed=4 * rows * width + 4 * rows * cols + 2 * width * cols,
            transcendentals=0,
        ),
        name="head_grad",
    )(pos, hidden, hidden_oth, g, g_oth)


def body(teacher, hidden, head, ids, assignment, row_scale):
    c, x, y = (lax.axis_index(a) for a in ("c", "x", "y"))
    rows, depth = hidden.shape
    cols = head.shape[1]
    chips = ("y", "z", "x")
    ny, nz, nx = (lax.axis_size(a) for a in chips)
    pos = jnp.stack([c, lax.axis_index(chips) * cols, y, x]).astype(jnp.int32)
    assign = assignment.reshape(-1, 128)
    ids = ids.reshape(-1, 128)
    scale = row_scale.reshape(-1, 128)

    teacher_oth = shift(teacher, "c", 1)
    logits = student_logits(hidden, head)
    stats, teacher_rows = local_stats(pos, logits, teacher, teacher_oth, assign, ids)
    stats, scale = lax.optimization_barrier((stats, scale))
    stats = jnp.broadcast_to(stats[None], (nz * nx,) + stats.shape)
    stats = merge_stats(lax.all_to_all(stats, ("z", "x"), 0, 0, tiled=True))
    parts = [stats] + [shift(stats, "y", d) for d in (2, 1, 3)]
    hidden_oth = shift(lax.optimization_barrier((hidden, stats))[0], "c", 1)
    g, loss_part = grad_logits(pos, logits, teacher_rows, ids, scale, parts)
    g_oth = shift(g, "c", 1)

    sub = depth // (ny * nz * nx) // 2
    head6 = head.reshape(ny, nz, nx, 2, sub, cols)

    def send(value, axis, by):
        return shift((value * SEND_SCALE).astype(F16), axis, by)

    def taken(value):
        return value.astype(F32) * (1.0 / SEND_SCALE)

    def first_step(g, half, axis):
        up, down, c1, c3, c0 = hidden_part(pos, head6, g, axis == "x", half)
        up, down = ((v * SEND_SCALE).astype(F16) for v in (up, down))
        g, up, down = lax.optimization_barrier((g, up, down))
        return g, (c0, c1, c3), (shift(up, axis, 1), shift(down, axis, -1))

    def second_step(kept, got, axis):
        (c0, c1, c3), (up, down) = kept, got
        up2 = send(c1 + taken(up[:2]), axis, 1)
        down2 = send(c3 + taken(down[:2]), axis, -1)
        return c0[:2] + taken(down[2:]) + taken(up2), c0[2:] + taken(up[2:]) + taken(down2)

    g_then, kept_a, got_a = first_step(g, 0, "x")
    _, kept_b, got_b = first_step(g_then, 1, "y")
    head_out = head_grad(pos, hidden, hidden_oth, g, g_oth)
    loss_all = loss_part + shift(loss_part, "c", 1)
    got_a, _, loss_all = lax.optimization_barrier((got_a, head_out, loss_all))
    got_b, head_out = lax.optimization_barrier((got_b, head_out))
    low_a, high_a = second_step(kept_a, got_a, "x")
    low_b, high_b = second_step(kept_b, got_b, "y")

    def second_level(low, high, axis):
        far = [send(f, axis, d) for d, f in ((2, high[0]), (1, low[1]), (3, high[1]))]
        return low[0] + sum(taken(f) for f in far)

    both = jnp.concatenate(
        [second_level(low_a, high_a, "y"), second_level(low_b, high_b, "x")], axis=1
    )
    both = lax.all_to_all((both * SEND_SCALE).astype(F16), "z", 0, 0, tiled=True)
    hidden_grad = jnp.sum(taken(both), axis=0).T.astype(BF16)

    loss = loss_all[0, :1] / (2 * rows)
    return loss, hidden_grad, head_out


def solution(mesh):
    ny, nzx, nc = mesh.devices.shape
    nx = 4
    fine = Mesh(mesh.devices.reshape(ny, nzx // nx, nx, nc), ("y", "z", "x", "c"))
    vocab = ("y", "z", "x")
    in_specs = (
        P(None, vocab + ("c",)),
        P("c", None),
        P(None, vocab),
        P("c"),
        P(),
        P("c"),
    )
    out_specs = (P(), P("c", vocab), P("c", vocab))
    return jax.shard_map(body, mesh=fine, in_specs=in_specs, out_specs=out_specs, check_vma=False)
```

```python
import functools

import jax
import jax.numpy as jnp
from jax import lax
from jax.experimental import pallas as pl
from jax.experimental.pallas import tpu as pltpu
from jax.sharding import Mesh, PartitionSpec as P

CE_WEIGHT = 0.5
SEND_SCALE = 64.0
SPARE = 256
LOSS_ROWS = 16
F32 = jnp.float32
BF16 = jnp.bfloat16
F16 = jnp.float16


LIGHT = pl.CostEstimate(flops=1, bytes_accessed=1, transcendentals=0)
WHOLE = pl.BlockSpec(memory_space=pltpu.VMEM)


def params(mib, *semantics):
    return pltpu.CompilerParams(
        vmem_limit_bytes=mib * 1024 * 1024, dimension_semantics=semantics or None
    )


def shift(a, axis, by):
    n = lax.axis_size(axis)
    return lax.ppermute(a, axis, [(i, (i + by) % n) for i in range(n)])


def logits_kernel(steps, h_ref, w_ref, out_ref, h_buf, w_buf, h_sem, w_sem):
    kb = w_buf.shape[1]

    def copies(k):
        at = pl.ds(k * kb, kb)
        return (
            pltpu.make_async_copy(h_ref.at[:, at], h_buf.at[k], h_sem.at[k]),
            pltpu.make_async_copy(w_ref.at[at], w_buf.at[k], w_sem.at[k]),
        )

    for k in range(steps):
        for copy in copies(k):
            copy.start()
    out_ref[...] = jnp.zeros_like(out_ref)

    def step(k, carry):
        for copy in copies(k):
            copy.wait()
        out_ref[...] += jnp.dot(h_buf[k], w_buf[k], preferred_element_type=F32)
        return carry

    lax.fori_loop(0, steps, step, 0)


def student_logits(hidden, head, steps=4):
    rows, depth = hidden.shape
    cols = head.shape[1]
    kb = depth // steps
    return pl.pallas_call(
        functools.partial(logits_kernel, steps),
        out_shape=jax.ShapeDtypeStruct((rows, cols), F32),
        in_specs=[pl.BlockSpec(memory_space=pl.ANY)] * 2,
        out_specs=WHOLE,
        scratch_shapes=[
            pltpu.VMEM((steps, rows, kb), BF16),
            pltpu.VMEM((steps, kb, cols), BF16),
            pltpu.SemaphoreType.DMA((steps,)),
            pltpu.SemaphoreType.DMA((steps,)),
        ],
        compiler_params=params(52),
        cost_estimate=pl.CostEstimate(
            flops=2 * rows * depth * cols,
            bytes_accessed=2 * (rows * depth + depth * cols) + 4 * rows * cols,
            transcendentals=0,
        ),
        name="student_logits",
    )(hidden, head)


def columns_of(*rows):
    n = rows[0].shape[1]
    sub = lax.broadcasted_iota(jnp.int32, (128, n), 0)
    packed = jnp.zeros((128, n), F32)
    for at, row in enumerate(rows):
        packed = jnp.where(sub == at, row.astype(F32), packed)
    turned = packed.T
    return [turned[:, at : at + 1] for at in range(len(rows))]


def in_row(ref):
    return jnp.concatenate([ref[i : i + 1, :] for i in range(ref.shape[0])], axis=1)


def pack_stats(out_ref, lse_s, lse_t, cross, picked):
    rows = lse_s.shape[1]
    spare = out_ref.shape[1] - rows
    far = 2 * rows - spare
    out_ref[0:1, :rows] = lse_s
    out_ref[1:2, :rows] = lse_t
    out_ref[0:1, rows:] = cross[:, :spare]
    out_ref[1:2, rows:far] = cross[:, spare:]
    lane = lax.broadcasted_iota(jnp.int32, (1, out_ref.shape[1] - far), 1)
    out_ref[1:2, far:] = jnp.where(lane == 0, picked, 0.0)


def logsumexp(values):
    top = jnp.max(values, axis=0, keepdims=True)
    return top + jnp.log(jnp.sum(jnp.exp(values - top), axis=0, keepdims=True))


def merge(first, second):
    rows = first.shape[1] - SPARE
    far = 2 * rows - SPARE
    lse_s = logsumexp(first[:, :rows])
    lse_t = logsumexp(second[:, :rows])
    share_t = jnp.exp(second[:, :rows] - lse_t)
    cross = jnp.concatenate([first[:, rows:], second[:, rows:far]], axis=1)
    cross = jnp.sum(cross * share_t, axis=0, keepdims=True)
    picked = jnp.sum(second[:, far:], axis=0, keepdims=True)
    return lse_s, lse_t, cross, jnp.sum(picked, axis=1, keepdims=True)


def merge_kernel(in_ref, out_ref):
    pack_stats(out_ref, *merge(in_ref[:, 0, :], in_ref[:, 1, :]))


def merge_stats(stats):
    return pl.pallas_call(
        merge_kernel,
        out_shape=jax.ShapeDtypeStruct(stats.shape[1:], F32),
        in_specs=[WHOLE],
        out_specs=WHOLE,
        compiler_params=params(16),
        name="merge_stats",
    )(stats)


def stats_kernel(pos_ref, l_ref, own_ref, oth_ref, assign_ref, ids_ref, stats_ref, t_ref):
    rows, cols = l_ref.shape
    total = own_ref.shape[0]
    first = pos_ref[0] == 0
    assign = in_row(assign_ref)
    assign = jnp.where(first, assign[:, :rows], assign[:, rows:])
    assign, ids = columns_of(assign, in_row(ids_ref))
    lanes = lax.broadcasted_iota(jnp.int32, (rows, total), 1).astype(F32)
    pick = (lanes == assign).astype(BF16)
    own = jnp.dot(pick, own_ref[...], preferred_element_type=F32)
    oth = jnp.dot(pick, oth_ref[...], preferred_element_type=F32)
    teacher = jnp.concatenate([jnp.where(first, own, oth), jnp.where(first, oth, own)], axis=1)
    t_ref[...] = teacher.astype(BF16)
    logits = l_ref[...]
    top_s = jnp.max(logits, axis=1, keepdims=True)
    sum_s = jnp.sum(jnp.exp(logits - top_s), axis=1, keepdims=True)
    top_t = jnp.max(teacher, axis=1, keepdims=True)
    exp_t = jnp.exp(teacher - top_t)
    sum_t = jnp.sum(exp_t, axis=1, keepdims=True)
    cross = jnp.sum(exp_t * (teacher - logits), axis=1, keepdims=True)
    columns = pos_ref[1] + lax.broadcasted_iota(jnp.int32, (rows, cols), 1)
    hot = columns.astype(F32) == ids
    picked = jnp.sum(jnp.where(hot, logits, 0.0), axis=1, keepdims=True)
    lane = lax.broadcasted_iota(jnp.int32, (rows, 128), 1)
    packed = jnp.zeros((rows, 128), F32)
    for at, value in enumerate((top_s, sum_s, top_t, sum_t, cross, picked)):
        packed = jnp.where(lane == at, value, packed)
    packed = packed.T
    top_s, sum_s, top_t, sum_t, cross, picked = (packed[at : at + 1] for at in range(6))
    cross = cross / sum_t
    picked = jnp.sum(picked, axis=1, keepdims=True)
    pack_stats(stats_ref, top_s + jnp.log(sum_s), top_t + jnp.log(sum_t), cross, picked)


def local_stats(pos, logits, own, oth, assign, ids):
    rows, cols = logits.shape
    return pl.pallas_call(
        stats_kernel,
        out_shape=(
            jax.ShapeDtypeStruct((2, rows + SPARE), F32),
            jax.ShapeDtypeStruct((rows, cols), BF16),
        ),
        in_specs=[pl.BlockSpec(memory_space=pltpu.SMEM)] + [WHOLE] * 5,
        out_specs=(WHOLE, WHOLE),
        compiler_params=params(16),
        cost_estimate=pl.CostEstimate(
            flops=2 * rows * cols * own.shape[0],
            bytes_accessed=4 * rows * cols + 4 * own.size + 2 * rows * cols,
            transcendentals=2 * rows * cols,
        ),
        name="local_stats",
    )(pos, logits, own, oth, assign, ids)


def grad_kernel(pos_ref, l_ref, t_ref, ids_ref, scale_ref, s0, s1, s2, s3, g_ref):
    rows, cols = l_ref.shape
    parts = (s0, s1, s2, s3)
    first, second = (
        jnp.concatenate([part[at : at + 1, :] for part in parts], axis=0) for at in (0, 1)
    )
    norm_s, norm_t, cross, picked = merge(first, second)
    terms = cross - norm_t + (1.0 + CE_WEIGHT) * norm_s
    terms = jnp.sum(terms, axis=1, keepdims=True) - CE_WEIGHT * picked
    high = terms.astype(BF16).astype(F32)
    middle = (terms - high).astype(BF16).astype(F32)
    low = terms - high - middle
    at = lax.broadcasted_iota(jnp.int32, (LOSS_ROWS, cols), 0)
    tail = jnp.where(at == 0, high, jnp.where(at == 1, middle, jnp.where(at == 2, low, 0.0)))
    g_ref[rows:, :] = tail.astype(BF16)
    norm_s, norm_t, ids, scale = columns_of(norm_s, norm_t, in_row(ids_ref), in_row(scale_ref))
    columns = pos_ref[1] + lax.broadcasted_iota(jnp.int32, (rows, cols), 1)
    hot = jnp.where(columns.astype(F32) == ids, CE_WEIGHT, 0.0)
    prob_s = jnp.exp(l_ref[...] - norm_s)
    prob_t = jnp.exp(t_ref[...].astype(F32) - norm_t)
    g_ref[:rows, :] = (scale * ((1.0 + CE_WEIGHT) * prob_s - prob_t - hot)).astype(BF16)


def grad_logits(pos, logits, teacher, ids, scale, parts):
    rows, cols = logits.shape
    return pl.pallas_call(
        grad_kernel,
        out_shape=jax.ShapeDtypeStruct((rows + LOSS_ROWS, cols), BF16),
        in_specs=[pl.BlockSpec(memory_space=pltpu.SMEM)] + [WHOLE] * 8,
        out_specs=WHOLE,
        compiler_params=params(16),
        cost_estimate=pl.CostEstimate(
            flops=8 * rows * cols,
            bytes_accessed=8 * rows * cols,
            transcendentals=2 * rows * cols,
        ),
        name="grad_logits",
    )(pos, logits, teacher, ids, scale, *parts)


SENT = (((2, 0), (2, 1), (1, 2), (1, 3)), ((2, 2), (2, 3), (3, 0), (3, 1)))
KEPT = (((1, 0), (1, 1)), ((3, 2), (3, 3)), ((0, 0), (0, 1), (0, 2), (0, 3)))


def hidden_kernel(groups, pos_ref, w_ref, g_ref, *outs):
    ny, nz, nx, _, sub, cols = w_ref.shape
    y, x = pos_ref[2], pos_ref[3]
    g = g_ref[: outs[0].shape[-1], :]

    def block(part, far, near):
        dy, dx = (near, far) if part == 0 else (far, near)
        w = w_ref[lax.rem(y + dy, ny), :, lax.rem(x + dx, nx), part]
        return w.reshape(nz * sub, cols)

    for at, out in enumerate(outs):
        part, names = divmod(at, len(groups))
        names = groups[names]
        w = jnp.concatenate([block(part, *name) for name in names], axis=0)
        product = lax.dot_general(w, g, (((1,), (1,)), ((), ())), preferred_element_type=F32)
        out[...] = product.reshape(out.shape)


def hidden_part(pos, head6, g, groups):
    _, nz, _, _, sub, cols = head6.shape
    rows = g.shape[0] - LOSS_ROWS
    out_shape = [
        jax.ShapeDtypeStruct((len(names), nz, sub, rows), F32) for _ in range(2) for names in groups
    ]
    return pl.pallas_call(
        functools.partial(hidden_kernel, groups),
        out_shape=out_shape,
        in_specs=[pl.BlockSpec(memory_space=pltpu.SMEM), WHOLE, WHOLE],
        out_specs=[WHOLE] * len(out_shape),
        compiler_params=params(16),
        cost_estimate=LIGHT,
        name="hidden_part",
    )(pos, head6, g)


def head_kernel(pos_ref, own_ref, oth_ref, g_own_ref, g_oth_ref, out_ref, loss_ref, buf, sem):
    steps, block, _ = buf.shape
    rows = own_ref.shape[0]
    g = jnp.concatenate([g_own_ref[:rows, :], g_oth_ref[:rows, :]], axis=0)
    copies = []
    for i in range(steps):
        at = pl.ds(pl.multiple_of(pos_ref[0] * (steps * block) + i * block, block), block)
        h = jnp.concatenate([own_ref[:, at], oth_ref[:, at]], axis=0)
        total = lax.dot_general(h, g, (((0,), (0,)), ((), ())), preferred_element_type=F32)
        buf[i] = total.astype(BF16)
        copy = pltpu.make_async_copy(buf.at[i], out_ref.at[pl.ds(i * block, block)], sem.at[i])
        copy.start()
        copies.append(copy)

    def loss(ref):
        parts = ref[rows:, :128].astype(F32)
        return (parts[0:1] + parts[1:2]) + parts[2:3]

    loss_ref[...] = (loss(g_own_ref) + loss(g_oth_ref)) * (1.0 / (2 * rows))
    for copy in copies:
        copy.wait()


def head_grad(pos, hidden, hidden_oth, g, g_oth, steps=2):
    rows, depth = hidden.shape
    cols = g.shape[1]
    width = depth // 2
    return pl.pallas_call(
        head_kernel,
        out_shape=(
            jax.ShapeDtypeStruct((width, cols), BF16),
            jax.ShapeDtypeStruct((1, 128), F32),
        ),
        in_specs=[pl.BlockSpec(memory_space=pltpu.SMEM)] + [WHOLE] * 4,
        out_specs=(pl.BlockSpec(memory_space=pl.ANY), WHOLE),
        scratch_shapes=[
            pltpu.VMEM((steps, width // steps, cols), BF16),
            pltpu.SemaphoreType.DMA((steps,)),
        ],
        compiler_params=params(20),
        cost_estimate=LIGHT,
        name="head_grad",
    )(pos, hidden, hidden_oth, g, g_oth)


def body(teacher, hidden, head, ids, assignment, row_scale):
    c, x, y = (lax.axis_index(a) for a in ("c", "x", "y"))
    rows, depth = hidden.shape
    cols = head.shape[1]
    chips = ("y", "z", "x")
    ny, nz, nx = (lax.axis_size(a) for a in chips)
    pos = jnp.stack([c, lax.axis_index(chips) * cols, y, x]).astype(jnp.int32)
    assign = assignment.reshape(-1, 128)
    ids = ids.reshape(-1, 128)
    scale = row_scale.reshape(-1, 128)

    teacher_oth = shift(teacher, "c", 1)
    logits = student_logits(hidden, head)
    stats, teacher_rows = local_stats(pos, logits, teacher, teacher_oth, assign, ids)
    stats, scale = lax.optimization_barrier((stats, scale))
    stats = jnp.broadcast_to(stats[None], (nz * nx,) + stats.shape)
    stats = merge_stats(lax.all_to_all(stats, ("z", "x"), 0, 0, tiled=True))
    parts = [stats] + [shift(stats, "y", d) for d in (2, 1, 3)]
    hidden_oth = shift(lax.optimization_barrier((hidden, stats))[0], "c", 1)
    g = grad_logits(pos, logits, teacher_rows, ids, scale, parts)
    g, hidden_oth = lax.optimization_barrier((g, hidden_oth))
    sub = depth // (ny * nz * nx) // 2
    head6 = head.reshape(ny, nz, nx, 2, sub, cols)

    def send(value, axis, by):
        return shift((value * SEND_SCALE).astype(F16), axis, by)

    def taken(value):
        return value.astype(F32) * (1.0 / SEND_SCALE)

    sent = [(v * SEND_SCALE).astype(F16) for v in hidden_part(pos, head6, g, SENT)]
    *sent, g = lax.optimization_barrier((*sent, g))
    up_a, down_a, up_b, down_b = sent
    got_a = shift(up_a, "x", 1), shift(down_a, "x", -1)
    got_b = shift(up_b, "y", 1), shift(down_b, "y", -1)
    g_oth = shift(g, "c", 1)
    kept = hidden_part(pos, head6, g, KEPT)
    kept_a, kept_b = kept[:3], kept[3:]
    head_out, loss = head_grad(pos, hidden, hidden_oth, g, g_oth)
    loss = loss[0, :1]
    got_a, loss, _ = lax.optimization_barrier((got_a, loss, head_out))
    got_b, head_out = lax.optimization_barrier((got_b, head_out))

    def second_step(kept, got, axis):
        (c1, c3, c0), (up, down) = kept, got
        up2 = send(c1 + taken(up[:2]), axis, 1)
        down2 = send(c3 + taken(down[:2]), axis, -1)
        return c0[:2] + taken(down[2:]) + taken(up2), c0[2:] + taken(up[2:]) + taken(down2)

    low_a, high_a = second_step(kept_a, got_a, "x")
    low_b, high_b = second_step(kept_b, got_b, "y")

    def second_level(low, high, axis):
        far = [send(f, axis, d) for d, f in ((2, high[0]), (1, low[1]), (3, high[1]))]
        return low[0] + sum(taken(f) for f in far)

    both = (second_level(low_a, high_a, "y"), second_level(low_b, high_b, "x"))
    both = (jnp.concatenate(both, axis=1) * SEND_SCALE).astype(F16)
    both = lax.all_to_all(both, "z", 0, 0, tiled=True)
    hidden_grad = jnp.sum(taken(both), axis=0).T.astype(BF16)
    return loss, hidden_grad, head_out


def solution(mesh):
    ny, nzx, nc = mesh.devices.shape
    nx = 4
    fine = Mesh(mesh.devices.reshape(ny, nzx // nx, nx, nc), ("y", "z", "x", "c"))
    vocab = ("y", "z", "x")
    in_specs = (
        P(None, vocab + ("c",)),
        P("c", None),
        P(None, vocab),
        P("c"),
        P(),
        P("c"),
    )
    out_specs = (P(), P("c", vocab), P("c", vocab))
    return jax.shard_map(body, mesh=fine, in_specs=in_specs, out_specs=out_specs, check_vma=False)
```

```python
import functools

import jax
import jax.numpy as jnp
import numpy as np
from jax import lax
from jax.experimental import pallas as pl
from jax.experimental.pallas import tpu as pltpu
from jax.sharding import Mesh, PartitionSpec as P

CE_WEIGHT = 0.5
SEND_SCALE = 64.0
SPARE = 256
LOSS_ROWS = 16
F32 = jnp.float32
BF16 = jnp.bfloat16
F16 = jnp.float16


LIGHT = pl.CostEstimate(flops=1, bytes_accessed=1, transcendentals=0)
WHOLE = pl.BlockSpec(memory_space=pltpu.VMEM)


def params(mib, *semantics):
    return pltpu.CompilerParams(
        vmem_limit_bytes=mib * 1024 * 1024, dimension_semantics=semantics or None
    )


def shift(a, axis, by):
    n = lax.axis_size(axis)
    return lax.ppermute(a, axis, [(i, (i + by) % n) for i in range(n)])


def shift_by_core(a, by, first):
    axes = ("y", "z", "x", "c")
    shape = tuple(lax.axis_size(axis) for axis in axes)
    pairs = []
    for source in np.ndindex(shape):
        target = list(source)
        axis = 2 if (source[3] == 0) == first else 0
        target[axis] = (target[axis] + by) % shape[axis]
        pairs.append(tuple(int(np.ravel_multi_index(at, shape)) for at in (source, target)))
    return lax.ppermute(a, axes, pairs)


def logits_kernel(steps, h_ref, w_ref, out_ref, h_buf, w_buf, h_sem, w_sem):
    kb = w_buf.shape[1]

    def copies(k):
        at = pl.ds(k * kb, kb)
        return (
            pltpu.make_async_copy(h_ref.at[:, at], h_buf.at[k], h_sem.at[k]),
            pltpu.make_async_copy(w_ref.at[at], w_buf.at[k], w_sem.at[k]),
        )

    for k in range(steps):
        for copy in copies(k):
            copy.start()
    out_ref[...] = jnp.zeros_like(out_ref)

    def step(k, carry):
        for copy in copies(k):
            copy.wait()
        out_ref[...] += jnp.dot(h_buf[k], w_buf[k], preferred_element_type=F32)
        return carry

    lax.fori_loop(0, steps, step, 0)


def student_logits(hidden, head, steps=4):
    rows, depth = hidden.shape
    cols = head.shape[1]
    kb = depth // steps
    return pl.pallas_call(
        functools.partial(logits_kernel, steps),
        out_shape=jax.ShapeDtypeStruct((rows, cols), F32),
        in_specs=[pl.BlockSpec(memory_space=pl.ANY)] * 2,
        out_specs=WHOLE,
        scratch_shapes=[
            pltpu.VMEM((steps, rows, kb), BF16),
            pltpu.VMEM((steps, kb, cols), BF16),
            pltpu.SemaphoreType.DMA((steps,)),
            pltpu.SemaphoreType.DMA((steps,)),
        ],
        compiler_params=params(52),
        cost_estimate=pl.CostEstimate(
            flops=2 * rows * depth * cols,
            bytes_accessed=2 * (rows * depth + depth * cols) + 4 * rows * cols,
            transcendentals=0,
        ),
        name="student_logits",
    )(hidden, head)


def columns_of(*rows):
    n = rows[0].shape[1]
    sub = lax.broadcasted_iota(jnp.int32, (128, n), 0)
    packed = jnp.zeros((128, n), F32)
    for at, row in enumerate(rows):
        packed = jnp.where(sub == at, row.astype(F32), packed)
    turned = packed.T
    return [turned[:, at : at + 1] for at in range(len(rows))]


def in_row(ref):
    return jnp.concatenate([ref[i : i + 1, :] for i in range(ref.shape[0])], axis=1)


def pack_stats(out_ref, lse_s, lse_t, cross, picked):
    rows = lse_s.shape[1]
    spare = out_ref.shape[1] - rows
    far = 2 * rows - spare
    out_ref[0:1, :rows] = lse_s
    out_ref[1:2, :rows] = lse_t
    out_ref[0:1, rows:] = cross[:, :spare]
    out_ref[1:2, rows:far] = cross[:, spare:]
    lane = lax.broadcasted_iota(jnp.int32, (1, out_ref.shape[1] - far), 1)
    out_ref[1:2, far:] = jnp.where(lane == 0, picked, 0.0)


def logsumexp(values):
    top = jnp.max(values, axis=0, keepdims=True)
    return top + jnp.log(jnp.sum(jnp.exp(values - top), axis=0, keepdims=True))


def merge(first, second):
    rows = first.shape[1] - SPARE
    far = 2 * rows - SPARE
    lse_s = logsumexp(first[:, :rows])
    lse_t = logsumexp(second[:, :rows])
    share_t = jnp.exp(second[:, :rows] - lse_t)
    cross = jnp.concatenate([first[:, rows:], second[:, rows:far]], axis=1)
    cross = jnp.sum(cross * share_t, axis=0, keepdims=True)
    picked = jnp.sum(second[:, far:], axis=0, keepdims=True)
    return lse_s, lse_t, cross, jnp.sum(picked, axis=1, keepdims=True)


def merge_kernel(in_ref, out_ref):
    pack_stats(out_ref, *merge(in_ref[:, 0, :], in_ref[:, 1, :]))


def merge_stats(stats):
    return pl.pallas_call(
        merge_kernel,
        out_shape=jax.ShapeDtypeStruct(stats.shape[1:], F32),
        in_specs=[WHOLE],
        out_specs=WHOLE,
        compiler_params=params(16),
        name="merge_stats",
    )(stats)


def stats_kernel(pos_ref, l_ref, own_ref, oth_ref, assign_ref, ids_ref, stats_ref, t_ref):
    rows, cols = l_ref.shape
    total = own_ref.shape[0]
    first = pos_ref[0] == 0
    assign = in_row(assign_ref)
    assign = jnp.where(first, assign[:, :rows], assign[:, rows:])
    assign, ids = columns_of(assign, in_row(ids_ref))
    lanes = lax.broadcasted_iota(jnp.int32, (rows, total), 1).astype(F32)
    pick = (lanes == assign).astype(BF16)
    own = jnp.dot(pick, own_ref[...], preferred_element_type=F32)
    oth = jnp.dot(pick, oth_ref[...], preferred_element_type=F32)
    teacher = jnp.concatenate([jnp.where(first, own, oth), jnp.where(first, oth, own)], axis=1)
    t_ref[...] = teacher.astype(BF16)
    logits = l_ref[...]
    top_s = jnp.max(logits, axis=1, keepdims=True)
    sum_s = jnp.sum(jnp.exp(logits - top_s), axis=1, keepdims=True)
    top_t = jnp.max(teacher, axis=1, keepdims=True)
    exp_t = jnp.exp(teacher - top_t)
    sum_t = jnp.sum(exp_t, axis=1, keepdims=True)
    cross = jnp.sum(exp_t * (teacher - logits), axis=1, keepdims=True)
    columns = pos_ref[1] + lax.broadcasted_iota(jnp.int32, (rows, cols), 1)
    hot = columns.astype(F32) == ids
    picked = jnp.sum(jnp.where(hot, logits, 0.0), axis=1, keepdims=True)
    lane = lax.broadcasted_iota(jnp.int32, (rows, 128), 1)
    packed = jnp.zeros((rows, 128), F32)
    for at, value in enumerate((top_s, sum_s, top_t, sum_t, cross, picked)):
        packed = jnp.where(lane == at, value, packed)
    packed = packed.T
    top_s, sum_s, top_t, sum_t, cross, picked = (packed[at : at + 1] for at in range(6))
    cross = cross / sum_t
    picked = jnp.sum(picked, axis=1, keepdims=True)
    pack_stats(stats_ref, top_s + jnp.log(sum_s), top_t + jnp.log(sum_t), cross, picked)


def local_stats(pos, logits, own, oth, assign, ids):
    rows, cols = logits.shape
    return pl.pallas_call(
        stats_kernel,
        out_shape=(
            jax.ShapeDtypeStruct((2, rows + SPARE), F32),
            jax.ShapeDtypeStruct((rows, cols), BF16),
        ),
        in_specs=[pl.BlockSpec(memory_space=pltpu.SMEM)] + [WHOLE] * 5,
        out_specs=(WHOLE, WHOLE),
        compiler_params=params(16),
        cost_estimate=pl.CostEstimate(
            flops=2 * rows * cols * own.shape[0],
            bytes_accessed=4 * rows * cols + 4 * own.size + 2 * rows * cols,
            transcendentals=2 * rows * cols,
        ),
        name="local_stats",
    )(pos, logits, own, oth, assign, ids)


def grad_kernel(pos_ref, l_ref, t_ref, ids_ref, scale_ref, s0, s1, s2, s3, g_ref):
    rows, cols = l_ref.shape
    parts = (s0, s1, s2, s3)
    first, second = (
        jnp.concatenate([part[at : at + 1, :] for part in parts], axis=0) for at in (0, 1)
    )
    norm_s, norm_t, cross, picked = merge(first, second)
    terms = cross - norm_t + (1.0 + CE_WEIGHT) * norm_s
    terms = jnp.sum(terms, axis=1, keepdims=True) - CE_WEIGHT * picked
    high = terms.astype(BF16).astype(F32)
    middle = (terms - high).astype(BF16).astype(F32)
    low = terms - high - middle
    at = lax.broadcasted_iota(jnp.int32, (LOSS_ROWS, cols), 0)
    tail = jnp.where(at == 0, high, jnp.where(at == 1, middle, jnp.where(at == 2, low, 0.0)))
    g_ref[rows:, :] = tail.astype(BF16)
    norm_s, norm_t, ids, scale = columns_of(norm_s, norm_t, in_row(ids_ref), in_row(scale_ref))
    columns = pos_ref[1] + lax.broadcasted_iota(jnp.int32, (rows, cols), 1)
    hot = jnp.where(columns.astype(F32) == ids, CE_WEIGHT, 0.0)
    prob_s = jnp.exp(l_ref[...] - norm_s)
    prob_t = jnp.exp(t_ref[...].astype(F32) - norm_t)
    g_ref[:rows, :] = (scale * ((1.0 + CE_WEIGHT) * prob_s - prob_t - hot)).astype(BF16)


def grad_logits(pos, logits, teacher, ids, scale, parts):
    rows, cols = logits.shape
    return pl.pallas_call(
        grad_kernel,
        out_shape=jax.ShapeDtypeStruct((rows + LOSS_ROWS, cols), BF16),
        in_specs=[pl.BlockSpec(memory_space=pltpu.SMEM)] + [WHOLE] * 8,
        out_specs=WHOLE,
        compiler_params=params(16),
        cost_estimate=pl.CostEstimate(
            flops=8 * rows * cols,
            bytes_accessed=8 * rows * cols,
            transcendentals=2 * rows * cols,
        ),
        name="grad_logits",
    )(pos, logits, teacher, ids, scale, *parts)


SENT = (((2, 0), (2, 1), (1, 2), (1, 3)), ((2, 2), (2, 3), (3, 0), (3, 1)))
KEPT = (((1, 0), (1, 1)), ((3, 2), (3, 3)), ((0, 0), (0, 1), (0, 2), (0, 3)))


def hidden_kernel(groups, pos_ref, w_ref, g_ref, *outs):
    ny, nz, nx, sub, cols = w_ref.shape
    x_first, y, x = pos_ref[0] == 0, pos_ref[2], pos_ref[3]
    g = g_ref[: outs[0].shape[-1], :]

    def block(far, near):
        dx = jnp.where(x_first, far, near)
        dy = jnp.where(x_first, near, far)
        w = w_ref[lax.rem(y + dy, ny), :, lax.rem(x + dx, nx)]
        return w.reshape(nz * sub, cols)

    for names, out in zip(groups, outs):
        w = jnp.concatenate([block(*name) for name in names], axis=0)
        product = lax.dot_general(w, g, (((1,), (1,)), ((), ())), preferred_element_type=F32)
        out[...] = product.reshape(out.shape)


def hidden_part(pos, head5, g, groups):
    nz, sub = head5.shape[1], head5.shape[3]
    rows = g.shape[0] - LOSS_ROWS
    out_shape = [jax.ShapeDtypeStruct((len(names), nz, sub, rows), F32) for names in groups]
    return pl.pallas_call(
        functools.partial(hidden_kernel, groups),
        out_shape=out_shape,
        in_specs=[pl.BlockSpec(memory_space=pltpu.SMEM), WHOLE, WHOLE],
        out_specs=[WHOLE] * len(out_shape),
        compiler_params=params(16),
        cost_estimate=LIGHT,
        name="hidden_part",
    )(pos, head5, g)


def head_kernel(pos_ref, own_ref, oth_ref, g_own_ref, g_oth_ref, out_ref, loss_ref, buf, sem):
    steps, block, _ = buf.shape
    rows = own_ref.shape[0]
    g = jnp.concatenate([g_own_ref[:rows, :], g_oth_ref[:rows, :]], axis=0)
    copies = []
    for i in range(steps):
        at = pl.ds(pl.multiple_of(pos_ref[0] * (steps * block) + i * block, block), block)
        h = jnp.concatenate([own_ref[:, at], oth_ref[:, at]], axis=0)
        total = lax.dot_general(h, g, (((0,), (0,)), ((), ())), preferred_element_type=F32)
        buf[i] = total.astype(BF16)
        copy = pltpu.make_async_copy(buf.at[i], out_ref.at[pl.ds(i * block, block)], sem.at[i])
        copy.start()
        copies.append(copy)

    def loss(ref):
        parts = ref[rows:, :128].astype(F32)
        return (parts[0:1] + parts[1:2]) + parts[2:3]

    loss_ref[...] = (loss(g_own_ref) + loss(g_oth_ref)) * (1.0 / (2 * rows))
    for copy in copies:
        copy.wait()


def head_grad(pos, hidden, hidden_oth, g, g_oth, steps=2):
    rows, depth = hidden.shape
    cols = g.shape[1]
    width = depth // 2
    return pl.pallas_call(
        head_kernel,
        out_shape=(
            jax.ShapeDtypeStruct((width, cols), BF16),
            jax.ShapeDtypeStruct((1, 128), F32),
        ),
        in_specs=[pl.BlockSpec(memory_space=pltpu.SMEM)] + [WHOLE] * 4,
        out_specs=(pl.BlockSpec(memory_space=pl.ANY), WHOLE),
        scratch_shapes=[
            pltpu.VMEM((steps, width // steps, cols), BF16),
            pltpu.SemaphoreType.DMA((steps,)),
        ],
        compiler_params=params(20),
        cost_estimate=LIGHT,
        name="head_grad",
    )(pos, hidden, hidden_oth, g, g_oth)


def body(teacher, hidden, head, ids, assignment, row_scale):
    c, x, y = (lax.axis_index(a) for a in ("c", "x", "y"))
    rows, depth = hidden.shape
    cols = head.shape[1]
    chips = ("y", "z", "x")
    ny, nz, nx = (lax.axis_size(a) for a in chips)
    pos = jnp.stack([c, lax.axis_index(chips) * cols, y, x]).astype(jnp.int32)
    assign = assignment.reshape(-1, 128)
    ids = ids.reshape(-1, 128)
    scale = row_scale.reshape(-1, 128)

    teacher_oth = shift(teacher, "c", 1)
    logits = student_logits(hidden, head)
    stats, teacher_rows = local_stats(pos, logits, teacher, teacher_oth, assign, ids)
    stats, scale = lax.optimization_barrier((stats, scale))
    stats = jnp.broadcast_to(stats[None], (nz * nx,) + stats.shape)
    stats = merge_stats(lax.all_to_all(stats, ("z", "x"), 0, 0, tiled=True))
    parts = [stats] + [shift(stats, "y", d) for d in (2, 1, 3)]
    hidden_oth = shift(lax.optimization_barrier((hidden, stats))[0], "c", 1)
    g = grad_logits(pos, logits, teacher_rows, ids, scale, parts)
    g, hidden_oth = lax.optimization_barrier((g, hidden_oth))
    head5 = head.reshape(ny, nz, nx, depth // (ny * nz * nx), cols)

    def coded(value):
        return (value * SEND_SCALE).astype(F16)

    def taken(value):
        return value.astype(F32) * (1.0 / SEND_SCALE)

    up, down = (coded(v) for v in hidden_part(pos, head5, g, SENT))
    up, down, g = lax.optimization_barrier((up, down, g))
    up, down = shift_by_core(up, 1, True), shift_by_core(down, -1, True)
    g_oth = shift(g, "c", 1)
    c1, c3, c0 = hidden_part(pos, head5, g, KEPT)
    head_out, loss = head_grad(pos, hidden, hidden_oth, g, g_oth)
    loss = loss[0, :1]
    up, down, loss, head_out = lax.optimization_barrier((up, down, loss, head_out))

    up2 = shift_by_core(coded(c1 + taken(up[:2])), 1, True)
    down2 = shift_by_core(coded(c3 + taken(down[:2])), -1, True)
    low = c0[:2] + taken(down[2:]) + taken(up2)
    high = c0[2:] + taken(up[2:]) + taken(down2)

    far = [shift_by_core(coded(v), d, False) for d, v in ((2, high[0]), (1, low[1]), (3, high[1]))]
    both = coded(low[0] + sum(taken(v) for v in far))
    both = lax.all_to_all(both, "z", 0, 0, tiled=True)
    hidden_grad = jnp.sum(taken(both), axis=0).T.astype(BF16)
    return loss, hidden_grad, head_out


def solution(mesh):
    ny, nzx, nc = mesh.devices.shape
    nx = 4
    fine = Mesh(mesh.devices.reshape(ny, nzx // nx, nx, nc), ("y", "z", "x", "c"))
    vocab = ("y", "z", "x")
    in_specs = (
        P(None, vocab + ("c",)),
        P("c", None),
        P(None, vocab),
        P("c"),
        P(),
        P("c"),
    )
    out_specs = (P(), P("c", vocab), P("c", vocab))
    return jax.shard_map(body, mesh=fine, in_specs=in_specs, out_specs=out_specs, check_vma=False)
```

```python
import functools

import jax
import jax.numpy as jnp
import numpy as np
from jax import lax
from jax.experimental import pallas as pl
from jax.experimental.pallas import tpu as pltpu
from jax.sharding import Mesh, PartitionSpec as P

CE_WEIGHT = 0.5
SEND_SCALE = 64.0
SPARE = 256
LOSS_ROWS = 16
F32 = jnp.float32
BF16 = jnp.bfloat16
F16 = jnp.float16


LIGHT = pl.CostEstimate(flops=1, bytes_accessed=1, transcendentals=0)
WHOLE = pl.BlockSpec(memory_space=pltpu.VMEM)


def params(mib, *semantics):
    return pltpu.CompilerParams(
        vmem_limit_bytes=mib * 1024 * 1024, dimension_semantics=semantics or None
    )


def shift(a, axis, by):
    n = lax.axis_size(axis)
    return lax.ppermute(a, axis, [(i, (i + by) % n) for i in range(n)])


def shift_by_core(a, by, first):
    axes = ("y", "z", "x", "c")
    shape = tuple(lax.axis_size(axis) for axis in axes)
    pairs = []
    for source in np.ndindex(shape):
        target = list(source)
        axis = 2 if (source[3] == 0) == first else 0
        target[axis] = (target[axis] + by) % shape[axis]
        pairs.append(tuple(int(np.ravel_multi_index(at, shape)) for at in (source, target)))
    return lax.ppermute(a, axes, pairs)


def logits_kernel(steps, h_ref, w_ref, out_ref, h_buf, w_buf, h_sem, w_sem):
    kb = w_buf.shape[1]

    def copies(k):
        at = pl.ds(k * kb, kb)
        return (
            pltpu.make_async_copy(h_ref.at[:, at], h_buf.at[k], h_sem.at[k]),
            pltpu.make_async_copy(w_ref.at[at], w_buf.at[k], w_sem.at[k]),
        )

    for k in range(steps):
        for copy in copies(k):
            copy.start()
    out_ref[...] = jnp.zeros_like(out_ref)

    def step(k, carry):
        for copy in copies(k):
            copy.wait()
        out_ref[...] += jnp.dot(h_buf[k], w_buf[k], preferred_element_type=F32)
        return carry

    lax.fori_loop(0, steps, step, 0)


def student_logits(hidden, head, steps=4):
    rows, depth = hidden.shape
    cols = head.shape[1]
    kb = depth // steps
    return pl.pallas_call(
        functools.partial(logits_kernel, steps),
        out_shape=jax.ShapeDtypeStruct((rows, cols), F32),
        in_specs=[pl.BlockSpec(memory_space=pl.ANY)] * 2,
        out_specs=WHOLE,
        scratch_shapes=[
            pltpu.VMEM((steps, rows, kb), BF16),
            pltpu.VMEM((steps, kb, cols), BF16),
            pltpu.SemaphoreType.DMA((steps,)),
            pltpu.SemaphoreType.DMA((steps,)),
        ],
        compiler_params=params(52),
        cost_estimate=pl.CostEstimate(
            flops=2 * rows * depth * cols,
            bytes_accessed=2 * (rows * depth + depth * cols) + 4 * rows * cols,
            transcendentals=0,
        ),
        name="student_logits",
    )(hidden, head)


def columns_of(*rows):
    n = rows[0].shape[1]
    sub = lax.broadcasted_iota(jnp.int32, (128, n), 0)
    packed = jnp.zeros((128, n), F32)
    for at, row in enumerate(rows):
        packed = jnp.where(sub == at, row.astype(F32), packed)
    turned = packed.T
    return [turned[:, at : at + 1] for at in range(len(rows))]


def in_row(ref):
    return jnp.concatenate([ref[i : i + 1, :] for i in range(ref.shape[0])], axis=1)


def pack_stats(out_ref, lse_s, lse_t, cross, picked):
    rows = lse_s.shape[1]
    spare = out_ref.shape[1] - rows
    far = 2 * rows - spare
    out_ref[0:1, :rows] = lse_s
    out_ref[1:2, :rows] = lse_t
    out_ref[0:1, rows:] = cross[:, :spare]
    out_ref[1:2, rows:far] = cross[:, spare:]
    lane = lax.broadcasted_iota(jnp.int32, (1, out_ref.shape[1] - far), 1)
    out_ref[1:2, far:] = jnp.where(lane == 0, picked, 0.0)


def logsumexp(values):
    top = jnp.max(values, axis=0, keepdims=True)
    return top + jnp.log(jnp.sum(jnp.exp(values - top), axis=0, keepdims=True))


def merge(first, second):
    rows = first.shape[1] - SPARE
    far = 2 * rows - SPARE
    lse_s = logsumexp(first[:, :rows])
    lse_t = logsumexp(second[:, :rows])
    share_t = jnp.exp(second[:, :rows] - lse_t)
    cross = jnp.concatenate([first[:, rows:], second[:, rows:far]], axis=1)
    cross = jnp.sum(cross * share_t, axis=0, keepdims=True)
    picked = jnp.sum(second[:, far:], axis=0, keepdims=True)
    return lse_s, lse_t, cross, jnp.sum(picked, axis=1, keepdims=True)


def merge_kernel(in_ref, out_ref):
    pack_stats(out_ref, *merge(in_ref[:, 0, :], in_ref[:, 1, :]))


def merge_stats(stats):
    return pl.pallas_call(
        merge_kernel,
        out_shape=jax.ShapeDtypeStruct(stats.shape[1:], F32),
        in_specs=[WHOLE],
        out_specs=WHOLE,
        compiler_params=params(16),
        name="merge_stats",
    )(stats)


def stats_kernel(pos_ref, l_ref, own_ref, oth_ref, assign_ref, ids_ref, stats_ref, t_ref):
    rows, cols = l_ref.shape
    total = own_ref.shape[0]
    first = pos_ref[0] == 0
    assign = in_row(assign_ref)
    assign = jnp.where(first, assign[:, :rows], assign[:, rows:])
    assign, ids = columns_of(assign, in_row(ids_ref))
    lanes = lax.broadcasted_iota(jnp.int32, (rows, total), 1).astype(F32)
    pick = (lanes == assign).astype(BF16)
    own = jnp.dot(pick, own_ref[...], preferred_element_type=F32)
    oth = jnp.dot(pick, oth_ref[...], preferred_element_type=F32)
    teacher = jnp.concatenate([jnp.where(first, own, oth), jnp.where(first, oth, own)], axis=1)
    t_ref[...] = teacher.astype(BF16)
    logits = l_ref[...]
    top_s = jnp.max(logits, axis=1, keepdims=True)
    sum_s = jnp.sum(jnp.exp(logits - top_s), axis=1, keepdims=True)
    top_t = jnp.max(teacher, axis=1, keepdims=True)
    exp_t = jnp.exp(teacher - top_t)
    sum_t = jnp.sum(exp_t, axis=1, keepdims=True)
    cross = jnp.sum(exp_t * (teacher - logits), axis=1, keepdims=True)
    columns = pos_ref[1] + lax.broadcasted_iota(jnp.int32, (rows, cols), 1)
    hot = columns.astype(F32) == ids
    picked = jnp.sum(jnp.where(hot, logits, 0.0), axis=1, keepdims=True)
    lane = lax.broadcasted_iota(jnp.int32, (rows, 128), 1)
    packed = jnp.zeros((rows, 128), F32)
    for at, value in enumerate((top_s, sum_s, top_t, sum_t, cross, picked)):
        packed = jnp.where(lane == at, value, packed)
    packed = packed.T
    top_s, sum_s, top_t, sum_t, cross, picked = (packed[at : at + 1] for at in range(6))
    cross = cross / sum_t
    picked = jnp.sum(picked, axis=1, keepdims=True)
    pack_stats(stats_ref, top_s + jnp.log(sum_s), top_t + jnp.log(sum_t), cross, picked)


def local_stats(pos, logits, own, oth, assign, ids):
    rows, cols = logits.shape
    return pl.pallas_call(
        stats_kernel,
        out_shape=(
            jax.ShapeDtypeStruct((2, rows + SPARE), F32),
            jax.ShapeDtypeStruct((rows, cols), BF16),
        ),
        in_specs=[pl.BlockSpec(memory_space=pltpu.SMEM)] + [WHOLE] * 5,
        out_specs=(WHOLE, WHOLE),
        compiler_params=params(16),
        cost_estimate=pl.CostEstimate(
            flops=2 * rows * cols * own.shape[0],
            bytes_accessed=4 * rows * cols + 4 * own.size + 2 * rows * cols,
            transcendentals=2 * rows * cols,
        ),
        name="local_stats",
    )(pos, logits, own, oth, assign, ids)


def grad_kernel(pos_ref, l_ref, t_ref, ids_ref, scale_ref, s0, s1, s2, s3, g_ref):
    rows, cols = l_ref.shape
    parts = (s0, s1, s2, s3)
    first, second = (
        jnp.concatenate([part[at : at + 1, :] for part in parts], axis=0) for at in (0, 1)
    )
    norm_s, norm_t, cross, picked = merge(first, second)
    terms = cross - norm_t + (1.0 + CE_WEIGHT) * norm_s
    terms = jnp.sum(terms, axis=1, keepdims=True) - CE_WEIGHT * picked
    high = terms.astype(BF16).astype(F32)
    middle = (terms - high).astype(BF16).astype(F32)
    low = terms - high - middle
    at = lax.broadcasted_iota(jnp.int32, (LOSS_ROWS, cols), 0)
    tail = jnp.where(at == 0, high, jnp.where(at == 1, middle, jnp.where(at == 2, low, 0.0)))
    g_ref[rows:, :] = tail.astype(BF16)
    norm_s, norm_t, ids, scale = columns_of(norm_s, norm_t, in_row(ids_ref), in_row(scale_ref))
    columns = pos_ref[1] + lax.broadcasted_iota(jnp.int32, (rows, cols), 1)
    hot = jnp.where(columns.astype(F32) == ids, CE_WEIGHT, 0.0)
    prob_s = jnp.exp(l_ref[...] - norm_s)
    prob_t = jnp.exp(t_ref[...].astype(F32) - norm_t)
    g_ref[:rows, :] = (scale * ((1.0 + CE_WEIGHT) * prob_s - prob_t - hot)).astype(BF16)


def grad_logits(pos, logits, teacher, ids, scale, parts):
    rows, cols = logits.shape
    return pl.pallas_call(
        grad_kernel,
        out_shape=jax.ShapeDtypeStruct((rows + LOSS_ROWS, cols), BF16),
        in_specs=[pl.BlockSpec(memory_space=pltpu.SMEM)] + [WHOLE] * 8,
        out_specs=WHOLE,
        compiler_params=params(16),
        cost_estimate=pl.CostEstimate(
            flops=8 * rows * cols,
            bytes_accessed=8 * rows * cols,
            transcendentals=2 * rows * cols,
        ),
        name="grad_logits",
    )(pos, logits, teacher, ids, scale, *parts)


SENT = tuple(tuple((far, near) for near in range(4)) for far in (2, 1, 3))
KEPT = (tuple((0, near) for near in range(4)),)


def hidden_kernel(groups, pos_ref, w_ref, g_ref, *outs):
    ny, nz, nx, sub, cols = w_ref.shape
    x_first, y, x = pos_ref[0] == 0, pos_ref[2], pos_ref[3]
    g = g_ref[: outs[0].shape[-1], :]

    def block(far, near):
        dx = jnp.where(x_first, far, near)
        dy = jnp.where(x_first, near, far)
        w = w_ref[lax.rem(y + dy, ny), :, lax.rem(x + dx, nx)]
        return w.reshape(nz * sub, cols)

    for names, out in zip(groups, outs):
        w = jnp.concatenate([block(*name) for name in names], axis=0)
        product = lax.dot_general(w, g, (((1,), (1,)), ((), ())), preferred_element_type=F32)
        out[...] = product.reshape(out.shape)


def hidden_part(pos, head5, g, groups):
    nz, sub = head5.shape[1], head5.shape[3]
    rows = g.shape[0] - LOSS_ROWS
    out_shape = [jax.ShapeDtypeStruct((len(names), nz, sub, rows), F32) for names in groups]
    return pl.pallas_call(
        functools.partial(hidden_kernel, groups),
        out_shape=out_shape,
        in_specs=[pl.BlockSpec(memory_space=pltpu.SMEM), WHOLE, WHOLE],
        out_specs=[WHOLE] * len(out_shape),
        compiler_params=params(16),
        cost_estimate=LIGHT,
        name="hidden_part",
    )(pos, head5, g)


def head_kernel(pos_ref, own_ref, oth_ref, g_own_ref, g_oth_ref, out_ref, loss_ref, buf, sem):
    steps, block, _ = buf.shape
    rows = own_ref.shape[0]
    g = jnp.concatenate([g_own_ref[:rows, :], g_oth_ref[:rows, :]], axis=0)
    copies = []
    for i in range(steps):
        at = pl.ds(pl.multiple_of(pos_ref[0] * (steps * block) + i * block, block), block)
        h = jnp.concatenate([own_ref[:, at], oth_ref[:, at]], axis=0)
        total = lax.dot_general(h, g, (((0,), (0,)), ((), ())), preferred_element_type=F32)
        buf[i] = total.astype(BF16)
        copy = pltpu.make_async_copy(buf.at[i], out_ref.at[pl.ds(i * block, block)], sem.at[i])
        copy.start()
        copies.append(copy)

    def loss(ref):
        parts = ref[rows:, :128].astype(F32)
        return (parts[0:1] + parts[1:2]) + parts[2:3]

    loss_ref[...] = (loss(g_own_ref) + loss(g_oth_ref)) * (1.0 / (2 * rows))
    for copy in copies:
        copy.wait()


def head_grad(pos, hidden, hidden_oth, g, g_oth, steps=2):
    rows, depth = hidden.shape
    cols = g.shape[1]
    width = depth // 2
    return pl.pallas_call(
        head_kernel,
        out_shape=(
            jax.ShapeDtypeStruct((width, cols), BF16),
            jax.ShapeDtypeStruct((1, 128), F32),
        ),
        in_specs=[pl.BlockSpec(memory_space=pltpu.SMEM)] + [WHOLE] * 4,
        out_specs=(pl.BlockSpec(memory_space=pl.ANY), WHOLE),
        scratch_shapes=[
            pltpu.VMEM((steps, width // steps, cols), BF16),
            pltpu.SemaphoreType.DMA((steps,)),
        ],
        compiler_params=params(20),
        cost_estimate=LIGHT,
        name="head_grad",
    )(pos, hidden, hidden_oth, g, g_oth)


def body(teacher, hidden, head, ids, assignment, row_scale):
    c, x, y = (lax.axis_index(a) for a in ("c", "x", "y"))
    rows, depth = hidden.shape
    cols = head.shape[1]
    chips = ("y", "z", "x")
    ny, nz, nx = (lax.axis_size(a) for a in chips)
    pos = jnp.stack([c, lax.axis_index(chips) * cols, y, x]).astype(jnp.int32)
    assign = assignment.reshape(-1, 128)
    ids = ids.reshape(-1, 128)
    scale = row_scale.reshape(-1, 128)

    teacher_oth = shift(teacher, "c", 1)
    logits = student_logits(hidden, head)
    stats, teacher_rows = local_stats(pos, logits, teacher, teacher_oth, assign, ids)
    stats, scale = lax.optimization_barrier((stats, scale))
    stats = jnp.broadcast_to(stats[None], (nz * nx,) + stats.shape)
    stats = merge_stats(lax.all_to_all(stats, ("z", "x"), 0, 0, tiled=True))
    parts = [stats] + [shift(stats, "y", d) for d in (2, 1, 3)]
    hidden_oth = shift(lax.optimization_barrier((hidden, stats))[0], "c", 1)
    g = grad_logits(pos, logits, teacher_rows, ids, scale, parts)
    g, hidden_oth = lax.optimization_barrier((g, hidden_oth))
    head5 = head.reshape(ny, nz, nx, depth // (ny * nz * nx), cols)

    def coded(value):
        return (value * SEND_SCALE).astype(F16)

    def taken(value):
        return value.astype(F32) * (1.0 / SEND_SCALE)

    def exchange(chunks, first):
        return [shift_by_core(v, d, first) for v, d in zip(chunks, (2, 1, 3))]

    sent = [coded(v) for v in hidden_part(pos, head5, g, SENT)]
    *sent, g = lax.optimization_barrier((*sent, g))
    got = exchange(sent, True)
    g_oth = shift(g, "c", 1)
    (own,) = hidden_part(pos, head5, g, KEPT)
    head_out, loss = head_grad(pos, hidden, hidden_oth, g, g_oth)
    loss = loss[0, :1]
    *got, loss, head_out = lax.optimization_barrier((*got, loss, head_out))
    total = own + sum(taken(v) for v in got)
    got = exchange([coded(total[d]) for d in (2, 1, 3)], False)
    both = coded(total[0] + sum(taken(v) for v in got))
    both = lax.all_to_all(both, "z", 0, 0, tiled=True)
    hidden_grad = jnp.sum(taken(both), axis=0).T.astype(BF16)
    return loss, hidden_grad, head_out


def solution(mesh):
    ny, nzx, nc = mesh.devices.shape
    nx = 4
    fine = Mesh(mesh.devices.reshape(ny, nzx // nx, nx, nc), ("y", "z", "x", "c"))
    vocab = ("y", "z", "x")
    in_specs = (
        P(None, vocab + ("c",)),
        P("c", None),
        P(None, vocab),
        P("c"),
        P(),
        P("c"),
    )
    out_specs = (P(), P("c", vocab), P("c", vocab))
    return jax.shard_map(body, mesh=fine, in_specs=in_specs, out_specs=out_specs, check_vma=False)
```

```python
import functools

import jax
import jax.numpy as jnp
import numpy as np
from jax import lax
from jax.experimental import pallas as pl
from jax.experimental.pallas import tpu as pltpu
from jax.sharding import Mesh, PartitionSpec as P

CE_WEIGHT = 0.5
SEND_SCALE = 64.0
SPARE = 256
LOSS_ROWS = 16
F32 = jnp.float32
BF16 = jnp.bfloat16
F16 = jnp.float16


LIGHT = pl.CostEstimate(flops=1, bytes_accessed=1, transcendentals=0)
WHOLE = pl.BlockSpec(memory_space=pltpu.VMEM)


def params(mib, *semantics):
    return pltpu.CompilerParams(
        vmem_limit_bytes=mib * 1024 * 1024, dimension_semantics=semantics or None
    )


def shift(a, axis, by):
    n = lax.axis_size(axis)
    return lax.ppermute(a, axis, [(i, (i + by) % n) for i in range(n)])


def shift_by_core(a, by, first):
    axes = ("y", "z", "x", "c")
    shape = tuple(lax.axis_size(axis) for axis in axes)
    pairs = []
    for source in np.ndindex(shape):
        target = list(source)
        axis = 2 if (source[3] == 0) == first else 0
        target[axis] = (target[axis] + by) % shape[axis]
        pairs.append(tuple(int(np.ravel_multi_index(at, shape)) for at in (source, target)))
    return lax.ppermute(a, axes, pairs)


def logits_kernel(steps, h_ref, w_ref, out_ref, h_buf, w_buf, h_sem, w_sem):
    kb = w_buf.shape[1]

    def copies(k):
        at = pl.ds(k * kb, kb)
        return (
            pltpu.make_async_copy(h_ref.at[:, at], h_buf.at[k], h_sem.at[k]),
            pltpu.make_async_copy(w_ref.at[at], w_buf.at[k], w_sem.at[k]),
        )

    for k in range(steps):
        for copy in copies(k):
            copy.start()
    out_ref[...] = jnp.zeros_like(out_ref)

    def step(k, carry):
        for copy in copies(k):
            copy.wait()
        out_ref[...] += jnp.dot(h_buf[k], w_buf[k], preferred_element_type=F32)
        return carry

    lax.fori_loop(0, steps, step, 0)


def student_logits(hidden, head, steps=4):
    rows, depth = hidden.shape
    cols = head.shape[1]
    kb = depth // steps
    return pl.pallas_call(
        functools.partial(logits_kernel, steps),
        out_shape=jax.ShapeDtypeStruct((rows, cols), F32),
        in_specs=[pl.BlockSpec(memory_space=pl.ANY)] * 2,
        out_specs=WHOLE,
        scratch_shapes=[
            pltpu.VMEM((steps, rows, kb), BF16),
            pltpu.VMEM((steps, kb, cols), BF16),
            pltpu.SemaphoreType.DMA((steps,)),
            pltpu.SemaphoreType.DMA((steps,)),
        ],
        compiler_params=params(52),
        cost_estimate=pl.CostEstimate(
            flops=2 * rows * depth * cols,
            bytes_accessed=2 * (rows * depth + depth * cols) + 4 * rows * cols,
            transcendentals=0,
        ),
        name="student_logits",
    )(hidden, head)


def columns_of(*rows):
    n = rows[0].shape[1]
    sub = lax.broadcasted_iota(jnp.int32, (128, n), 0)
    packed = jnp.zeros((128, n), F32)
    for at, row in enumerate(rows):
        packed = jnp.where(sub == at, row.astype(F32), packed)
    turned = packed.T
    return [turned[:, at : at + 1] for at in range(len(rows))]


def in_row(ref):
    return jnp.concatenate([ref[i : i + 1, :] for i in range(ref.shape[0])], axis=1)


def pack_stats(out_ref, lse_s, lse_t, cross, picked):
    rows = lse_s.shape[1]
    spare = out_ref.shape[1] - rows
    far = 2 * rows - spare
    out_ref[0:1, :rows] = lse_s
    out_ref[1:2, :rows] = lse_t
    out_ref[0:1, rows:] = cross[:, :spare]
    out_ref[1:2, rows:far] = cross[:, spare:]
    lane = lax.broadcasted_iota(jnp.int32, (1, out_ref.shape[1] - far), 1)
    out_ref[1:2, far:] = jnp.where(lane == 0, picked, 0.0)


def logsumexp(values):
    top = jnp.max(values, axis=0, keepdims=True)
    return top + jnp.log(jnp.sum(jnp.exp(values - top), axis=0, keepdims=True))


def merge(first, second):
    rows = first.shape[1] - SPARE
    far = 2 * rows - SPARE
    lse_s = logsumexp(first[:, :rows])
    lse_t = logsumexp(second[:, :rows])
    share_t = jnp.exp(second[:, :rows] - lse_t)
    cross = jnp.concatenate([first[:, rows:], second[:, rows:far]], axis=1)
    cross = jnp.sum(cross * share_t, axis=0, keepdims=True)
    picked = jnp.sum(second[:, far:], axis=0, keepdims=True)
    return lse_s, lse_t, cross, jnp.sum(picked, axis=1, keepdims=True)


def merge_kernel(in_ref, out_ref):
    pack_stats(out_ref, *merge(in_ref[:, 0, :], in_ref[:, 1, :]))


def merge_stats(stats):
    return pl.pallas_call(
        merge_kernel,
        out_shape=jax.ShapeDtypeStruct(stats.shape[1:], F32),
        in_specs=[WHOLE],
        out_specs=WHOLE,
        compiler_params=params(16),
        name="merge_stats",
    )(stats)


def stats_kernel(pos_ref, l_ref, own_ref, oth_ref, assign_ref, ids_ref, stats_ref, t_ref):
    rows, cols = l_ref.shape
    total = own_ref.shape[0]
    first = pos_ref[0] == 0
    assign = in_row(assign_ref)
    assign = jnp.where(first, assign[:, :rows], assign[:, rows:])
    assign, ids = columns_of(assign, in_row(ids_ref))
    lanes = lax.broadcasted_iota(jnp.int32, (rows, total), 1).astype(F32)
    pick = (lanes == assign).astype(BF16)
    own = jnp.dot(pick, own_ref[...], preferred_element_type=F32)
    oth = jnp.dot(pick, oth_ref[...], preferred_element_type=F32)
    teacher = jnp.concatenate([jnp.where(first, own, oth), jnp.where(first, oth, own)], axis=1)
    t_ref[...] = teacher.astype(BF16)
    logits = l_ref[...]
    top_s = jnp.max(logits, axis=1, keepdims=True)
    sum_s = jnp.sum(jnp.exp(logits - top_s), axis=1, keepdims=True)
    top_t = jnp.max(teacher, axis=1, keepdims=True)
    exp_t = jnp.exp(teacher - top_t)
    sum_t = jnp.sum(exp_t, axis=1, keepdims=True)
    cross = jnp.sum(exp_t * (teacher - logits), axis=1, keepdims=True)
    columns = pos_ref[1] + lax.broadcasted_iota(jnp.int32, (rows, cols), 1)
    hot = columns.astype(F32) == ids
    picked = jnp.sum(jnp.where(hot, logits, 0.0), axis=1, keepdims=True)
    lane = lax.broadcasted_iota(jnp.int32, (rows, 128), 1)
    packed = jnp.zeros((rows, 128), F32)
    for at, value in enumerate((top_s, sum_s, top_t, sum_t, cross, picked)):
        packed = jnp.where(lane == at, value, packed)
    packed = packed.T
    top_s, sum_s, top_t, sum_t, cross, picked = (packed[at : at + 1] for at in range(6))
    cross = cross / sum_t
    picked = jnp.sum(picked, axis=1, keepdims=True)
    pack_stats(stats_ref, top_s + jnp.log(sum_s), top_t + jnp.log(sum_t), cross, picked)


def local_stats(pos, logits, own, oth, assign, ids):
    rows, cols = logits.shape
    return pl.pallas_call(
        stats_kernel,
        out_shape=(
            jax.ShapeDtypeStruct((2, rows + SPARE), F32),
            jax.ShapeDtypeStruct((rows, cols), BF16),
        ),
        in_specs=[pl.BlockSpec(memory_space=pltpu.SMEM)] + [WHOLE] * 5,
        out_specs=(WHOLE, WHOLE),
        compiler_params=params(16),
        cost_estimate=pl.CostEstimate(
            flops=2 * rows * cols * own.shape[0],
            bytes_accessed=4 * rows * cols + 4 * own.size + 2 * rows * cols,
            transcendentals=2 * rows * cols,
        ),
        name="local_stats",
    )(pos, logits, own, oth, assign, ids)


def chunk(far):
    return tuple((far, near) for near in range(4))


def hidden_product(groups, pos_ref, w_ref, g, outs):
    ny, nz, nx, sub, cols = w_ref.shape
    x_first, y, x = pos_ref[0] == 0, pos_ref[2], pos_ref[3]

    def block(far, near):
        dx = jnp.where(x_first, far, near)
        dy = jnp.where(x_first, near, far)
        w = w_ref[lax.rem(y + dy, ny), :, lax.rem(x + dx, nx)]
        return w.reshape(nz * sub, cols)

    for names, out in zip(groups, outs):
        w = jnp.concatenate([block(*name) for name in names], axis=0)
        product = lax.dot_general(w, g, (((1,), (1,)), ((), ())), preferred_element_type=F32)
        out[...] = product.reshape(out.shape)


def hidden_kernel(groups, pos_ref, w_ref, g_ref, *outs):
    hidden_product(groups, pos_ref, w_ref, g_ref[: outs[0].shape[-1], :], outs)


def hidden_part(pos, head5, g, groups):
    nz, sub = head5.shape[1], head5.shape[3]
    rows = g.shape[0] - LOSS_ROWS
    out_shape = [jax.ShapeDtypeStruct((len(names), nz, sub, rows), F32) for names in groups]
    return pl.pallas_call(
        functools.partial(hidden_kernel, groups),
        out_shape=out_shape,
        in_specs=[pl.BlockSpec(memory_space=pltpu.SMEM), WHOLE, WHOLE],
        out_specs=[WHOLE] * len(out_shape),
        compiler_params=params(16),
        cost_estimate=LIGHT,
        name="hidden_part",
    )(pos, head5, g)


def grad_kernel(
    pos_ref, l_ref, t_ref, ids_ref, scale_ref, s0, s1, s2, s3, w_ref, g_ref, far_ref
):
    rows, cols = l_ref.shape
    parts = (s0, s1, s2, s3)
    first, second = (
        jnp.concatenate([part[at : at + 1, :] for part in parts], axis=0) for at in (0, 1)
    )
    norm_s, norm_t, cross, picked = merge(first, second)
    terms = cross - norm_t + (1.0 + CE_WEIGHT) * norm_s
    terms = jnp.sum(terms, axis=1, keepdims=True) - CE_WEIGHT * picked
    high = terms.astype(BF16).astype(F32)
    middle = (terms - high).astype(BF16).astype(F32)
    low = terms - high - middle
    at = lax.broadcasted_iota(jnp.int32, (LOSS_ROWS, cols), 0)
    tail = jnp.where(at == 0, high, jnp.where(at == 1, middle, jnp.where(at == 2, low, 0.0)))
    g_ref[rows:, :] = tail.astype(BF16)
    norm_s, norm_t, ids, scale = columns_of(norm_s, norm_t, in_row(ids_ref), in_row(scale_ref))
    columns = pos_ref[1] + lax.broadcasted_iota(jnp.int32, (rows, cols), 1)
    hot = jnp.where(columns.astype(F32) == ids, CE_WEIGHT, 0.0)
    prob_s = jnp.exp(l_ref[...] - norm_s)
    prob_t = jnp.exp(t_ref[...].astype(F32) - norm_t)
    g = (scale * ((1.0 + CE_WEIGHT) * prob_s - prob_t - hot)).astype(BF16)
    g_ref[:rows, :] = g
    hidden_product((chunk(2),), pos_ref, w_ref, g, (far_ref,))


def grad_logits(pos, logits, teacher, ids, scale, parts, head5):
    rows, cols = logits.shape
    _, nz, _, sub, _ = head5.shape
    return pl.pallas_call(
        grad_kernel,
        out_shape=(
            jax.ShapeDtypeStruct((rows + LOSS_ROWS, cols), BF16),
            jax.ShapeDtypeStruct((4, nz, sub, rows), F32),
        ),
        in_specs=[pl.BlockSpec(memory_space=pltpu.SMEM)] + [WHOLE] * 9,
        out_specs=(WHOLE, WHOLE),
        compiler_params=params(16),
        cost_estimate=pl.CostEstimate(
            flops=8 * rows * cols,
            bytes_accessed=8 * rows * cols,
            transcendentals=2 * rows * cols,
        ),
        name="grad_logits",
    )(pos, logits, teacher, ids, scale, *parts, head5)


def head_kernel(pos_ref, own_ref, oth_ref, g_own_ref, g_oth_ref, out_ref, loss_ref, buf, sem):
    steps, block, _ = buf.shape
    rows = own_ref.shape[0]
    g = jnp.concatenate([g_own_ref[:rows, :], g_oth_ref[:rows, :]], axis=0)
    copies = []
    for i in range(steps):
        at = pl.ds(pl.multiple_of(pos_ref[0] * (steps * block) + i * block, block), block)
        h = jnp.concatenate([own_ref[:, at], oth_ref[:, at]], axis=0)
        total = lax.dot_general(h, g, (((0,), (0,)), ((), ())), preferred_element_type=F32)
        buf[i] = total.astype(BF16)
        copy = pltpu.make_async_copy(buf.at[i], out_ref.at[pl.ds(i * block, block)], sem.at[i])
        copy.start()
        copies.append(copy)

    def loss(ref):
        parts = ref[rows:, :128].astype(F32)
        return (parts[0:1] + parts[1:2]) + parts[2:3]

    loss_ref[...] = (loss(g_own_ref) + loss(g_oth_ref)) * (1.0 / (2 * rows))
    for copy in copies:
        copy.wait()


def head_grad(pos, hidden, hidden_oth, g, g_oth, steps=2):
    rows, depth = hidden.shape
    cols = g.shape[1]
    width = depth // 2
    return pl.pallas_call(
        head_kernel,
        out_shape=(
            jax.ShapeDtypeStruct((width, cols), BF16),
            jax.ShapeDtypeStruct((1, 128), F32),
        ),
        in_specs=[pl.BlockSpec(memory_space=pltpu.SMEM)] + [WHOLE] * 4,
        out_specs=(pl.BlockSpec(memory_space=pl.ANY), WHOLE),
        scratch_shapes=[
            pltpu.VMEM((steps, width // steps, cols), BF16),
            pltpu.SemaphoreType.DMA((steps,)),
        ],
        compiler_params=params(20),
        cost_estimate=LIGHT,
        name="head_grad",
    )(pos, hidden, hidden_oth, g, g_oth)


def body(teacher, hidden, head, ids, assignment, row_scale):
    c, x, y = (lax.axis_index(a) for a in ("c", "x", "y"))
    rows, depth = hidden.shape
    cols = head.shape[1]
    chips = ("y", "z", "x")
    ny, nz, nx = (lax.axis_size(a) for a in chips)
    pos = jnp.stack([c, lax.axis_index(chips) * cols, y, x]).astype(jnp.int32)
    assign = assignment.reshape(-1, 128)
    ids = ids.reshape(-1, 128)
    scale = row_scale.reshape(-1, 128)

    teacher_oth = shift(teacher, "c", 1)
    logits = student_logits(hidden, head)
    stats, teacher_rows = local_stats(pos, logits, teacher, teacher_oth, assign, ids)
    stats, scale = lax.optimization_barrier((stats, scale))
    stats = jnp.broadcast_to(stats[None], (nz * nx,) + stats.shape)
    stats = merge_stats(lax.all_to_all(stats, ("z", "x"), 0, 0, tiled=True))
    parts = [stats] + [shift(stats, "y", d) for d in (2, 1, 3)]
    hidden_oth = shift(lax.optimization_barrier((hidden, stats))[0], "c", 1)
    head5 = head.reshape(ny, nz, nx, depth // (ny * nz * nx), cols)
    g, far2 = grad_logits(pos, logits, teacher_rows, ids, scale, parts, head5)
    g, far2, hidden_oth = lax.optimization_barrier((g, far2, hidden_oth))

    def coded(value):
        return (value * SEND_SCALE).astype(F16)

    def taken(value):
        return value.astype(F32) * (1.0 / SEND_SCALE)

    far2, g = lax.optimization_barrier((coded(far2), g))
    got2 = shift_by_core(far2, 2, True)
    far1, far3 = hidden_part(pos, head5, g, (chunk(1), chunk(3)))
    far1, far3, g = lax.optimization_barrier((coded(far1), coded(far3), g))
    got = [got2, shift_by_core(far1, 1, True), shift_by_core(far3, 3, True)]
    g_oth = shift(g, "c", 1)
    (own,) = hidden_part(pos, head5, g, (chunk(0),))
    head_out, loss = head_grad(pos, hidden, hidden_oth, g, g_oth)
    loss = loss[0, :1]
    *got, loss, head_out = lax.optimization_barrier((*got, loss, head_out))
    total = own + sum(taken(v) for v in got)
    got = [shift_by_core(coded(total[d]), d, False) for d in (2, 1, 3)]
    both = coded(total[0] + sum(taken(v) for v in got))
    both = lax.all_to_all(both, "z", 0, 0, tiled=True)
    hidden_grad = jnp.sum(taken(both), axis=0).T.astype(BF16)
    return loss, hidden_grad, head_out


def solution(mesh):
    ny, nzx, nc = mesh.devices.shape
    nx = 4
    fine = Mesh(mesh.devices.reshape(ny, nzx // nx, nx, nc), ("y", "z", "x", "c"))
    vocab = ("y", "z", "x")
    in_specs = (
        P(None, vocab + ("c",)),
        P("c", None),
        P(None, vocab),
        P("c"),
        P(),
        P("c"),
    )
    out_specs = (P(), P("c", vocab), P("c", vocab))
    return jax.shard_map(body, mesh=fine, in_specs=in_specs, out_specs=out_specs, check_vma=False)
```

```python
import functools

import jax
import jax.numpy as jnp
import numpy as np
from jax import lax
from jax.experimental import pallas as pl
from jax.experimental.pallas import tpu as pltpu
from jax.sharding import Mesh, PartitionSpec as P

CE_WEIGHT = 0.5
SEND_SCALE = 64.0
SPARE = 256
LOSS_ROWS = 16
F32 = jnp.float32
BF16 = jnp.bfloat16
F16 = jnp.float16


LIGHT = pl.CostEstimate(flops=1, bytes_accessed=1, transcendentals=0)
WHOLE = pl.BlockSpec(memory_space=pltpu.VMEM)


def params(mib, *semantics):
    return pltpu.CompilerParams(
        vmem_limit_bytes=mib * 1024 * 1024, dimension_semantics=semantics or None
    )


def shift(a, axis, by):
    n = lax.axis_size(axis)
    return lax.ppermute(a, axis, [(i, (i + by) % n) for i in range(n)])


def shift_by_core(a, by, first):
    axes = ("y", "z", "x", "c")
    shape = tuple(lax.axis_size(axis) for axis in axes)
    pairs = []
    for source in np.ndindex(shape):
        target = list(source)
        axis = 2 if (source[3] == 0) == first else 0
        target[axis] = (target[axis] + by) % shape[axis]
        pairs.append(tuple(int(np.ravel_multi_index(at, shape)) for at in (source, target)))
    return lax.ppermute(a, axes, pairs)


def logits_kernel(steps, h_ref, w_ref, out_ref, h_buf, w_buf, h_sem, w_sem):
    kb = w_buf.shape[1]

    def copies(k):
        at = pl.ds(k * kb, kb)
        return (
            pltpu.make_async_copy(h_ref.at[:, at], h_buf.at[k], h_sem.at[k]),
            pltpu.make_async_copy(w_ref.at[at], w_buf.at[k], w_sem.at[k]),
        )

    for k in range(steps):
        for copy in copies(k):
            copy.start()
    out_ref[...] = jnp.zeros_like(out_ref)

    def step(k, carry):
        for copy in copies(k):
            copy.wait()
        out_ref[...] += jnp.dot(h_buf[k], w_buf[k], preferred_element_type=F32)
        return carry

    lax.fori_loop(0, steps, step, 0)


def student_logits(hidden, head, steps=4):
    rows, depth = hidden.shape
    cols = head.shape[1]
    kb = depth // steps
    return pl.pallas_call(
        functools.partial(logits_kernel, steps),
        out_shape=jax.ShapeDtypeStruct((rows, cols), F32),
        in_specs=[pl.BlockSpec(memory_space=pl.ANY)] * 2,
        out_specs=WHOLE,
        scratch_shapes=[
            pltpu.VMEM((steps, rows, kb), BF16),
            pltpu.VMEM((steps, kb, cols), BF16),
            pltpu.SemaphoreType.DMA((steps,)),
            pltpu.SemaphoreType.DMA((steps,)),
        ],
        compiler_params=params(52),
        cost_estimate=pl.CostEstimate(
            flops=2 * rows * depth * cols,
            bytes_accessed=2 * (rows * depth + depth * cols) + 4 * rows * cols,
            transcendentals=0,
        ),
        name="student_logits",
    )(hidden, head)


def columns_of(*rows):
    n = rows[0].shape[1]
    sub = lax.broadcasted_iota(jnp.int32, (128, n), 0)
    packed = jnp.zeros((128, n), F32)
    for at, row in enumerate(rows):
        packed = jnp.where(sub == at, row.astype(F32), packed)
    turned = packed.T
    return [turned[:, at : at + 1] for at in range(len(rows))]


def in_row(ref):
    return jnp.concatenate([ref[i : i + 1, :] for i in range(ref.shape[0])], axis=1)


def pack_stats(out_ref, lse_s, lse_t, cross, picked):
    rows = lse_s.shape[1]
    spare = out_ref.shape[1] - rows
    far = 2 * rows - spare
    out_ref[0:1, :rows] = lse_s
    out_ref[1:2, :rows] = lse_t
    out_ref[0:1, rows:] = cross[:, :spare]
    out_ref[1:2, rows:far] = cross[:, spare:]
    lane = lax.broadcasted_iota(jnp.int32, (1, out_ref.shape[1] - far), 1)
    out_ref[1:2, far:] = jnp.where(lane == 0, picked, 0.0)


def logsumexp(values):
    top = jnp.max(values, axis=0, keepdims=True)
    return top + jnp.log(jnp.sum(jnp.exp(values - top), axis=0, keepdims=True))


def merge(first, second):
    rows = first.shape[1] - SPARE
    far = 2 * rows - SPARE
    lse_s = logsumexp(first[:, :rows])
    lse_t = logsumexp(second[:, :rows])
    share_t = jnp.exp(second[:, :rows] - lse_t)
    cross = jnp.concatenate([first[:, rows:], second[:, rows:far]], axis=1)
    cross = jnp.sum(cross * share_t, axis=0, keepdims=True)
    picked = jnp.sum(second[:, far:], axis=0, keepdims=True)
    return lse_s, lse_t, cross, jnp.sum(picked, axis=1, keepdims=True)


def merge_kernel(in_ref, out_ref):
    pack_stats(out_ref, *merge(in_ref[:, 0, :], in_ref[:, 1, :]))


def merge_stats(stats):
    return pl.pallas_call(
        merge_kernel,
        out_shape=jax.ShapeDtypeStruct(stats.shape[1:], F32),
        in_specs=[WHOLE],
        out_specs=WHOLE,
        compiler_params=params(16),
        name="merge_stats",
    )(stats)


def stats_kernel(pos_ref, l_ref, own_ref, oth_ref, assign_ref, ids_ref, stats_ref, t_ref):
    rows, cols = l_ref.shape
    total = own_ref.shape[0]
    first = pos_ref[0] == 0
    assign = in_row(assign_ref)
    assign = jnp.where(first, assign[:, :rows], assign[:, rows:])
    assign, ids = columns_of(assign, in_row(ids_ref))
    lanes = lax.broadcasted_iota(jnp.int32, (rows, total), 1).astype(F32)
    pick = (lanes == assign).astype(BF16)
    own = jnp.dot(pick, own_ref[...], preferred_element_type=F32)
    oth = jnp.dot(pick, oth_ref[...], preferred_element_type=F32)
    teacher = jnp.concatenate([jnp.where(first, own, oth), jnp.where(first, oth, own)], axis=1)
    t_ref[...] = teacher.astype(BF16)
    logits = l_ref[...]
    top_s = jnp.max(logits, axis=1, keepdims=True)
    sum_s = jnp.sum(jnp.exp(logits - top_s), axis=1, keepdims=True)
    top_t = jnp.max(teacher, axis=1, keepdims=True)
    exp_t = jnp.exp(teacher - top_t)
    sum_t = jnp.sum(exp_t, axis=1, keepdims=True)
    cross = jnp.sum(exp_t * (teacher - logits), axis=1, keepdims=True)
    columns = pos_ref[1] + lax.broadcasted_iota(jnp.int32, (rows, cols), 1)
    hot = columns.astype(F32) == ids
    picked = jnp.sum(jnp.where(hot, logits, 0.0), axis=1, keepdims=True)
    lane = lax.broadcasted_iota(jnp.int32, (rows, 128), 1)
    packed = jnp.zeros((rows, 128), F32)
    for at, value in enumerate((top_s, sum_s, top_t, sum_t, cross, picked)):
        packed = jnp.where(lane == at, value, packed)
    packed = packed.T
    top_s, sum_s, top_t, sum_t, cross, picked = (packed[at : at + 1] for at in range(6))
    cross = cross / sum_t
    picked = jnp.sum(picked, axis=1, keepdims=True)
    pack_stats(stats_ref, top_s + jnp.log(sum_s), top_t + jnp.log(sum_t), cross, picked)


def local_stats(pos, logits, own, oth, assign, ids):
    rows, cols = logits.shape
    return pl.pallas_call(
        stats_kernel,
        out_shape=(
            jax.ShapeDtypeStruct((2, rows + SPARE), F32),
            jax.ShapeDtypeStruct((rows, cols), BF16),
        ),
        in_specs=[pl.BlockSpec(memory_space=pltpu.SMEM)] + [WHOLE] * 5,
        out_specs=(WHOLE, WHOLE),
        compiler_params=params(16),
        cost_estimate=pl.CostEstimate(
            flops=2 * rows * cols * own.shape[0],
            bytes_accessed=4 * rows * cols + 4 * own.size + 2 * rows * cols,
            transcendentals=2 * rows * cols,
        ),
        name="local_stats",
    )(pos, logits, own, oth, assign, ids)


def half(far, at):
    return ((far, 2 * at), (far, 2 * at + 1))


def hidden_product(groups, pos_ref, w_ref, g, outs):
    ny, nz, nx, sub, cols = w_ref.shape
    x_first, y, x = pos_ref[0] == 0, pos_ref[2], pos_ref[3]

    def block(far, near):
        dx = jnp.where(x_first, far, near)
        dy = jnp.where(x_first, near, far)
        w = w_ref[lax.rem(y + dy, ny), :, lax.rem(x + dx, nx)]
        return w.reshape(nz * sub, cols)

    for names, out in zip(groups, outs):
        w = jnp.concatenate([block(*name) for name in names], axis=0)
        product = lax.dot_general(w, g, (((1,), (1,)), ((), ())), preferred_element_type=F32)
        out[...] = product.reshape(out.shape)


def hidden_kernel(groups, pos_ref, w_ref, g_ref, *outs):
    hidden_product(groups, pos_ref, w_ref, g_ref[: outs[0].shape[-1], :], outs)


def hidden_part(pos, head5, g, groups):
    nz, sub = head5.shape[1], head5.shape[3]
    rows = g.shape[0] - LOSS_ROWS
    out_shape = [jax.ShapeDtypeStruct((len(names), nz, sub, rows), F32) for names in groups]
    return pl.pallas_call(
        functools.partial(hidden_kernel, groups),
        out_shape=out_shape,
        in_specs=[pl.BlockSpec(memory_space=pltpu.SMEM), WHOLE, WHOLE],
        out_specs=[WHOLE] * len(out_shape),
        compiler_params=params(16),
        cost_estimate=LIGHT,
        name="hidden_part",
    )(pos, head5, g)


def grad_kernel(
    pos_ref, l_ref, t_ref, ids_ref, scale_ref, s0, s1, s2, s3, w_ref, g_ref, low_ref, high_ref
):
    rows, cols = l_ref.shape
    parts = (s0, s1, s2, s3)
    first, second = (
        jnp.concatenate([part[at : at + 1, :] for part in parts], axis=0) for at in (0, 1)
    )
    norm_s, norm_t, cross, picked = merge(first, second)
    terms = cross - norm_t + (1.0 + CE_WEIGHT) * norm_s
    terms = jnp.sum(terms, axis=1, keepdims=True) - CE_WEIGHT * picked
    high = terms.astype(BF16).astype(F32)
    middle = (terms - high).astype(BF16).astype(F32)
    low = terms - high - middle
    at = lax.broadcasted_iota(jnp.int32, (LOSS_ROWS, cols), 0)
    tail = jnp.where(at == 0, high, jnp.where(at == 1, middle, jnp.where(at == 2, low, 0.0)))
    g_ref[rows:, :] = tail.astype(BF16)
    norm_s, norm_t, ids, scale = columns_of(norm_s, norm_t, in_row(ids_ref), in_row(scale_ref))
    columns = pos_ref[1] + lax.broadcasted_iota(jnp.int32, (rows, cols), 1)
    hot = jnp.where(columns.astype(F32) == ids, CE_WEIGHT, 0.0)
    prob_s = jnp.exp(l_ref[...] - norm_s)
    prob_t = jnp.exp(t_ref[...].astype(F32) - norm_t)
    g = (scale * ((1.0 + CE_WEIGHT) * prob_s - prob_t - hot)).astype(BF16)
    g_ref[:rows, :] = g
    hidden_product((half(2, 0), half(2, 1)), pos_ref, w_ref, g, (low_ref, high_ref))


def grad_logits(pos, logits, teacher, ids, scale, parts, head5):
    rows, cols = logits.shape
    _, nz, _, sub, _ = head5.shape
    return pl.pallas_call(
        grad_kernel,
        out_shape=(
            jax.ShapeDtypeStruct((rows + LOSS_ROWS, cols), BF16),
            jax.ShapeDtypeStruct((2, nz, sub, rows), F32),
            jax.ShapeDtypeStruct((2, nz, sub, rows), F32),
        ),
        in_specs=[pl.BlockSpec(memory_space=pltpu.SMEM)] + [WHOLE] * 9,
        out_specs=(WHOLE, WHOLE, WHOLE),
        compiler_params=params(16),
        cost_estimate=pl.CostEstimate(
            flops=8 * rows * cols,
            bytes_accessed=8 * rows * cols,
            transcendentals=2 * rows * cols,
        ),
        name="grad_logits",
    )(pos, logits, teacher, ids, scale, *parts, head5)


def head_kernel(pos_ref, own_ref, oth_ref, g_own_ref, g_oth_ref, out_ref, loss_ref, buf, sem):
    steps, block, _ = buf.shape
    rows = own_ref.shape[0]
    g = jnp.concatenate([g_own_ref[:rows, :], g_oth_ref[:rows, :]], axis=0)
    copies = []
    for i in range(steps):
        at = pl.ds(pl.multiple_of(pos_ref[0] * (steps * block) + i * block, block), block)
        h = jnp.concatenate([own_ref[:, at], oth_ref[:, at]], axis=0)
        total = lax.dot_general(h, g, (((0,), (0,)), ((), ())), preferred_element_type=F32)
        buf[i] = total.astype(BF16)
        copy = pltpu.make_async_copy(buf.at[i], out_ref.at[pl.ds(i * block, block)], sem.at[i])
        copy.start()
        copies.append(copy)

    def loss(ref):
        parts = ref[rows:, :128].astype(F32)
        return (parts[0:1] + parts[1:2]) + parts[2:3]

    loss_ref[...] = (loss(g_own_ref) + loss(g_oth_ref)) * (1.0 / (2 * rows))
    for copy in copies:
        copy.wait()


def head_grad(pos, hidden, hidden_oth, g, g_oth, steps=2):
    rows, depth = hidden.shape
    cols = g.shape[1]
    width = depth // 2
    return pl.pallas_call(
        head_kernel,
        out_shape=(
            jax.ShapeDtypeStruct((width, cols), BF16),
            jax.ShapeDtypeStruct((1, 128), F32),
        ),
        in_specs=[pl.BlockSpec(memory_space=pltpu.SMEM)] + [WHOLE] * 4,
        out_specs=(pl.BlockSpec(memory_space=pl.ANY), WHOLE),
        scratch_shapes=[
            pltpu.VMEM((steps, width // steps, cols), BF16),
            pltpu.SemaphoreType.DMA((steps,)),
        ],
        compiler_params=params(20),
        cost_estimate=LIGHT,
        name="head_grad",
    )(pos, hidden, hidden_oth, g, g_oth)


def body(teacher, hidden, head, ids, assignment, row_scale):
    c, x, y = (lax.axis_index(a) for a in ("c", "x", "y"))
    rows, depth = hidden.shape
    cols = head.shape[1]
    chips = ("y", "z", "x")
    ny, nz, nx = (lax.axis_size(a) for a in chips)
    pos = jnp.stack([c, lax.axis_index(chips) * cols, y, x]).astype(jnp.int32)
    assign = assignment.reshape(-1, 128)
    ids = ids.reshape(-1, 128)
    scale = row_scale.reshape(-1, 128)

    teacher_oth = shift(teacher, "c", 1)
    logits = student_logits(hidden, head)
    stats, teacher_rows = local_stats(pos, logits, teacher, teacher_oth, assign, ids)
    stats, scale = lax.optimization_barrier((stats, scale))
    stats = jnp.broadcast_to(stats[None], (nz * nx,) + stats.shape)
    stats = merge_stats(lax.all_to_all(stats, ("z", "x"), 0, 0, tiled=True))
    parts = [stats] + [shift(stats, "y", d) for d in (2, 1, 3)]
    hidden_oth = shift(lax.optimization_barrier((hidden, stats))[0], "c", 1)
    head5 = head.reshape(ny, nz, nx, depth // (ny * nz * nx), cols)
    g, low2, high2 = grad_logits(pos, logits, teacher_rows, ids, scale, parts, head5)
    g, low2, high2, hidden_oth = lax.optimization_barrier((g, low2, high2, hidden_oth))

    def coded(value):
        return (value * SEND_SCALE).astype(F16)

    def taken(value):
        return value.astype(F32) * (1.0 / SEND_SCALE)

    low2, high2, g = lax.optimization_barrier((coded(low2), coded(high2), g))
    from_back, from_front = shift_by_core(low2, 1, True), shift_by_core(high2, -1, True)
    groups = (half(1, 1), half(3, 0), half(1, 0), half(3, 1))
    high1, low3, low1, high3 = hidden_part(pos, head5, g, groups)
    high1, low3, low1, high3 = lax.optimization_barrier((coded(high1), coded(low3), low1, high3))
    to_high, to_low = shift_by_core(high1, 1, True), shift_by_core(low3, -1, True)
    low1, high3 = coded(low1 + taken(from_back)), coded(high3 + taken(from_front))
    low1, high3, g = lax.optimization_barrier((low1, high3, g))
    to_low = [to_low, shift_by_core(low1, 1, True)]
    to_high = [to_high, shift_by_core(high3, -1, True)]
    g_oth = shift(g, "c", 1)
    low, high = hidden_part(pos, head5, g, (half(0, 0), half(0, 1)))
    head_out, loss = head_grad(pos, hidden, hidden_oth, g, g_oth)
    loss = loss[0, :1]
    *got, loss, head_out = lax.optimization_barrier((*to_low, *to_high, loss, head_out))
    low = low + taken(got[0]) + taken(got[1])
    high = high + taken(got[2]) + taken(got[3])
    got = [shift_by_core(coded(v), d, False) for d, v in ((2, high[0]), (1, low[1]), (3, high[1]))]
    both = coded(low[0] + sum(taken(v) for v in got))
    both = lax.all_to_all(both, "z", 0, 0, tiled=True)
    hidden_grad = jnp.sum(taken(both), axis=0).T.astype(BF16)
    return loss, hidden_grad, head_out


def solution(mesh):
    ny, nzx, nc = mesh.devices.shape
    nx = 4
    fine = Mesh(mesh.devices.reshape(ny, nzx // nx, nx, nc), ("y", "z", "x", "c"))
    vocab = ("y", "z", "x")
    in_specs = (
        P(None, vocab + ("c",)),
        P("c", None),
        P(None, vocab),
        P("c"),
        P(),
        P("c"),
    )
    out_specs = (P(), P("c", vocab), P("c", vocab))
    return jax.shard_map(body, mesh=fine, in_specs=in_specs, out_specs=out_specs, check_vma=False)
```

```python
import functools

import jax
import jax.numpy as jnp
import numpy as np
from jax import lax
from jax.experimental import pallas as pl
from jax.experimental.pallas import tpu as pltpu
from jax.sharding import Mesh, PartitionSpec as P

CE_WEIGHT = 0.5
SEND_SCALE = 64.0
SPARE = 256
LOSS_ROWS = 16
F32 = jnp.float32
BF16 = jnp.bfloat16
F16 = jnp.float16


LIGHT = pl.CostEstimate(flops=1, bytes_accessed=1, transcendentals=0)
WHOLE = pl.BlockSpec(memory_space=pltpu.VMEM)


def params(mib, *semantics):
    return pltpu.CompilerParams(
        vmem_limit_bytes=mib * 1024 * 1024, dimension_semantics=semantics or None
    )


def shift(a, axis, by):
    n = lax.axis_size(axis)
    return lax.ppermute(a, axis, [(i, (i + by) % n) for i in range(n)])


def shift_by_core(a, by, first):
    axes = ("y", "z", "x", "c")
    shape = tuple(lax.axis_size(axis) for axis in axes)
    pairs = []
    for source in np.ndindex(shape):
        target = list(source)
        axis = 2 if (source[3] == 0) == first else 0
        target[axis] = (target[axis] + by) % shape[axis]
        pairs.append(tuple(int(np.ravel_multi_index(at, shape)) for at in (source, target)))
    return lax.ppermute(a, axes, pairs)


def logits_kernel(steps, h_ref, w_ref, out_ref, h_buf, w_buf, h_sem, w_sem):
    kb = w_buf.shape[1]

    def copies(k):
        at = pl.ds(k * kb, kb)
        return (
            pltpu.make_async_copy(h_ref.at[:, at], h_buf.at[k], h_sem.at[k]),
            pltpu.make_async_copy(w_ref.at[at], w_buf.at[k], w_sem.at[k]),
        )

    for k in range(steps):
        for copy in copies(k):
            copy.start()
    out_ref[...] = jnp.zeros_like(out_ref)

    def step(k, carry):
        for copy in copies(k):
            copy.wait()
        out_ref[...] += jnp.dot(h_buf[k], w_buf[k], preferred_element_type=F32)
        return carry

    lax.fori_loop(0, steps, step, 0)


def student_logits(hidden, head, steps=4):
    rows, depth = hidden.shape
    cols = head.shape[1]
    kb = depth // steps
    return pl.pallas_call(
        functools.partial(logits_kernel, steps),
        out_shape=jax.ShapeDtypeStruct((rows, cols), F32),
        in_specs=[pl.BlockSpec(memory_space=pl.ANY)] * 2,
        out_specs=WHOLE,
        scratch_shapes=[
            pltpu.VMEM((steps, rows, kb), BF16),
            pltpu.VMEM((steps, kb, cols), BF16),
            pltpu.SemaphoreType.DMA((steps,)),
            pltpu.SemaphoreType.DMA((steps,)),
        ],
        compiler_params=params(52),
        cost_estimate=pl.CostEstimate(
            flops=2 * rows * depth * cols,
            bytes_accessed=2 * (rows * depth + depth * cols) + 4 * rows * cols,
            transcendentals=0,
        ),
        name="student_logits",
    )(hidden, head)


def columns_of(*rows):
    n = rows[0].shape[1]
    sub = lax.broadcasted_iota(jnp.int32, (128, n), 0)
    packed = jnp.zeros((128, n), F32)
    for at, row in enumerate(rows):
        packed = jnp.where(sub == at, row.astype(F32), packed)
    turned = packed.T
    return [turned[:, at : at + 1] for at in range(len(rows))]


def in_row(ref):
    return jnp.concatenate([ref[i : i + 1, :] for i in range(ref.shape[0])], axis=1)


def pack_stats(out_ref, lse_s, lse_t, cross, picked):
    rows = lse_s.shape[1]
    spare = out_ref.shape[1] - rows
    far = 2 * rows - spare
    out_ref[0:1, :rows] = lse_s
    out_ref[1:2, :rows] = lse_t
    out_ref[0:1, rows:] = cross[:, :spare]
    out_ref[1:2, rows:far] = cross[:, spare:]
    lane = lax.broadcasted_iota(jnp.int32, (1, out_ref.shape[1] - far), 1)
    out_ref[1:2, far:] = jnp.where(lane == 0, picked, 0.0)


def logsumexp(values):
    top = jnp.max(values, axis=0, keepdims=True)
    return top + jnp.log(jnp.sum(jnp.exp(values - top), axis=0, keepdims=True))


def merge(first, second):
    rows = first.shape[1] - SPARE
    far = 2 * rows - SPARE
    lse_s = logsumexp(first[:, :rows])
    lse_t = logsumexp(second[:, :rows])
    share_t = jnp.exp(second[:, :rows] - lse_t)
    cross = jnp.concatenate([first[:, rows:], second[:, rows:far]], axis=1)
    cross = jnp.sum(cross * share_t, axis=0, keepdims=True)
    picked = jnp.sum(second[:, far:], axis=0, keepdims=True)
    return lse_s, lse_t, cross, jnp.sum(picked, axis=1, keepdims=True)


def merge_kernel(in_ref, out_ref):
    pack_stats(out_ref, *merge(in_ref[:, 0, :], in_ref[:, 1, :]))


def merge_stats(stats):
    return pl.pallas_call(
        merge_kernel,
        out_shape=jax.ShapeDtypeStruct(stats.shape[1:], F32),
        in_specs=[WHOLE],
        out_specs=WHOLE,
        compiler_params=params(16),
        name="merge_stats",
    )(stats)


def stats_kernel(pos_ref, l_ref, own_ref, oth_ref, assign_ref, ids_ref, stats_ref, t_ref):
    rows, cols = l_ref.shape
    total = own_ref.shape[0]
    first = pos_ref[0] == 0
    assign = in_row(assign_ref)
    assign = jnp.where(first, assign[:, :rows], assign[:, rows:])
    assign, ids = columns_of(assign, in_row(ids_ref))
    lanes = lax.broadcasted_iota(jnp.int32, (rows, total), 1).astype(F32)
    pick = (lanes == assign).astype(BF16)
    own = jnp.dot(pick, own_ref[...], preferred_element_type=F32)
    oth = jnp.dot(pick, oth_ref[...], preferred_element_type=F32)
    teacher = jnp.concatenate([jnp.where(first, own, oth), jnp.where(first, oth, own)], axis=1)
    t_ref[...] = teacher.astype(BF16)
    logits = l_ref[...]
    top_s = jnp.max(logits, axis=1, keepdims=True)
    sum_s = jnp.sum(jnp.exp(logits - top_s), axis=1, keepdims=True)
    top_t = jnp.max(teacher, axis=1, keepdims=True)
    exp_t = jnp.exp(teacher - top_t)
    sum_t = jnp.sum(exp_t, axis=1, keepdims=True)
    cross = jnp.sum(exp_t * (teacher - logits), axis=1, keepdims=True)
    columns = pos_ref[1] + lax.broadcasted_iota(jnp.int32, (rows, cols), 1)
    hot = columns.astype(F32) == ids
    picked = jnp.sum(jnp.where(hot, logits, 0.0), axis=1, keepdims=True)
    lane = lax.broadcasted_iota(jnp.int32, (rows, 128), 1)
    packed = jnp.zeros((rows, 128), F32)
    for at, value in enumerate((top_s, sum_s, top_t, sum_t, cross, picked)):
        packed = jnp.where(lane == at, value, packed)
    packed = packed.T
    top_s, sum_s, top_t, sum_t, cross, picked = (packed[at : at + 1] for at in range(6))
    cross = cross / sum_t
    picked = jnp.sum(picked, axis=1, keepdims=True)
    pack_stats(stats_ref, top_s + jnp.log(sum_s), top_t + jnp.log(sum_t), cross, picked)


def local_stats(pos, logits, own, oth, assign, ids):
    rows, cols = logits.shape
    return pl.pallas_call(
        stats_kernel,
        out_shape=(
            jax.ShapeDtypeStruct((2, rows + SPARE), F32),
            jax.ShapeDtypeStruct((rows, cols), BF16),
        ),
        in_specs=[pl.BlockSpec(memory_space=pltpu.SMEM)] + [WHOLE] * 5,
        out_specs=(WHOLE, WHOLE),
        compiler_params=params(16),
        cost_estimate=pl.CostEstimate(
            flops=2 * rows * cols * own.shape[0],
            bytes_accessed=4 * rows * cols + 4 * own.size + 2 * rows * cols,
            transcendentals=2 * rows * cols,
        ),
        name="local_stats",
    )(pos, logits, own, oth, assign, ids)


def chunk(far):
    return tuple((far, near) for near in range(4))


def hidden_product(groups, pos_ref, w_ref, g, outs):
    ny, nz, nx, sub, cols = w_ref.shape
    x_first, y, x = pos_ref[0] == 0, pos_ref[2], pos_ref[3]

    def block(far, near):
        dx = jnp.where(x_first, far, near)
        dy = jnp.where(x_first, near, far)
        w = w_ref[lax.rem(y + dy, ny), :, lax.rem(x + dx, nx)]
        return w.reshape(nz * sub, cols)

    for names, out in zip(groups, outs):
        w = jnp.concatenate([block(*name) for name in names], axis=0)
        product = lax.dot_general(w, g, (((1,), (1,)), ((), ())), preferred_element_type=F32)
        out[...] = product.reshape(out.shape)


def hidden_kernel(groups, pos_ref, w_ref, g_ref, *outs):
    hidden_product(groups, pos_ref, w_ref, g_ref[: outs[0].shape[-1], :], outs)


def hidden_part(pos, head5, g, groups):
    nz, sub = head5.shape[1], head5.shape[3]
    rows = g.shape[0] - LOSS_ROWS
    out_shape = [jax.ShapeDtypeStruct((len(names), nz, sub, rows), F32) for names in groups]
    return pl.pallas_call(
        functools.partial(hidden_kernel, groups),
        out_shape=out_shape,
        in_specs=[pl.BlockSpec(memory_space=pltpu.SMEM), WHOLE, WHOLE],
        out_specs=[WHOLE] * len(out_shape),
        compiler_params=params(16),
        cost_estimate=LIGHT,
        name="hidden_part",
    )(pos, head5, g)


def grad_kernel(pos_ref, l_ref, t_ref, ids_ref, scale_ref, stats_ref, w_ref, g_ref, far_ref):
    rows, cols = l_ref.shape
    norm_s, norm_t, cross, picked = merge(stats_ref[:, 0, :], stats_ref[:, 1, :])
    terms = cross - norm_t + (1.0 + CE_WEIGHT) * norm_s
    terms = jnp.sum(terms, axis=1, keepdims=True) - CE_WEIGHT * picked
    high = terms.astype(BF16).astype(F32)
    middle = (terms - high).astype(BF16).astype(F32)
    low = terms - high - middle
    at = lax.broadcasted_iota(jnp.int32, (LOSS_ROWS, cols), 0)
    tail = jnp.where(at == 0, high, jnp.where(at == 1, middle, jnp.where(at == 2, low, 0.0)))
    g_ref[rows:, :] = tail.astype(BF16)
    norm_s, norm_t, ids, scale = columns_of(norm_s, norm_t, in_row(ids_ref), in_row(scale_ref))
    columns = pos_ref[1] + lax.broadcasted_iota(jnp.int32, (rows, cols), 1)
    hot = jnp.where(columns.astype(F32) == ids, CE_WEIGHT, 0.0)
    prob_s = jnp.exp(l_ref[...] - norm_s)
    prob_t = jnp.exp(t_ref[...].astype(F32) - norm_t)
    g = (scale * ((1.0 + CE_WEIGHT) * prob_s - prob_t - hot)).astype(BF16)
    g_ref[:rows, :] = g
    hidden_product((chunk(2),), pos_ref, w_ref, g, (far_ref,))


def grad_logits(pos, logits, teacher, ids, scale, stats, head5):
    rows, cols = logits.shape
    _, nz, _, sub, _ = head5.shape
    return pl.pallas_call(
        grad_kernel,
        out_shape=(
            jax.ShapeDtypeStruct((rows + LOSS_ROWS, cols), BF16),
            jax.ShapeDtypeStruct((4, nz, sub, rows), F32),
        ),
        in_specs=[pl.BlockSpec(memory_space=pltpu.SMEM)] + [WHOLE] * 6,
        out_specs=(WHOLE, WHOLE),
        compiler_params=params(16),
        cost_estimate=pl.CostEstimate(
            flops=8 * rows * cols,
            bytes_accessed=8 * rows * cols,
            transcendentals=2 * rows * cols,
        ),
        name="grad_logits",
    )(pos, logits, teacher, ids, scale, stats, head5)


def head_kernel(pos_ref, own_ref, oth_ref, g_own_ref, g_oth_ref, out_ref, loss_ref, buf, sem):
    steps, block, _ = buf.shape
    rows = own_ref.shape[0]
    g = jnp.concatenate([g_own_ref[:rows, :], g_oth_ref[:rows, :]], axis=0)
    copies = []
    for i in range(steps):
        at = pl.ds(pl.multiple_of(pos_ref[0] * (steps * block) + i * block, block), block)
        h = jnp.concatenate([own_ref[:, at], oth_ref[:, at]], axis=0)
        total = lax.dot_general(h, g, (((0,), (0,)), ((), ())), preferred_element_type=F32)
        buf[i] = total.astype(BF16)
        copy = pltpu.make_async_copy(buf.at[i], out_ref.at[pl.ds(i * block, block)], sem.at[i])
        copy.start()
        copies.append(copy)

    def loss(ref):
        parts = ref[rows:, :128].astype(F32)
        return (parts[0:1] + parts[1:2]) + parts[2:3]

    loss_ref[...] = (loss(g_own_ref) + loss(g_oth_ref)) * (1.0 / (2 * rows))
    for copy in copies:
        copy.wait()


def head_grad(pos, hidden, hidden_oth, g, g_oth, steps=2):
    rows, depth = hidden.shape
    cols = g.shape[1]
    width = depth // 2
    return pl.pallas_call(
        head_kernel,
        out_shape=(
            jax.ShapeDtypeStruct((width, cols), BF16),
            jax.ShapeDtypeStruct((1, 128), F32),
        ),
        in_specs=[pl.BlockSpec(memory_space=pltpu.SMEM)] + [WHOLE] * 4,
        out_specs=(pl.BlockSpec(memory_space=pl.ANY), WHOLE),
        scratch_shapes=[
            pltpu.VMEM((steps, width // steps, cols), BF16),
            pltpu.SemaphoreType.DMA((steps,)),
        ],
        compiler_params=params(20),
        cost_estimate=LIGHT,
        name="head_grad",
    )(pos, hidden, hidden_oth, g, g_oth)


def body(teacher, hidden, head, ids, assignment, row_scale):
    c, x, y = (lax.axis_index(a) for a in ("c", "x", "y"))
    rows, depth = hidden.shape
    cols = head.shape[1]
    chips = ("y", "z", "x")
    ny, nz, nx = (lax.axis_size(a) for a in chips)
    pos = jnp.stack([c, lax.axis_index(chips) * cols, y, x]).astype(jnp.int32)
    assign = assignment.reshape(-1, 128)
    ids = ids.reshape(-1, 128)
    scale = row_scale.reshape(-1, 128)

    teacher_oth = shift(teacher, "c", 1)
    hidden_oth = shift(lax.optimization_barrier((hidden, pos))[0], "c", 1)
    logits = student_logits(hidden, head)
    stats, teacher_rows = local_stats(pos, logits, teacher, teacher_oth, assign, ids)
    stats, scale, hidden_oth = lax.optimization_barrier((stats, scale, hidden_oth))

    def gathered(value, axes, n):
        value = jnp.broadcast_to(value[None], (n,) + value.shape)
        return lax.all_to_all(value, axes, 0, 0, tiled=True)

    stats = gathered(merge_stats(gathered(stats, ("y", "x"), ny * nx)), "z", nz)
    head5 = head.reshape(ny, nz, nx, depth // (ny * nz * nx), cols)
    g, far2 = grad_logits(pos, logits, teacher_rows, ids, scale, stats, head5)

    def coded(value):
        return (value * SEND_SCALE).astype(F16)

    def taken(value):
        return value.astype(F32) * (1.0 / SEND_SCALE)

    far2, g = lax.optimization_barrier((coded(far2), g))
    got2 = shift_by_core(far2, 2, True)
    far1, far3 = hidden_part(pos, head5, g, (chunk(1), chunk(3)))
    far1, far3, g = lax.optimization_barrier((coded(far1), coded(far3), g))
    got = [got2, shift_by_core(far1, 1, True), shift_by_core(far3, 3, True)]
    g_oth = shift(g, "c", 1)
    (own,) = hidden_part(pos, head5, g, (chunk(0),))
    head_out, loss = head_grad(pos, hidden, hidden_oth, g, g_oth)
    loss = loss[0, :1]
    *got, loss, head_out = lax.optimization_barrier((*got, loss, head_out))
    total = own + sum(taken(v) for v in got)
    got = [shift_by_core(coded(total[d]), d, False) for d in (2, 1, 3)]
    both = coded(total[0] + sum(taken(v) for v in got))
    both = lax.all_to_all(both, "z", 0, 0, tiled=True)
    hidden_grad = jnp.sum(taken(both), axis=0).T.astype(BF16)
    return loss, hidden_grad, head_out


def solution(mesh):
    ny, nzx, nc = mesh.devices.shape
    nx = 4
    fine = Mesh(mesh.devices.reshape(ny, nzx // nx, nx, nc), ("y", "z", "x", "c"))
    vocab = ("y", "z", "x")
    in_specs = (
        P(None, vocab + ("c",)),
        P("c", None),
        P(None, vocab),
        P("c"),
        P(),
        P("c"),
    )
    out_specs = (P(), P("c", vocab), P("c", vocab))
    return jax.shard_map(body, mesh=fine, in_specs=in_specs, out_specs=out_specs, check_vma=False)
```

```python
import functools

import jax
import jax.numpy as jnp
import numpy as np
from jax import lax
from jax.experimental import pallas as pl
from jax.experimental.pallas import tpu as pltpu
from jax.sharding import Mesh, PartitionSpec as P

CE_WEIGHT = 0.5
SEND_SCALE = 64.0
SPARE = 256
LOSS_ROWS = 16
F32 = jnp.float32
BF16 = jnp.bfloat16
F16 = jnp.float16


LIGHT = pl.CostEstimate(flops=1, bytes_accessed=1, transcendentals=0)
WHOLE = pl.BlockSpec(memory_space=pltpu.VMEM)


def params(mib, *semantics):
    return pltpu.CompilerParams(
        vmem_limit_bytes=mib * 1024 * 1024, dimension_semantics=semantics or None
    )


def shift(a, axis, by):
    n = lax.axis_size(axis)
    return lax.ppermute(a, axis, [(i, (i + by) % n) for i in range(n)])


def shift_by_core(a, by, first):
    axes = ("y", "z", "x", "c")
    shape = tuple(lax.axis_size(axis) for axis in axes)
    pairs = []
    for source in np.ndindex(shape):
        target = list(source)
        axis = 2 if (source[3] == 0) == first else 0
        target[axis] = (target[axis] + by) % shape[axis]
        pairs.append(tuple(int(np.ravel_multi_index(at, shape)) for at in (source, target)))
    return lax.ppermute(a, axes, pairs)


def logits_kernel(steps, h_ref, w_ref, out_ref, h_buf, w_buf, h_sem, w_sem):
    kb = w_buf.shape[1]

    def copies(k):
        at = pl.ds(k * kb, kb)
        return (
            pltpu.make_async_copy(h_ref.at[:, at], h_buf.at[k], h_sem.at[k]),
            pltpu.make_async_copy(w_ref.at[at], w_buf.at[k], w_sem.at[k]),
        )

    for k in range(steps):
        for copy in copies(k):
            copy.start()
    out_ref[...] = jnp.zeros_like(out_ref)

    def step(k, carry):
        for copy in copies(k):
            copy.wait()
        out_ref[...] += jnp.dot(h_buf[k], w_buf[k], preferred_element_type=F32)
        return carry

    lax.fori_loop(0, steps, step, 0)


def student_logits(hidden, head, steps=4):
    rows, depth = hidden.shape
    cols = head.shape[1]
    kb = depth // steps
    return pl.pallas_call(
        functools.partial(logits_kernel, steps),
        out_shape=jax.ShapeDtypeStruct((rows, cols), F32),
        in_specs=[pl.BlockSpec(memory_space=pl.ANY)] * 2,
        out_specs=WHOLE,
        scratch_shapes=[
            pltpu.VMEM((steps, rows, kb), BF16),
            pltpu.VMEM((steps, kb, cols), BF16),
            pltpu.SemaphoreType.DMA((steps,)),
            pltpu.SemaphoreType.DMA((steps,)),
        ],
        compiler_params=params(52),
        cost_estimate=pl.CostEstimate(
            flops=2 * rows * depth * cols,
            bytes_accessed=2 * (rows * depth + depth * cols) + 4 * rows * cols,
            transcendentals=0,
        ),
        name="student_logits",
    )(hidden, head)


def columns_of(*rows):
    n = rows[0].shape[1]
    sub = lax.broadcasted_iota(jnp.int32, (128, n), 0)
    packed = jnp.zeros((128, n), F32)
    for at, row in enumerate(rows):
        packed = jnp.where(sub == at, row.astype(F32), packed)
    turned = packed.T
    return [turned[:, at : at + 1] for at in range(len(rows))]


def in_row(ref):
    return jnp.concatenate([ref[i : i + 1, :] for i in range(ref.shape[0])], axis=1)


def pack_stats(out_ref, lse_s, lse_t, cross, picked):
    rows = lse_s.shape[1]
    spare = out_ref.shape[1] - rows
    far = 2 * rows - spare
    out_ref[0:1, :rows] = lse_s
    out_ref[1:2, :rows] = lse_t
    out_ref[0:1, rows:] = cross[:, :spare]
    out_ref[1:2, rows:far] = cross[:, spare:]
    lane = lax.broadcasted_iota(jnp.int32, (1, out_ref.shape[1] - far), 1)
    out_ref[1:2, far:] = jnp.where(lane == 0, picked, 0.0)


def logsumexp(values):
    top = jnp.max(values, axis=0, keepdims=True)
    return top + jnp.log(jnp.sum(jnp.exp(values - top), axis=0, keepdims=True))


def merge(first, second):
    rows = first.shape[1] - SPARE
    far = 2 * rows - SPARE
    lse_s = logsumexp(first[:, :rows])
    lse_t = logsumexp(second[:, :rows])
    share_t = jnp.exp(second[:, :rows] - lse_t)
    cross = jnp.concatenate([first[:, rows:], second[:, rows:far]], axis=1)
    cross = jnp.sum(cross * share_t, axis=0, keepdims=True)
    picked = jnp.sum(second[:, far:], axis=0, keepdims=True)
    return lse_s, lse_t, cross, jnp.sum(picked, axis=1, keepdims=True)


def merge_kernel(in_ref, out_ref):
    pack_stats(out_ref, *merge(in_ref[:, 0, :], in_ref[:, 1, :]))


def merge_stats(stats):
    return pl.pallas_call(
        merge_kernel,
        out_shape=jax.ShapeDtypeStruct(stats.shape[1:], F32),
        in_specs=[WHOLE],
        out_specs=WHOLE,
        compiler_params=params(16),
        name="merge_stats",
    )(stats)


def stats_kernel(pos_ref, l_ref, own_ref, oth_ref, assign_ref, ids_ref, stats_ref, t_ref):
    rows, cols = l_ref.shape
    total = own_ref.shape[0]
    first = pos_ref[0] == 0
    assign = in_row(assign_ref)
    assign = jnp.where(first, assign[:, :rows], assign[:, rows:])
    assign, ids = columns_of(assign, in_row(ids_ref))
    lanes = lax.broadcasted_iota(jnp.int32, (rows, total), 1).astype(F32)
    pick = (lanes == assign).astype(BF16)
    own = jnp.dot(pick, own_ref[...], preferred_element_type=F32)
    oth = jnp.dot(pick, oth_ref[...], preferred_element_type=F32)
    teacher = jnp.concatenate([jnp.where(first, own, oth), jnp.where(first, oth, own)], axis=1)
    t_ref[...] = teacher.astype(BF16)
    logits = l_ref[...]
    top_s = jnp.max(logits, axis=1, keepdims=True)
    sum_s = jnp.sum(jnp.exp(logits - top_s), axis=1, keepdims=True)
    top_t = jnp.max(teacher, axis=1, keepdims=True)
    exp_t = jnp.exp(teacher - top_t)
    sum_t = jnp.sum(exp_t, axis=1, keepdims=True)
    cross = jnp.sum(exp_t * (teacher - logits), axis=1, keepdims=True)
    columns = pos_ref[1] + lax.broadcasted_iota(jnp.int32, (rows, cols), 1)
    hot = columns.astype(F32) == ids
    picked = jnp.sum(jnp.where(hot, logits, 0.0), axis=1, keepdims=True)
    lane = lax.broadcasted_iota(jnp.int32, (rows, 128), 1)
    packed = jnp.zeros((rows, 128), F32)
    for at, value in enumerate((top_s, sum_s, top_t, sum_t, cross, picked)):
        packed = jnp.where(lane == at, value, packed)
    packed = packed.T
    top_s, sum_s, top_t, sum_t, cross, picked = (packed[at : at + 1] for at in range(6))
    cross = cross / sum_t
    picked = jnp.sum(picked, axis=1, keepdims=True)
    pack_stats(stats_ref, top_s + jnp.log(sum_s), top_t + jnp.log(sum_t), cross, picked)


def local_stats(pos, logits, own, oth, assign, ids):
    rows, cols = logits.shape
    return pl.pallas_call(
        stats_kernel,
        out_shape=(
            jax.ShapeDtypeStruct((2, rows + SPARE), F32),
            jax.ShapeDtypeStruct((rows, cols), BF16),
        ),
        in_specs=[pl.BlockSpec(memory_space=pltpu.SMEM)] + [WHOLE] * 5,
        out_specs=(WHOLE, WHOLE),
        compiler_params=params(16),
        cost_estimate=pl.CostEstimate(
            flops=2 * rows * cols * own.shape[0],
            bytes_accessed=4 * rows * cols + 4 * own.size + 2 * rows * cols,
            transcendentals=2 * rows * cols,
        ),
        name="local_stats",
    )(pos, logits, own, oth, assign, ids)


def chunk(far):
    return tuple((far, near) for near in range(4))


def hidden_product(groups, pos_ref, w_ref, g, outs):
    ny, nz, nx, sub, cols = w_ref.shape
    x_first, y, x = pos_ref[0] == 0, pos_ref[2], pos_ref[3]

    def block(far, near):
        dx = jnp.where(x_first, far, near)
        dy = jnp.where(x_first, near, far)
        w = w_ref[lax.rem(y + dy, ny), :, lax.rem(x + dx, nx)]
        return w.reshape(nz * sub, cols)

    for names, out in zip(groups, outs):
        w = jnp.concatenate([block(*name) for name in names], axis=0)
        product = lax.dot_general(w, g, (((1,), (1,)), ((), ())), preferred_element_type=F32)
        out[...] = product.reshape(out.shape)


def hidden_kernel(groups, pos_ref, w_ref, g_ref, *outs):
    hidden_product(groups, pos_ref, w_ref, g_ref[: outs[0].shape[-1], :], outs)


def hidden_part(pos, head5, g, groups):
    nz, sub = head5.shape[1], head5.shape[3]
    rows = g.shape[0] - LOSS_ROWS
    out_shape = [jax.ShapeDtypeStruct((len(names), nz, sub, rows), F32) for names in groups]
    return pl.pallas_call(
        functools.partial(hidden_kernel, groups),
        out_shape=out_shape,
        in_specs=[pl.BlockSpec(memory_space=pltpu.SMEM), WHOLE, WHOLE],
        out_specs=[WHOLE] * len(out_shape),
        compiler_params=params(16),
        cost_estimate=LIGHT,
        name="hidden_part",
    )(pos, head5, g)


def grad_kernel(pos_ref, l_ref, t_ref, ids_ref, scale_ref, stats_ref, w_ref, g_ref, far_ref):
    rows, cols = l_ref.shape
    norm_s, norm_t, cross, picked = merge(stats_ref[:, 0, :], stats_ref[:, 1, :])
    terms = cross - norm_t + (1.0 + CE_WEIGHT) * norm_s
    terms = jnp.sum(terms, axis=1, keepdims=True) - CE_WEIGHT * picked
    high = terms.astype(BF16).astype(F32)
    middle = (terms - high).astype(BF16).astype(F32)
    low = terms - high - middle
    at = lax.broadcasted_iota(jnp.int32, (LOSS_ROWS, cols), 0)
    tail = jnp.where(at == 0, high, jnp.where(at == 1, middle, jnp.where(at == 2, low, 0.0)))
    g_ref[rows:, :] = tail.astype(BF16)
    norm_s, norm_t, ids, scale = columns_of(norm_s, norm_t, in_row(ids_ref), in_row(scale_ref))
    columns = pos_ref[1] + lax.broadcasted_iota(jnp.int32, (rows, cols), 1)
    hot = jnp.where(columns.astype(F32) == ids, CE_WEIGHT, 0.0)
    prob_s = jnp.exp(l_ref[...] - norm_s)
    prob_t = jnp.exp(t_ref[...].astype(F32) - norm_t)
    g = (scale * ((1.0 + CE_WEIGHT) * prob_s - prob_t - hot)).astype(BF16)
    g_ref[:rows, :] = g
    hidden_product((chunk(2),), pos_ref, w_ref, g, (far_ref,))


def grad_logits(pos, logits, teacher, ids, scale, stats, head5):
    rows, cols = logits.shape
    _, nz, _, sub, _ = head5.shape
    return pl.pallas_call(
        grad_kernel,
        out_shape=(
            jax.ShapeDtypeStruct((rows + LOSS_ROWS, cols), BF16),
            jax.ShapeDtypeStruct((4, nz, sub, rows), F32),
        ),
        in_specs=[pl.BlockSpec(memory_space=pltpu.SMEM)] + [WHOLE] * 6,
        out_specs=(WHOLE, WHOLE),
        compiler_params=params(16),
        cost_estimate=pl.CostEstimate(
            flops=8 * rows * cols,
            bytes_accessed=8 * rows * cols,
            transcendentals=2 * rows * cols,
        ),
        name="grad_logits",
    )(pos, logits, teacher, ids, scale, stats, head5)


def head_kernel(pos_ref, own_ref, oth_ref, g_own_ref, g_oth_ref, out_ref, loss_ref, buf, sem):
    steps, block, _ = buf.shape
    rows = own_ref.shape[0]
    g = jnp.concatenate([g_own_ref[:rows, :], g_oth_ref[:rows, :]], axis=0)
    copies = []
    for i in range(steps):
        at = pl.ds(pl.multiple_of(pos_ref[0] * (steps * block) + i * block, block), block)
        h = jnp.concatenate([own_ref[:, at], oth_ref[:, at]], axis=0)
        total = lax.dot_general(h, g, (((0,), (0,)), ((), ())), preferred_element_type=F32)
        buf[i] = total.astype(BF16)
        copy = pltpu.make_async_copy(buf.at[i], out_ref.at[pl.ds(i * block, block)], sem.at[i])
        copy.start()
        copies.append(copy)

    def loss(ref):
        parts = ref[rows:, :128].astype(F32)
        return (parts[0:1] + parts[1:2]) + parts[2:3]

    loss_ref[...] = (loss(g_own_ref) + loss(g_oth_ref)) * (1.0 / (2 * rows))
    for copy in copies:
        copy.wait()


def head_grad(pos, hidden, hidden_oth, g, g_oth, steps=2):
    rows, depth = hidden.shape
    cols = g.shape[1]
    width = depth // 2
    return pl.pallas_call(
        head_kernel,
        out_shape=(
            jax.ShapeDtypeStruct((width, cols), BF16),
            jax.ShapeDtypeStruct((1, 128), F32),
        ),
        in_specs=[pl.BlockSpec(memory_space=pltpu.SMEM)] + [WHOLE] * 4,
        out_specs=(pl.BlockSpec(memory_space=pl.ANY), WHOLE),
        scratch_shapes=[
            pltpu.VMEM((steps, width // steps, cols), BF16),
            pltpu.SemaphoreType.DMA((steps,)),
        ],
        compiler_params=params(20),
        cost_estimate=LIGHT,
        name="head_grad",
    )(pos, hidden, hidden_oth, g, g_oth)


def body(teacher, hidden, head, ids, assignment, row_scale):
    c, x, y = (lax.axis_index(a) for a in ("c", "x", "y"))
    rows, depth = hidden.shape
    cols = head.shape[1]
    chips = ("y", "z", "x")
    ny, nz, nx = (lax.axis_size(a) for a in chips)
    pos = jnp.stack([c, lax.axis_index(chips) * cols, y, x]).astype(jnp.int32)
    assign = assignment.reshape(-1, 128)
    ids = ids.reshape(-1, 128)
    scale = row_scale.reshape(-1, 128)

    teacher_oth = shift(teacher, "c", 1)
    logits = student_logits(hidden, head)
    stats, teacher_rows = local_stats(pos, logits, teacher, teacher_oth, assign, ids)
    stats, scale, hidden_far = lax.optimization_barrier((stats, scale, hidden))
    hidden_oth = shift(hidden_far, "c", 1)

    def gathered(value, axes, n):
        value = jnp.broadcast_to(value[None], (n,) + value.shape)
        return lax.all_to_all(value, axes, 0, 0, tiled=True)

    stats = gathered(merge_stats(gathered(stats, ("y", "x"), ny * nx)), "z", nz)
    head5 = head.reshape(ny, nz, nx, depth // (ny * nz * nx), cols)
    g, far2 = grad_logits(pos, logits, teacher_rows, ids, scale, stats, head5)

    def coded(value):
        return (value * SEND_SCALE).astype(F16)

    def taken(value):
        return value.astype(F32) * (1.0 / SEND_SCALE)

    far2, g = lax.optimization_barrier((coded(far2), g))
    got2 = shift_by_core(far2, 2, True)
    far1, far3 = hidden_part(pos, head5, g, (chunk(1), chunk(3)))
    far1, far3, g = lax.optimization_barrier((coded(far1), coded(far3), g))
    got = [got2, shift_by_core(far1, 1, True), shift_by_core(far3, 3, True)]
    g_oth = shift(g, "c", 1)
    (own,) = hidden_part(pos, head5, g, (chunk(0),))
    head_out, loss = head_grad(pos, hidden, hidden_oth, g, g_oth)
    loss = loss[0, :1]
    *got, loss, head_out = lax.optimization_barrier((*got, loss, head_out))

    def summed(near):
        return own[near] + sum(taken(v[near]) for v in got)

    far = [shift_by_core(coded(summed(d)), d, False) for d in (2, 1, 3)]
    both = coded(summed(0) + sum(taken(v) for v in far))
    both = lax.all_to_all(both, "z", 0, 0, tiled=True)
    hidden_grad = jnp.sum(taken(both), axis=0).T.astype(BF16)
    return loss, hidden_grad, head_out


def solution(mesh):
    ny, nzx, nc = mesh.devices.shape
    nx = 4
    fine = Mesh(mesh.devices.reshape(ny, nzx // nx, nx, nc), ("y", "z", "x", "c"))
    vocab = ("y", "z", "x")
    in_specs = (
        P(None, vocab + ("c",)),
        P("c", None),
        P(None, vocab),
        P("c"),
        P(),
        P("c"),
    )
    out_specs = (P(), P("c", vocab), P("c", vocab))
    return jax.shard_map(body, mesh=fine, in_specs=in_specs, out_specs=out_specs, check_vma=False)
```

```python
import functools

import jax
import jax.numpy as jnp
import numpy as np
from jax import lax
from jax.experimental import pallas as pl
from jax.experimental.pallas import tpu as pltpu
from jax.sharding import Mesh, PartitionSpec as P

CE_WEIGHT = 0.5
SEND_SCALE = 64.0
SPARE = 256
LOSS_ROWS = 16
F32 = jnp.float32
BF16 = jnp.bfloat16
F16 = jnp.float16


LIGHT = pl.CostEstimate(flops=1, bytes_accessed=1, transcendentals=0)
WHOLE = pl.BlockSpec(memory_space=pltpu.VMEM)


def params(mib, *semantics):
    return pltpu.CompilerParams(
        vmem_limit_bytes=mib * 1024 * 1024, dimension_semantics=semantics or None
    )


def shift(a, axis, by):
    n = lax.axis_size(axis)
    return lax.ppermute(a, axis, [(i, (i + by) % n) for i in range(n)])


def shift_by_core(a, by, first):
    axes = ("y", "z", "x", "c")
    shape = tuple(lax.axis_size(axis) for axis in axes)
    pairs = []
    for source in np.ndindex(shape):
        target = list(source)
        axis = 2 if (source[3] == 0) == first else 0
        target[axis] = (target[axis] + by) % shape[axis]
        pairs.append(tuple(int(np.ravel_multi_index(at, shape)) for at in (source, target)))
    return lax.ppermute(a, axes, pairs)


def logits_kernel(steps, h_ref, w_ref, out_ref, h_buf, w_buf, h_sem, w_sem):
    kb = w_buf.shape[1]

    def copies(k):
        at = pl.ds(k * kb, kb)
        return (
            pltpu.make_async_copy(h_ref.at[:, at], h_buf.at[k], h_sem.at[k]),
            pltpu.make_async_copy(w_ref.at[at], w_buf.at[k], w_sem.at[k]),
        )

    for k in range(steps):
        for copy in copies(k):
            copy.start()
    out_ref[...] = jnp.zeros_like(out_ref)

    def step(k, carry):
        for copy in copies(k):
            copy.wait()
        out_ref[...] += jnp.dot(h_buf[k], w_buf[k], preferred_element_type=F32)
        return carry

    lax.fori_loop(0, steps, step, 0)


def student_logits(hidden, head, steps=4):
    rows, depth = hidden.shape
    cols = head.shape[1]
    kb = depth // steps
    return pl.pallas_call(
        functools.partial(logits_kernel, steps),
        out_shape=jax.ShapeDtypeStruct((rows, cols), F32),
        in_specs=[pl.BlockSpec(memory_space=pl.ANY)] * 2,
        out_specs=WHOLE,
        scratch_shapes=[
            pltpu.VMEM((steps, rows, kb), BF16),
            pltpu.VMEM((steps, kb, cols), BF16),
            pltpu.SemaphoreType.DMA((steps,)),
            pltpu.SemaphoreType.DMA((steps,)),
        ],
        compiler_params=params(52),
        cost_estimate=pl.CostEstimate(
            flops=2 * rows * depth * cols,
            bytes_accessed=2 * (rows * depth + depth * cols) + 4 * rows * cols,
            transcendentals=0,
        ),
        name="student_logits",
    )(hidden, head)


def columns_of(*rows):
    n = rows[0].shape[1]
    sub = lax.broadcasted_iota(jnp.int32, (128, n), 0)
    packed = jnp.zeros((128, n), F32)
    for at, row in enumerate(rows):
        packed = jnp.where(sub == at, row.astype(F32), packed)
    turned = packed.T
    return [turned[:, at : at + 1] for at in range(len(rows))]


def in_row(ref):
    return jnp.concatenate([ref[i : i + 1, :] for i in range(ref.shape[0])], axis=1)


def pack_stats(out_ref, lse_s, lse_t, cross, picked):
    rows = lse_s.shape[1]
    spare = out_ref.shape[1] - rows
    far = 2 * rows - spare
    out_ref[0:1, :rows] = lse_s
    out_ref[1:2, :rows] = lse_t
    out_ref[0:1, rows:] = cross[:, :spare]
    out_ref[1:2, rows:far] = cross[:, spare:]
    lane = lax.broadcasted_iota(jnp.int32, (1, out_ref.shape[1] - far), 1)
    out_ref[1:2, far:] = jnp.where(lane == 0, picked, 0.0)


def logsumexp(values):
    top = jnp.max(values, axis=0, keepdims=True)
    return top + jnp.log(jnp.sum(jnp.exp(values - top), axis=0, keepdims=True))


def merge(first, second):
    rows = first.shape[1] - SPARE
    far = 2 * rows - SPARE
    lse_s = logsumexp(first[:, :rows])
    lse_t = logsumexp(second[:, :rows])
    share_t = jnp.exp(second[:, :rows] - lse_t)
    cross = jnp.concatenate([first[:, rows:], second[:, rows:far]], axis=1)
    cross = jnp.sum(cross * share_t, axis=0, keepdims=True)
    picked = jnp.sum(second[:, far:], axis=0, keepdims=True)
    return lse_s, lse_t, cross, jnp.sum(picked, axis=1, keepdims=True)


def merge_kernel(in_ref, out_ref):
    pack_stats(out_ref, *merge(in_ref[:, 0, :], in_ref[:, 1, :]))


def merge_stats(stats):
    return pl.pallas_call(
        merge_kernel,
        out_shape=jax.ShapeDtypeStruct(stats.shape[1:], F32),
        in_specs=[WHOLE],
        out_specs=WHOLE,
        compiler_params=params(16),
        name="merge_stats",
    )(stats)


def stats_kernel(pos_ref, l_ref, own_ref, oth_ref, assign_ref, ids_ref, stats_ref, t_ref):
    rows, cols = l_ref.shape
    total = own_ref.shape[0]
    first = pos_ref[0] == 0
    assign = in_row(assign_ref)
    assign = jnp.where(first, assign[:, :rows], assign[:, rows:])
    assign, ids = columns_of(assign, in_row(ids_ref))
    lanes = lax.broadcasted_iota(jnp.int32, (rows, total), 1).astype(F32)
    pick = (lanes == assign).astype(BF16)
    own = jnp.dot(pick, own_ref[...], preferred_element_type=F32)
    oth = jnp.dot(pick, oth_ref[...], preferred_element_type=F32)
    teacher = jnp.concatenate([jnp.where(first, own, oth), jnp.where(first, oth, own)], axis=1)
    t_ref[...] = teacher.astype(BF16)
    logits = l_ref[...]
    top_s = jnp.max(logits, axis=1, keepdims=True)
    sum_s = jnp.sum(jnp.exp(logits - top_s), axis=1, keepdims=True)
    top_t = jnp.max(teacher, axis=1, keepdims=True)
    exp_t = jnp.exp(teacher - top_t)
    sum_t = jnp.sum(exp_t, axis=1, keepdims=True)
    cross = jnp.sum(exp_t * (teacher - logits), axis=1, keepdims=True)
    columns = pos_ref[1] + lax.broadcasted_iota(jnp.int32, (rows, cols), 1)
    hot = columns.astype(F32) == ids
    picked = jnp.sum(jnp.where(hot, logits, 0.0), axis=1, keepdims=True)
    lane = lax.broadcasted_iota(jnp.int32, (rows, 128), 1)
    packed = jnp.zeros((rows, 128), F32)
    for at, value in enumerate((top_s, sum_s, top_t, sum_t, cross, picked)):
        packed = jnp.where(lane == at, value, packed)
    packed = packed.T
    top_s, sum_s, top_t, sum_t, cross, picked = (packed[at : at + 1] for at in range(6))
    cross = cross / sum_t
    picked = jnp.sum(picked, axis=1, keepdims=True)
    pack_stats(stats_ref, top_s + jnp.log(sum_s), top_t + jnp.log(sum_t), cross, picked)


def local_stats(pos, logits, own, oth, assign, ids):
    rows, cols = logits.shape
    return pl.pallas_call(
        stats_kernel,
        out_shape=(
            jax.ShapeDtypeStruct((2, rows + SPARE), F32),
            jax.ShapeDtypeStruct((rows, cols), BF16),
        ),
        in_specs=[pl.BlockSpec(memory_space=pltpu.SMEM)] + [WHOLE] * 5,
        out_specs=(WHOLE, WHOLE),
        compiler_params=params(16),
        cost_estimate=pl.CostEstimate(
            flops=2 * rows * cols * own.shape[0],
            bytes_accessed=4 * rows * cols + 4 * own.size + 2 * rows * cols,
            transcendentals=2 * rows * cols,
        ),
        name="local_stats",
    )(pos, logits, own, oth, assign, ids)


def chunk(far):
    return tuple((far, near) for near in range(4))


def hidden_product(groups, pos_ref, w_ref, g, outs):
    ny, nz, nx, sub, cols = w_ref.shape
    x_first, y, x = pos_ref[0] == 0, pos_ref[2], pos_ref[3]

    def block(far, near):
        dx = jnp.where(x_first, far, near)
        dy = jnp.where(x_first, near, far)
        w = w_ref[lax.rem(y + dy, ny), :, lax.rem(x + dx, nx)]
        return w.reshape(nz * sub, cols)

    for names, out in zip(groups, outs):
        w = jnp.concatenate([block(*name) for name in names], axis=0)
        product = lax.dot_general(w, g, (((1,), (1,)), ((), ())), preferred_element_type=F32)
        out[...] = product.reshape(out.shape)


def hidden_kernel(groups, pos_ref, w_ref, g_ref, *outs):
    hidden_product(groups, pos_ref, w_ref, g_ref[: outs[0].shape[-1], :], outs)


def hidden_part(pos, head5, g, groups):
    nz, sub = head5.shape[1], head5.shape[3]
    rows = g.shape[0] - LOSS_ROWS
    out_shape = [jax.ShapeDtypeStruct((len(names), nz, sub, rows), F32) for names in groups]
    return pl.pallas_call(
        functools.partial(hidden_kernel, groups),
        out_shape=out_shape,
        in_specs=[pl.BlockSpec(memory_space=pltpu.SMEM), WHOLE, WHOLE],
        out_specs=[WHOLE] * len(out_shape),
        compiler_params=params(16),
        cost_estimate=LIGHT,
        name="hidden_part",
    )(pos, head5, g)


def grad_kernel(pos_ref, l_ref, t_ref, ids_ref, scale_ref, stats_ref, w_ref, g_ref, far_ref):
    rows, cols = l_ref.shape
    norm_s, norm_t, cross, picked = merge(stats_ref[:, 0, :], stats_ref[:, 1, :])
    terms = cross - norm_t + (1.0 + CE_WEIGHT) * norm_s
    terms = jnp.sum(terms, axis=1, keepdims=True) - CE_WEIGHT * picked
    high = terms.astype(BF16).astype(F32)
    middle = (terms - high).astype(BF16).astype(F32)
    low = terms - high - middle
    at = lax.broadcasted_iota(jnp.int32, (LOSS_ROWS, cols), 0)
    tail = jnp.where(at == 0, high, jnp.where(at == 1, middle, jnp.where(at == 2, low, 0.0)))
    g_ref[rows:, :] = tail.astype(BF16)
    norm_s, norm_t, ids, scale = columns_of(norm_s, norm_t, in_row(ids_ref), in_row(scale_ref))
    columns = pos_ref[1] + lax.broadcasted_iota(jnp.int32, (rows, cols), 1)
    hot = jnp.where(columns.astype(F32) == ids, CE_WEIGHT, 0.0)
    prob_s = jnp.exp(l_ref[...] - norm_s)
    prob_t = jnp.exp(t_ref[...].astype(F32) - norm_t)
    g = (scale * ((1.0 + CE_WEIGHT) * prob_s - prob_t - hot)).astype(BF16)
    g_ref[:rows, :] = g
    hidden_product((chunk(2),), pos_ref, w_ref, g, (far_ref,))


def grad_logits(pos, logits, teacher, ids, scale, stats, head5):
    rows, cols = logits.shape
    _, nz, _, sub, _ = head5.shape
    return pl.pallas_call(
        grad_kernel,
        out_shape=(
            jax.ShapeDtypeStruct((rows + LOSS_ROWS, cols), BF16),
            jax.ShapeDtypeStruct((4, nz, sub, rows), F32),
        ),
        in_specs=[pl.BlockSpec(memory_space=pltpu.SMEM)] + [WHOLE] * 6,
        out_specs=(WHOLE, WHOLE),
        compiler_params=params(16),
        cost_estimate=pl.CostEstimate(
            flops=8 * rows * cols,
            bytes_accessed=8 * rows * cols,
            transcendentals=2 * rows * cols,
        ),
        name="grad_logits",
    )(pos, logits, teacher, ids, scale, stats, head5)


def head_kernel(pos_ref, own_ref, oth_ref, g_own_ref, g_oth_ref, out_ref, loss_ref, buf, sem):
    steps, block, _ = buf.shape
    rows = own_ref.shape[0]
    g = jnp.concatenate([g_own_ref[:rows, :], g_oth_ref[:rows, :]], axis=0)
    copies = []
    for i in range(steps):
        at = pl.ds(pl.multiple_of(pos_ref[0] * (steps * block) + i * block, block), block)
        h = jnp.concatenate([own_ref[:, at], oth_ref[:, at]], axis=0)
        total = lax.dot_general(h, g, (((0,), (0,)), ((), ())), preferred_element_type=F32)
        buf[i] = total.astype(BF16)
        copy = pltpu.make_async_copy(buf.at[i], out_ref.at[pl.ds(i * block, block)], sem.at[i])
        copy.start()
        copies.append(copy)

    def loss(ref):
        parts = ref[rows:, :128].astype(F32)
        return (parts[0:1] + parts[1:2]) + parts[2:3]

    loss_ref[...] = (loss(g_own_ref) + loss(g_oth_ref)) * (1.0 / (2 * rows))
    for copy in copies:
        copy.wait()


def head_grad(pos, hidden, hidden_oth, g, g_oth, steps=2):
    rows, depth = hidden.shape
    cols = g.shape[1]
    width = depth // 2
    return pl.pallas_call(
        head_kernel,
        out_shape=(
            jax.ShapeDtypeStruct((width, cols), BF16),
            jax.ShapeDtypeStruct((1, 128), F32),
        ),
        in_specs=[pl.BlockSpec(memory_space=pltpu.SMEM)] + [WHOLE] * 4,
        out_specs=(pl.BlockSpec(memory_space=pl.ANY), WHOLE),
        scratch_shapes=[
            pltpu.VMEM((steps, width // steps, cols), BF16),
            pltpu.SemaphoreType.DMA((steps,)),
        ],
        compiler_params=params(20),
        cost_estimate=LIGHT,
        name="head_grad",
    )(pos, hidden, hidden_oth, g, g_oth)


def body(teacher, hidden, head, ids, assignment, row_scale):
    c, x, y = (lax.axis_index(a) for a in ("c", "x", "y"))
    rows, depth = hidden.shape
    cols = head.shape[1]
    chips = ("y", "z", "x")
    ny, nz, nx = (lax.axis_size(a) for a in chips)
    pos = jnp.stack([c, lax.axis_index(chips) * cols, y, x]).astype(jnp.int32)
    assign = assignment.reshape(-1, 128)
    ids = ids.reshape(-1, 128)
    scale = row_scale.reshape(-1, 128)

    teacher_oth = shift(teacher, "c", 1)
    logits = student_logits(hidden, head)
    stats, teacher_rows = local_stats(pos, logits, teacher, teacher_oth, assign, ids)
    stats, scale = lax.optimization_barrier((stats, scale))

    def gathered(value, axes, n):
        value = jnp.broadcast_to(value[None], (n,) + value.shape)
        return lax.all_to_all(value, axes, 0, 0, tiled=True)

    stats = merge_stats(gathered(stats, ("y", "x"), ny * nx))
    stats, hidden_far = lax.optimization_barrier((stats, hidden))
    hidden_oth = shift(hidden_far, "c", 1)
    stats = gathered(stats, "z", nz)
    head5 = head.reshape(ny, nz, nx, depth // (ny * nz * nx), cols)
    g, far2 = grad_logits(pos, logits, teacher_rows, ids, scale, stats, head5)

    def coded(value):
        return (value * SEND_SCALE).astype(F16)

    def taken(value):
        return value.astype(F32) * (1.0 / SEND_SCALE)

    far2, g = lax.optimization_barrier((coded(far2), g))
    got2 = shift_by_core(far2, 2, True)
    far1, far3 = hidden_part(pos, head5, g, (chunk(1), chunk(3)))
    far1, far3, g = lax.optimization_barrier((coded(far1), coded(far3), g))
    got = [got2, shift_by_core(far1, 1, True), shift_by_core(far3, 3, True)]
    g_oth = shift(g, "c", 1)
    (own,) = hidden_part(pos, head5, g, (chunk(0),))
    head_out, loss = head_grad(pos, hidden, hidden_oth, g, g_oth)
    loss = loss[0, :1]
    *got, loss, head_out = lax.optimization_barrier((*got, loss, head_out))

    def summed(near):
        return own[near] + sum(taken(v[near]) for v in got)

    far2 = coded(summed(2))
    far2, own, *got = lax.optimization_barrier((far2, own, *got))
    far = [shift_by_core(coded(summed(d)), d, False) for d in (3, 1)]
    far += [shift_by_core(far2, 2, False)]
    both = coded(summed(0) + sum(taken(v) for v in far))
    both = lax.all_to_all(both, "z", 0, 0, tiled=True)
    hidden_grad = jnp.sum(taken(both), axis=0).T.astype(BF16)
    return loss, hidden_grad, head_out


def solution(mesh):
    ny, nzx, nc = mesh.devices.shape
    nx = 4
    fine = Mesh(mesh.devices.reshape(ny, nzx // nx, nx, nc), ("y", "z", "x", "c"))
    vocab = ("y", "z", "x")
    in_specs = (
        P(None, vocab + ("c",)),
        P("c", None),
        P(None, vocab),
        P("c"),
        P(),
        P("c"),
    )
    out_specs = (P(), P("c", vocab), P("c", vocab))
    return jax.shard_map(body, mesh=fine, in_specs=in_specs, out_specs=out_specs, check_vma=False)
```

```python
import functools

import jax
import jax.numpy as jnp
import numpy as np
from jax import lax
from jax.experimental import pallas as pl
from jax.experimental.pallas import tpu as pltpu
from jax.sharding import Mesh, PartitionSpec as P

CE_WEIGHT = 0.5
SEND_SCALE = 64.0
SPARE = 256
LOSS_ROWS = 16
F32 = jnp.float32
BF16 = jnp.bfloat16
F16 = jnp.float16


LIGHT = pl.CostEstimate(flops=1, bytes_accessed=1, transcendentals=0)
WHOLE = pl.BlockSpec(memory_space=pltpu.VMEM)


def params(mib, *semantics):
    return pltpu.CompilerParams(
        vmem_limit_bytes=mib * 1024 * 1024, dimension_semantics=semantics or None
    )


def shift(a, axis, by):
    n = lax.axis_size(axis)
    return lax.ppermute(a, axis, [(i, (i + by) % n) for i in range(n)])


def shift_by_core(a, by, first):
    axes = ("y", "z", "x", "c")
    shape = tuple(lax.axis_size(axis) for axis in axes)
    pairs = []
    for source in np.ndindex(shape):
        target = list(source)
        axis = 2 if (source[3] == 0) == first else 0
        target[axis] = (target[axis] + by) % shape[axis]
        pairs.append(tuple(int(np.ravel_multi_index(at, shape)) for at in (source, target)))
    return lax.ppermute(a, axes, pairs)


def logits_kernel(steps, h_ref, w_ref, out_ref, h_buf, w_buf, h_sem, w_sem):
    kb = w_buf.shape[1]

    def copies(k):
        at = pl.ds(k * kb, kb)
        return (
            pltpu.make_async_copy(h_ref.at[:, at], h_buf.at[k], h_sem.at[k]),
            pltpu.make_async_copy(w_ref.at[at], w_buf.at[k], w_sem.at[k]),
        )

    for k in range(steps):
        for copy in copies(k):
            copy.start()
    out_ref[...] = jnp.zeros_like(out_ref)

    def step(k, carry):
        for copy in copies(k):
            copy.wait()
        out_ref[...] += jnp.dot(h_buf[k], w_buf[k], preferred_element_type=F32)
        return carry

    lax.fori_loop(0, steps, step, 0)


def student_logits(hidden, head, steps=4):
    rows, depth = hidden.shape
    cols = head.shape[1]
    kb = depth // steps
    return pl.pallas_call(
        functools.partial(logits_kernel, steps),
        out_shape=jax.ShapeDtypeStruct((rows, cols), F32),
        in_specs=[pl.BlockSpec(memory_space=pl.ANY)] * 2,
        out_specs=WHOLE,
        scratch_shapes=[
            pltpu.VMEM((steps, rows, kb), BF16),
            pltpu.VMEM((steps, kb, cols), BF16),
            pltpu.SemaphoreType.DMA((steps,)),
            pltpu.SemaphoreType.DMA((steps,)),
        ],
        compiler_params=params(52),
        cost_estimate=pl.CostEstimate(
            flops=2 * rows * depth * cols,
            bytes_accessed=2 * (rows * depth + depth * cols) + 4 * rows * cols,
            transcendentals=0,
        ),
        name="student_logits",
    )(hidden, head)


def columns_of(*rows):
    n = rows[0].shape[1]
    sub = lax.broadcasted_iota(jnp.int32, (128, n), 0)
    packed = jnp.zeros((128, n), F32)
    for at, row in enumerate(rows):
        packed = jnp.where(sub == at, row.astype(F32), packed)
    turned = packed.T
    return [turned[:, at : at + 1] for at in range(len(rows))]


def in_row(ref):
    return jnp.concatenate([ref[i : i + 1, :] for i in range(ref.shape[0])], axis=1)


def pack_stats(out_ref, lse_s, lse_t, cross, picked):
    rows = lse_s.shape[1]
    spare = out_ref.shape[1] - rows
    far = 2 * rows - spare
    out_ref[0:1, :rows] = lse_s
    out_ref[1:2, :rows] = lse_t
    out_ref[0:1, rows:] = cross[:, :spare]
    out_ref[1:2, rows:far] = cross[:, spare:]
    lane = lax.broadcasted_iota(jnp.int32, (1, out_ref.shape[1] - far), 1)
    out_ref[1:2, far:] = jnp.where(lane == 0, picked, 0.0)


def logsumexp(values):
    top = jnp.max(values, axis=0, keepdims=True)
    return top + jnp.log(jnp.sum(jnp.exp(values - top), axis=0, keepdims=True))


def merge(first, second):
    rows = first.shape[1] - SPARE
    far = 2 * rows - SPARE
    lse_s = logsumexp(first[:, :rows])
    lse_t = logsumexp(second[:, :rows])
    share_t = jnp.exp(second[:, :rows] - lse_t)
    cross = jnp.concatenate([first[:, rows:], second[:, rows:far]], axis=1)
    cross = jnp.sum(cross * share_t, axis=0, keepdims=True)
    picked = jnp.sum(second[:, far:], axis=0, keepdims=True)
    return lse_s, lse_t, cross, jnp.sum(picked, axis=1, keepdims=True)


def merge_kernel(in_ref, out_ref):
    pack_stats(out_ref, *merge(in_ref[:, 0, :], in_ref[:, 1, :]))


def merge_stats(stats):
    return pl.pallas_call(
        merge_kernel,
        out_shape=jax.ShapeDtypeStruct(stats.shape[1:], F32),
        in_specs=[WHOLE],
        out_specs=WHOLE,
        compiler_params=params(16),
        name="merge_stats",
    )(stats)


def stats_kernel(pos_ref, l_ref, own_ref, oth_ref, assign_ref, ids_ref, stats_ref, t_ref):
    rows, cols = l_ref.shape
    total = own_ref.shape[0]
    first = pos_ref[0] == 0
    assign = in_row(assign_ref)
    assign = jnp.where(first, assign[:, :rows], assign[:, rows:])
    assign, ids = columns_of(assign, in_row(ids_ref))
    lanes = lax.broadcasted_iota(jnp.int32, (rows, total), 1).astype(F32)
    pick = (lanes == assign).astype(BF16)
    own = jnp.dot(pick, own_ref[...], preferred_element_type=F32)
    oth = jnp.dot(pick, oth_ref[...], preferred_element_type=F32)
    teacher = jnp.concatenate([jnp.where(first, own, oth), jnp.where(first, oth, own)], axis=1)
    t_ref[...] = teacher.astype(BF16)
    logits = l_ref[...]
    top_s = jnp.max(logits, axis=1, keepdims=True)
    sum_s = jnp.sum(jnp.exp(logits - top_s), axis=1, keepdims=True)
    top_t = jnp.max(teacher, axis=1, keepdims=True)
    exp_t = jnp.exp(teacher - top_t)
    sum_t = jnp.sum(exp_t, axis=1, keepdims=True)
    cross = jnp.sum(exp_t * (teacher - logits), axis=1, keepdims=True)
    columns = pos_ref[1] + lax.broadcasted_iota(jnp.int32, (rows, cols), 1)
    hot = columns.astype(F32) == ids
    picked = jnp.sum(jnp.where(hot, logits, 0.0), axis=1, keepdims=True)
    lane = lax.broadcasted_iota(jnp.int32, (rows, 128), 1)
    packed = jnp.zeros((rows, 128), F32)
    for at, value in enumerate((top_s, sum_s, top_t, sum_t, cross, picked)):
        packed = jnp.where(lane == at, value, packed)
    packed = packed.T
    top_s, sum_s, top_t, sum_t, cross, picked = (packed[at : at + 1] for at in range(6))
    cross = cross / sum_t
    picked = jnp.sum(picked, axis=1, keepdims=True)
    pack_stats(stats_ref, top_s + jnp.log(sum_s), top_t + jnp.log(sum_t), cross, picked)


def local_stats(pos, logits, own, oth, assign, ids):
    rows, cols = logits.shape
    return pl.pallas_call(
        stats_kernel,
        out_shape=(
            jax.ShapeDtypeStruct((2, rows + SPARE), F32),
            jax.ShapeDtypeStruct((rows, cols), BF16),
        ),
        in_specs=[pl.BlockSpec(memory_space=pltpu.SMEM)] + [WHOLE] * 5,
        out_specs=(WHOLE, WHOLE),
        compiler_params=params(16),
        cost_estimate=pl.CostEstimate(
            flops=2 * rows * cols * own.shape[0],
            bytes_accessed=4 * rows * cols + 4 * own.size + 2 * rows * cols,
            transcendentals=2 * rows * cols,
        ),
        name="local_stats",
    )(pos, logits, own, oth, assign, ids)


def chunk(far):
    return tuple((far, near) for near in range(4))


def hidden_product(groups, pos_ref, w_ref, g, outs):
    ny, nz, nx, sub, cols = w_ref.shape
    x_first, y, x = pos_ref[0] == 0, pos_ref[2], pos_ref[3]

    def block(far, near):
        dx = jnp.where(x_first, far, near)
        dy = jnp.where(x_first, near, far)
        w = w_ref[lax.rem(y + dy, ny), :, lax.rem(x + dx, nx)]
        return w.reshape(nz * sub, cols)

    for names, out in zip(groups, outs):
        w = jnp.concatenate([block(*name) for name in names], axis=0)
        product = lax.dot_general(w, g, (((1,), (1,)), ((), ())), preferred_element_type=F32)
        out[...] = product.reshape(out.shape)


def hidden_kernel(groups, pos_ref, w_ref, g_ref, *outs):
    hidden_product(groups, pos_ref, w_ref, g_ref[: outs[0].shape[-1], :], outs)


def hidden_part(pos, head5, g, groups):
    nz, sub = head5.shape[1], head5.shape[3]
    rows = g.shape[0] - LOSS_ROWS
    out_shape = [jax.ShapeDtypeStruct((len(names), nz, sub, rows), F32) for names in groups]
    return pl.pallas_call(
        functools.partial(hidden_kernel, groups),
        out_shape=out_shape,
        in_specs=[pl.BlockSpec(memory_space=pltpu.SMEM), WHOLE, WHOLE],
        out_specs=[WHOLE] * len(out_shape),
        compiler_params=params(16),
        cost_estimate=LIGHT,
        name="hidden_part",
    )(pos, head5, g)


def grad_kernel(pos_ref, l_ref, t_ref, ids_ref, scale_ref, stats_ref, w_ref, g_ref, far_ref):
    rows, cols = l_ref.shape
    norm_s, norm_t, cross, picked = merge(stats_ref[:, 0, :], stats_ref[:, 1, :])
    terms = cross - norm_t + (1.0 + CE_WEIGHT) * norm_s
    terms = jnp.sum(terms, axis=1, keepdims=True) - CE_WEIGHT * picked
    high = terms.astype(BF16).astype(F32)
    middle = (terms - high).astype(BF16).astype(F32)
    low = terms - high - middle
    at = lax.broadcasted_iota(jnp.int32, (LOSS_ROWS, cols), 0)
    tail = jnp.where(at == 0, high, jnp.where(at == 1, middle, jnp.where(at == 2, low, 0.0)))
    g_ref[rows:, :] = tail.astype(BF16)
    norm_s, norm_t, ids, scale = columns_of(norm_s, norm_t, in_row(ids_ref), in_row(scale_ref))
    columns = pos_ref[1] + lax.broadcasted_iota(jnp.int32, (rows, cols), 1)
    hot = jnp.where(columns.astype(F32) == ids, CE_WEIGHT, 0.0)
    prob_s = jnp.exp(l_ref[...] - norm_s)
    prob_t = jnp.exp(t_ref[...].astype(F32) - norm_t)
    g = (scale * ((1.0 + CE_WEIGHT) * prob_s - prob_t - hot)).astype(BF16)
    g_ref[:rows, :] = g
    hidden_product((chunk(2),), pos_ref, w_ref, g, (far_ref,))


def grad_logits(pos, logits, teacher, ids, scale, stats, head5):
    rows, cols = logits.shape
    _, nz, _, sub, _ = head5.shape
    return pl.pallas_call(
        grad_kernel,
        out_shape=(
            jax.ShapeDtypeStruct((rows + LOSS_ROWS, cols), BF16),
            jax.ShapeDtypeStruct((4, nz, sub, rows), F32),
        ),
        in_specs=[pl.BlockSpec(memory_space=pltpu.SMEM)] + [WHOLE] * 6,
        out_specs=(WHOLE, WHOLE),
        compiler_params=params(16),
        cost_estimate=pl.CostEstimate(
            flops=8 * rows * cols,
            bytes_accessed=8 * rows * cols,
            transcendentals=2 * rows * cols,
        ),
        name="grad_logits",
    )(pos, logits, teacher, ids, scale, stats, head5)


def head_kernel(pos_ref, own_ref, oth_ref, g_own_ref, g_oth_ref, out_ref, loss_ref, buf, sem):
    steps, block, _ = buf.shape
    rows = own_ref.shape[0]
    g = jnp.concatenate([g_own_ref[:rows, :], g_oth_ref[:rows, :]], axis=0)
    copies = []
    for i in range(steps):
        at = pl.ds(pl.multiple_of(pos_ref[0] * (steps * block) + i * block, block), block)
        h = jnp.concatenate([own_ref[:, at], oth_ref[:, at]], axis=0)
        total = lax.dot_general(h, g, (((0,), (0,)), ((), ())), preferred_element_type=F32)
        buf[i] = total.astype(BF16)
        copy = pltpu.make_async_copy(buf.at[i], out_ref.at[pl.ds(i * block, block)], sem.at[i])
        copy.start()
        copies.append(copy)

    def loss(ref):
        parts = ref[rows:, :128].astype(F32)
        return (parts[0:1] + parts[1:2]) + parts[2:3]

    loss_ref[...] = (loss(g_own_ref) + loss(g_oth_ref)) * (1.0 / (2 * rows))
    for copy in copies:
        copy.wait()


def head_grad(pos, hidden, hidden_oth, g, g_oth, steps=2):
    rows, depth = hidden.shape
    cols = g.shape[1]
    width = depth // 2
    return pl.pallas_call(
        head_kernel,
        out_shape=(
            jax.ShapeDtypeStruct((width, cols), BF16),
            jax.ShapeDtypeStruct((1, 128), F32),
        ),
        in_specs=[pl.BlockSpec(memory_space=pltpu.SMEM)] + [WHOLE] * 4,
        out_specs=(pl.BlockSpec(memory_space=pl.ANY), WHOLE),
        scratch_shapes=[
            pltpu.VMEM((steps, width // steps, cols), BF16),
            pltpu.SemaphoreType.DMA((steps,)),
        ],
        compiler_params=params(20),
        cost_estimate=LIGHT,
        name="head_grad",
    )(pos, hidden, hidden_oth, g, g_oth)


def body(teacher, hidden, head, ids, assignment, row_scale):
    c, x, y = (lax.axis_index(a) for a in ("c", "x", "y"))
    rows, depth = hidden.shape
    cols = head.shape[1]
    chips = ("y", "z", "x")
    ny, nz, nx = (lax.axis_size(a) for a in chips)
    pos = jnp.stack([c, lax.axis_index(chips) * cols, y, x]).astype(jnp.int32)
    assign = assignment.reshape(-1, 128)
    ids = ids.reshape(-1, 128)
    scale = row_scale.reshape(-1, 128)

    teacher_oth = shift(teacher, "c", 1)
    logits = student_logits(hidden, head)
    stats, teacher_rows = local_stats(pos, logits, teacher, teacher_oth, assign, ids)
    stats, scale = lax.optimization_barrier((stats, scale))

    def gathered(value, axes, n):
        value = jnp.broadcast_to(value[None], (n,) + value.shape)
        return lax.all_to_all(value, axes, 0, 0, tiled=True)

    stats = merge_stats(gathered(stats, ("y", "x"), ny * nx))
    stats, hidden_far = lax.optimization_barrier((stats, hidden))
    hidden_oth = shift(hidden_far, "c", 1)
    stats = gathered(stats, "z", nz)
    head5 = head.reshape(ny, nz, nx, depth // (ny * nz * nx), cols)
    g, far2 = grad_logits(pos, logits, teacher_rows, ids, scale, stats, head5)

    def coded(value):
        return (value * SEND_SCALE).astype(F16)

    def taken(value):
        return value.astype(F32) * (1.0 / SEND_SCALE)

    far2, g = lax.optimization_barrier((coded(far2), g))
    got2 = shift_by_core(far2, 2, True)
    groups = (chunk(1)[1:], chunk(3)[1:], chunk(1)[:1], chunk(3)[:1])
    far1, far3, late1, late3 = (coded(v) for v in hidden_part(pos, head5, g, groups))
    far1, far3, g = lax.optimization_barrier((far1, far3, g))
    got = [shift_by_core(far1, 1, True), shift_by_core(far3, 3, True)]
    g_oth = shift(g, "c", 1)
    (own,) = hidden_part(pos, head5, g, (chunk(0),))
    head_out, loss = head_grad(pos, hidden, hidden_oth, g, g_oth)
    loss = loss[0, :1]
    got2, *got, loss, head_out = lax.optimization_barrier((got2, *got, loss, head_out))

    def summed(near):
        return own[near] + taken(got2[near]) + sum(taken(v[near - 1]) for v in got)

    far2 = coded(summed(2))
    far2, own, got2, *got = lax.optimization_barrier((far2, own, got2, *got))
    far1, far3 = coded(summed(1)), coded(summed(3))
    far1, far3, late1, late3 = lax.optimization_barrier((far1, far3, late1, late3))
    last = [shift_by_core(late1, 1, True)[0], shift_by_core(late3, 3, True)[0]]
    last += [shift_by_core(v, d, False) for v, d in ((far3, 3), (far1, 1), (far2, 2))]
    both = coded(own[0] + taken(got2[0]) + sum(taken(v) for v in last))
    both = lax.all_to_all(both, "z", 0, 0, tiled=True)
    hidden_grad = jnp.sum(taken(both), axis=0).T.astype(BF16)
    return loss, hidden_grad, head_out


def solution(mesh):
    ny, nzx, nc = mesh.devices.shape
    nx = 4
    fine = Mesh(mesh.devices.reshape(ny, nzx // nx, nx, nc), ("y", "z", "x", "c"))
    vocab = ("y", "z", "x")
    in_specs = (
        P(None, vocab + ("c",)),
        P("c", None),
        P(None, vocab),
        P("c"),
        P(),
        P("c"),
    )
    out_specs = (P(), P("c", vocab), P("c", vocab))
    return jax.shard_map(body, mesh=fine, in_specs=in_specs, out_specs=out_specs, check_vma=False)
```

```python
import functools

import jax
import jax.numpy as jnp
import numpy as np
from jax import lax
from jax.experimental import pallas as pl
from jax.experimental.pallas import tpu as pltpu
from jax.sharding import Mesh, PartitionSpec as P

CE_WEIGHT = 0.5
SEND_SCALE = 64.0
SPARE = 256
LOSS_ROWS = 16
F32 = jnp.float32
BF16 = jnp.bfloat16
F16 = jnp.float16


LIGHT = pl.CostEstimate(flops=1, bytes_accessed=1, transcendentals=0)
WHOLE = pl.BlockSpec(memory_space=pltpu.VMEM)


def params(mib, *semantics):
    return pltpu.CompilerParams(
        vmem_limit_bytes=mib * 1024 * 1024, dimension_semantics=semantics or None
    )


def shift(a, axis, by):
    n = lax.axis_size(axis)
    return lax.ppermute(a, axis, [(i, (i + by) % n) for i in range(n)])


def shift_by_core(a, by, first):
    axes = ("y", "z", "x", "c")
    shape = tuple(lax.axis_size(axis) for axis in axes)
    pairs = []
    for source in np.ndindex(shape):
        target = list(source)
        axis = 2 if (source[3] == 0) == first else 0
        target[axis] = (target[axis] + by) % shape[axis]
        pairs.append(tuple(int(np.ravel_multi_index(at, shape)) for at in (source, target)))
    return lax.ppermute(a, axes, pairs)


def logits_kernel(steps, h_ref, w_ref, out_ref, h_buf, w_buf, h_sem, w_sem):
    kb = w_buf.shape[1]

    def copies(k):
        at = pl.ds(k * kb, kb)
        return (
            pltpu.make_async_copy(h_ref.at[:, at], h_buf.at[k], h_sem.at[k]),
            pltpu.make_async_copy(w_ref.at[at], w_buf.at[k], w_sem.at[k]),
        )

    for k in range(steps):
        for copy in copies(k):
            copy.start()
    out_ref[...] = jnp.zeros_like(out_ref)

    def step(k, carry):
        for copy in copies(k):
            copy.wait()
        out_ref[...] += jnp.dot(h_buf[k], w_buf[k], preferred_element_type=F32)
        return carry

    lax.fori_loop(0, steps, step, 0)


def student_logits(hidden, head, steps=4):
    rows, depth = hidden.shape
    cols = head.shape[1]
    kb = depth // steps
    return pl.pallas_call(
        functools.partial(logits_kernel, steps),
        out_shape=jax.ShapeDtypeStruct((rows, cols), F32),
        in_specs=[pl.BlockSpec(memory_space=pl.ANY)] * 2,
        out_specs=WHOLE,
        scratch_shapes=[
            pltpu.VMEM((steps, rows, kb), BF16),
            pltpu.VMEM((steps, kb, cols), BF16),
            pltpu.SemaphoreType.DMA((steps,)),
            pltpu.SemaphoreType.DMA((steps,)),
        ],
        compiler_params=params(52),
        cost_estimate=pl.CostEstimate(
            flops=2 * rows * depth * cols,
            bytes_accessed=2 * (rows * depth + depth * cols) + 4 * rows * cols,
            transcendentals=0,
        ),
        name="student_logits",
    )(hidden, head)


def columns_of(*rows):
    n = rows[0].shape[1]
    sub = lax.broadcasted_iota(jnp.int32, (128, n), 0)
    packed = jnp.zeros((128, n), F32)
    for at, row in enumerate(rows):
        packed = jnp.where(sub == at, row.astype(F32), packed)
    turned = packed.T
    return [turned[:, at : at + 1] for at in range(len(rows))]


def in_row(ref):
    return jnp.concatenate([ref[i : i + 1, :] for i in range(ref.shape[0])], axis=1)


def pack_stats(out_ref, lse_s, lse_t, cross, picked):
    rows = lse_s.shape[1]
    spare = out_ref.shape[1] - rows
    far = 2 * rows - spare
    out_ref[0:1, :rows] = lse_s
    out_ref[1:2, :rows] = lse_t
    out_ref[0:1, rows:] = cross[:, :spare]
    out_ref[1:2, rows:far] = cross[:, spare:]
    lane = lax.broadcasted_iota(jnp.int32, (1, out_ref.shape[1] - far), 1)
    out_ref[1:2, far:] = jnp.where(lane == 0, picked, 0.0)


def logsumexp(values):
    top = jnp.max(values, axis=0, keepdims=True)
    return top + jnp.log(jnp.sum(jnp.exp(values - top), axis=0, keepdims=True))


def merge(first, second):
    rows = first.shape[1] - SPARE
    far = 2 * rows - SPARE
    lse_s = logsumexp(first[:, :rows])
    lse_t = logsumexp(second[:, :rows])
    share_t = jnp.exp(second[:, :rows] - lse_t)
    cross = jnp.concatenate([first[:, rows:], second[:, rows:far]], axis=1)
    cross = jnp.sum(cross * share_t, axis=0, keepdims=True)
    picked = jnp.sum(second[:, far:], axis=0, keepdims=True)
    return lse_s, lse_t, cross, jnp.sum(picked, axis=1, keepdims=True)


def merge_kernel(in_ref, out_ref):
    pack_stats(out_ref, *merge(in_ref[:, 0, :], in_ref[:, 1, :]))


def merge_stats(stats):
    return pl.pallas_call(
        merge_kernel,
        out_shape=jax.ShapeDtypeStruct(stats.shape[1:], F32),
        in_specs=[WHOLE],
        out_specs=WHOLE,
        compiler_params=params(16),
        name="merge_stats",
    )(stats)


def stats_kernel(pos_ref, l_ref, own_ref, oth_ref, assign_ref, ids_ref, stats_ref, t_ref):
    rows, cols = l_ref.shape
    total = own_ref.shape[0]
    first = pos_ref[0] == 0
    assign = in_row(assign_ref)
    assign = jnp.where(first, assign[:, :rows], assign[:, rows:])
    assign, ids = columns_of(assign, in_row(ids_ref))
    lanes = lax.broadcasted_iota(jnp.int32, (rows, total), 1).astype(F32)
    pick = (lanes == assign).astype(BF16)
    own = jnp.dot(pick, own_ref[...], preferred_element_type=F32)
    oth = jnp.dot(pick, oth_ref[...], preferred_element_type=F32)
    teacher = jnp.concatenate([jnp.where(first, own, oth), jnp.where(first, oth, own)], axis=1)
    t_ref[...] = teacher.astype(BF16)
    logits = l_ref[...]
    top_s = jnp.max(logits, axis=1, keepdims=True)
    sum_s = jnp.sum(jnp.exp(logits - top_s), axis=1, keepdims=True)
    top_t = jnp.max(teacher, axis=1, keepdims=True)
    exp_t = jnp.exp(teacher - top_t)
    sum_t = jnp.sum(exp_t, axis=1, keepdims=True)
    cross = jnp.sum(exp_t * (teacher - logits), axis=1, keepdims=True)
    columns = pos_ref[1] + lax.broadcasted_iota(jnp.int32, (rows, cols), 1)
    hot = columns.astype(F32) == ids
    picked = jnp.sum(jnp.where(hot, logits, 0.0), axis=1, keepdims=True)
    lane = lax.broadcasted_iota(jnp.int32, (rows, 128), 1)
    packed = jnp.zeros((rows, 128), F32)
    for at, value in enumerate((top_s, sum_s, top_t, sum_t, cross, picked)):
        packed = jnp.where(lane == at, value, packed)
    packed = packed.T
    top_s, sum_s, top_t, sum_t, cross, picked = (packed[at : at + 1] for at in range(6))
    cross = cross / sum_t
    picked = jnp.sum(picked, axis=1, keepdims=True)
    pack_stats(stats_ref, top_s + jnp.log(sum_s), top_t + jnp.log(sum_t), cross, picked)


def local_stats(pos, logits, own, oth, assign, ids):
    rows, cols = logits.shape
    return pl.pallas_call(
        stats_kernel,
        out_shape=(
            jax.ShapeDtypeStruct((2, rows + SPARE), F32),
            jax.ShapeDtypeStruct((rows, cols), BF16),
        ),
        in_specs=[pl.BlockSpec(memory_space=pltpu.SMEM)] + [WHOLE] * 5,
        out_specs=(WHOLE, WHOLE),
        compiler_params=params(16),
        cost_estimate=pl.CostEstimate(
            flops=2 * rows * cols * own.shape[0],
            bytes_accessed=4 * rows * cols + 4 * own.size + 2 * rows * cols,
            transcendentals=2 * rows * cols,
        ),
        name="local_stats",
    )(pos, logits, own, oth, assign, ids)


def chunk(far):
    return tuple((far, near) for near in range(4))


def hidden_product(groups, pos_ref, w_ref, g, outs):
    ny, nz, nx, sub, cols = w_ref.shape
    x_first, y, x = pos_ref[0] == 0, pos_ref[2], pos_ref[3]

    def block(far, near):
        dx = jnp.where(x_first, far, near)
        dy = jnp.where(x_first, near, far)
        w = w_ref[lax.rem(y + dy, ny), :, lax.rem(x + dx, nx)]
        return w.reshape(nz * sub, cols)

    for names, out in zip(groups, outs):
        w = jnp.concatenate([block(*name) for name in names], axis=0)
        product = lax.dot_general(w, g, (((1,), (1,)), ((), ())), preferred_element_type=F32)
        out[...] = product.reshape(out.shape)


def hidden_kernel(groups, pos_ref, w_ref, g_ref, *outs):
    hidden_product(groups, pos_ref, w_ref, g_ref[: outs[0].shape[-1], :], outs)


def hidden_part(pos, head5, g, groups):
    nz, sub = head5.shape[1], head5.shape[3]
    rows = g.shape[0] - LOSS_ROWS
    out_shape = [jax.ShapeDtypeStruct((len(names), nz, sub, rows), F32) for names in groups]
    return pl.pallas_call(
        functools.partial(hidden_kernel, groups),
        out_shape=out_shape,
        in_specs=[pl.BlockSpec(memory_space=pltpu.SMEM), WHOLE, WHOLE],
        out_specs=[WHOLE] * len(out_shape),
        compiler_params=params(16),
        cost_estimate=LIGHT,
        name="hidden_part",
    )(pos, head5, g)


def grad_kernel(pos_ref, l_ref, t_ref, ids_ref, scale_ref, stats_ref, w_ref, g_ref, far_ref):
    rows, cols = l_ref.shape
    norm_s, norm_t, cross, picked = merge(stats_ref[:, 0, :], stats_ref[:, 1, :])
    terms = cross - norm_t + (1.0 + CE_WEIGHT) * norm_s
    terms = jnp.sum(terms, axis=1, keepdims=True) - CE_WEIGHT * picked
    high = terms.astype(BF16).astype(F32)
    middle = (terms - high).astype(BF16).astype(F32)
    low = terms - high - middle
    at = lax.broadcasted_iota(jnp.int32, (LOSS_ROWS, cols), 0)
    tail = jnp.where(at == 0, high, jnp.where(at == 1, middle, jnp.where(at == 2, low, 0.0)))
    g_ref[rows:, :] = tail.astype(BF16)
    norm_s, norm_t, ids, scale = columns_of(norm_s, norm_t, in_row(ids_ref), in_row(scale_ref))
    columns = pos_ref[1] + lax.broadcasted_iota(jnp.int32, (rows, cols), 1)
    hot = jnp.where(columns.astype(F32) == ids, CE_WEIGHT, 0.0)
    prob_s = jnp.exp(l_ref[...] - norm_s)
    prob_t = jnp.exp(t_ref[...].astype(F32) - norm_t)
    g = (scale * ((1.0 + CE_WEIGHT) * prob_s - prob_t - hot)).astype(BF16)
    g_ref[:rows, :] = g
    hidden_product((chunk(2),), pos_ref, w_ref, g, (far_ref,))


def grad_logits(pos, logits, teacher, ids, scale, stats, head5):
    rows, cols = logits.shape
    _, nz, _, sub, _ = head5.shape
    return pl.pallas_call(
        grad_kernel,
        out_shape=(
            jax.ShapeDtypeStruct((rows + LOSS_ROWS, cols), BF16),
            jax.ShapeDtypeStruct((4, nz, sub, rows), F32),
        ),
        in_specs=[pl.BlockSpec(memory_space=pltpu.SMEM)] + [WHOLE] * 6,
        out_specs=(WHOLE, WHOLE),
        compiler_params=params(16),
        cost_estimate=pl.CostEstimate(
            flops=8 * rows * cols,
            bytes_accessed=8 * rows * cols,
            transcendentals=2 * rows * cols,
        ),
        name="grad_logits",
    )(pos, logits, teacher, ids, scale, stats, head5)


def head_kernel(pos_ref, own_ref, oth_ref, g_own_ref, g_oth_ref, out_ref, loss_ref, buf, sem):
    steps, block, _ = buf.shape
    rows = own_ref.shape[0]
    g = jnp.concatenate([g_own_ref[:rows, :], g_oth_ref[:rows, :]], axis=0)
    copies = []
    for i in range(steps):
        at = pl.ds(pl.multiple_of(pos_ref[0] * (steps * block) + i * block, block), block)
        h = jnp.concatenate([own_ref[:, at], oth_ref[:, at]], axis=0)
        total = lax.dot_general(h, g, (((0,), (0,)), ((), ())), preferred_element_type=F32)
        buf[i] = total.astype(BF16)
        copy = pltpu.make_async_copy(buf.at[i], out_ref.at[pl.ds(i * block, block)], sem.at[i])
        copy.start()
        copies.append(copy)

    def loss(ref):
        parts = ref[rows:, :128].astype(F32)
        return (parts[0:1] + parts[1:2]) + parts[2:3]

    loss_ref[...] = (loss(g_own_ref) + loss(g_oth_ref)) * (1.0 / (2 * rows))
    for copy in copies:
        copy.wait()


def head_grad(pos, hidden, hidden_oth, g, g_oth, steps=2):
    rows, depth = hidden.shape
    cols = g.shape[1]
    width = depth // 2
    return pl.pallas_call(
        head_kernel,
        out_shape=(
            jax.ShapeDtypeStruct((width, cols), BF16),
            jax.ShapeDtypeStruct((1, 128), F32),
        ),
        in_specs=[pl.BlockSpec(memory_space=pltpu.SMEM)] + [WHOLE] * 4,
        out_specs=(pl.BlockSpec(memory_space=pl.ANY), WHOLE),
        scratch_shapes=[
            pltpu.VMEM((steps, width // steps, cols), BF16),
            pltpu.SemaphoreType.DMA((steps,)),
        ],
        compiler_params=params(20),
        cost_estimate=LIGHT,
        name="head_grad",
    )(pos, hidden, hidden_oth, g, g_oth)


def body(teacher, hidden, head, ids, assignment, row_scale):
    c, x, y = (lax.axis_index(a) for a in ("c", "x", "y"))
    rows, depth = hidden.shape
    cols = head.shape[1]
    chips = ("y", "z", "x")
    ny, nz, nx = (lax.axis_size(a) for a in chips)
    pos = jnp.stack([c, lax.axis_index(chips) * cols, y, x]).astype(jnp.int32)
    assign = assignment.reshape(-1, 128)
    ids = ids.reshape(-1, 128)
    scale = row_scale.reshape(-1, 128)

    teacher_oth = shift(teacher, "c", 1)
    logits = student_logits(hidden, head)
    stats, teacher_rows = local_stats(pos, logits, teacher, teacher_oth, assign, ids)
    stats, scale = lax.optimization_barrier((stats, scale))

    def gathered(value, axes, n):
        value = jnp.broadcast_to(value[None], (n,) + value.shape)
        return lax.all_to_all(value, axes, 0, 0, tiled=True)

    stats = merge_stats(gathered(stats, "z", nz))
    stats, hidden_far = lax.optimization_barrier((stats, hidden))
    hidden_oth = shift(hidden_far, "c", 1)
    stats = gathered(stats, ("y", "x"), ny * nx)
    head5 = head.reshape(ny, nz, nx, depth // (ny * nz * nx), cols)
    g, far2 = grad_logits(pos, logits, teacher_rows, ids, scale, stats, head5)

    def coded(value):
        return (value * SEND_SCALE).astype(F16)

    def taken(value):
        return value.astype(F32) * (1.0 / SEND_SCALE)

    far2, g = lax.optimization_barrier((coded(far2), g))
    got2 = shift_by_core(far2, 2, True)
    far1, far3 = hidden_part(pos, head5, g, (chunk(1), chunk(3)))
    far1, far3, g = lax.optimization_barrier((coded(far1), coded(far3), g))
    got = [got2, shift_by_core(far1, 1, True), shift_by_core(far3, 3, True)]
    g_oth = shift(g, "c", 1)
    (own,) = hidden_part(pos, head5, g, (chunk(0),))
    head_out, loss = head_grad(pos, hidden, hidden_oth, g, g_oth)
    loss = loss[0, :1]
    *got, loss, head_out = lax.optimization_barrier((*got, loss, head_out))

    def summed(near):
        return own[near] + sum(taken(v[near]) for v in got)

    far2 = coded(summed(2))
    far2, own, *got = lax.optimization_barrier((far2, own, *got))
    far = [shift_by_core(coded(summed(d)), d, False) for d in (3, 1)]
    far += [shift_by_core(far2, 2, False)]
    both = coded(summed(0) + sum(taken(v) for v in far))
    both = lax.all_to_all(both, "z", 0, 0, tiled=True)
    hidden_grad = jnp.sum(taken(both), axis=0).T.astype(BF16)
    return loss, hidden_grad, head_out


def solution(mesh):
    ny, nzx, nc = mesh.devices.shape
    nx = 4
    fine = Mesh(mesh.devices.reshape(ny, nzx // nx, nx, nc), ("y", "z", "x", "c"))
    vocab = ("y", "z", "x")
    in_specs = (
        P(None, vocab + ("c",)),
        P("c", None),
        P(None, vocab),
        P("c"),
        P(),
        P("c"),
    )
    out_specs = (P(), P("c", vocab), P("c", vocab))
    return jax.shard_map(body, mesh=fine, in_specs=in_specs, out_specs=out_specs, check_vma=False)
```

```python
import functools

import jax
import jax.numpy as jnp
import numpy as np
from jax import lax
from jax.experimental import pallas as pl
from jax.experimental.pallas import tpu as pltpu
from jax.sharding import Mesh, PartitionSpec as P

CE_WEIGHT = 0.5
SEND_SCALE = 64.0
SPARE = 256
LOSS_ROWS = 16
F32 = jnp.float32
BF16 = jnp.bfloat16
F16 = jnp.float16


LIGHT = pl.CostEstimate(flops=1, bytes_accessed=1, transcendentals=0)
WHOLE = pl.BlockSpec(memory_space=pltpu.VMEM)


def params(mib, *semantics):
    return pltpu.CompilerParams(
        vmem_limit_bytes=mib * 1024 * 1024, dimension_semantics=semantics or None
    )


def shift(a, axis, by):
    n = lax.axis_size(axis)
    return lax.ppermute(a, axis, [(i, (i + by) % n) for i in range(n)])


def shift_by_core(a, by, first):
    axes = ("y", "z", "x", "c")
    shape = tuple(lax.axis_size(axis) for axis in axes)
    pairs = []
    for source in np.ndindex(shape):
        target = list(source)
        axis = 0 if (source[3] == 0) == first else 2
        target[axis] = (target[axis] + by) % shape[axis]
        pairs.append(tuple(int(np.ravel_multi_index(at, shape)) for at in (source, target)))
    return lax.ppermute(a, axes, pairs)


def logits_kernel(steps, h_ref, w_ref, out_ref, h_buf, w_buf, h_sem, w_sem):
    kb = w_buf.shape[1]

    def copies(k):
        at = pl.ds(k * kb, kb)
        return (
            pltpu.make_async_copy(h_ref.at[:, at], h_buf.at[k], h_sem.at[k]),
            pltpu.make_async_copy(w_ref.at[at], w_buf.at[k], w_sem.at[k]),
        )

    for k in range(steps):
        for copy in copies(k):
            copy.start()
    out_ref[...] = jnp.zeros_like(out_ref)

    def step(k, carry):
        for copy in copies(k):
            copy.wait()
        out_ref[...] += jnp.dot(h_buf[k], w_buf[k], preferred_element_type=F32)
        return carry

    lax.fori_loop(0, steps, step, 0)


def student_logits(hidden, head, steps=4):
    rows, depth = hidden.shape
    cols = head.shape[1]
    kb = depth // steps
    return pl.pallas_call(
        functools.partial(logits_kernel, steps),
        out_shape=jax.ShapeDtypeStruct((rows, cols), F32),
        in_specs=[pl.BlockSpec(memory_space=pl.ANY)] * 2,
        out_specs=WHOLE,
        scratch_shapes=[
            pltpu.VMEM((steps, rows, kb), BF16),
            pltpu.VMEM((steps, kb, cols), BF16),
            pltpu.SemaphoreType.DMA((steps,)),
            pltpu.SemaphoreType.DMA((steps,)),
        ],
        compiler_params=params(52),
        cost_estimate=pl.CostEstimate(
            flops=2 * rows * depth * cols,
            bytes_accessed=2 * (rows * depth + depth * cols) + 4 * rows * cols,
            transcendentals=0,
        ),
        name="student_logits",
    )(hidden, head)


def columns_of(*rows):
    n = rows[0].shape[1]
    sub = lax.broadcasted_iota(jnp.int32, (128, n), 0)
    packed = jnp.zeros((128, n), F32)
    for at, row in enumerate(rows):
        packed = jnp.where(sub == at, row.astype(F32), packed)
    turned = packed.T
    return [turned[:, at : at + 1] for at in range(len(rows))]


def in_row(ref):
    return jnp.concatenate([ref[i : i + 1, :] for i in range(ref.shape[0])], axis=1)


def pack_stats(out_ref, lse_s, lse_t, cross, picked):
    rows = lse_s.shape[1]
    spare = out_ref.shape[1] - rows
    far = 2 * rows - spare
    out_ref[0:1, :rows] = lse_s
    out_ref[1:2, :rows] = lse_t
    out_ref[0:1, rows:] = cross[:, :spare]
    out_ref[1:2, rows:far] = cross[:, spare:]
    lane = lax.broadcasted_iota(jnp.int32, (1, out_ref.shape[1] - far), 1)
    out_ref[1:2, far:] = jnp.where(lane == 0, picked, 0.0)


def logsumexp(values):
    top = jnp.max(values, axis=0, keepdims=True)
    return top + jnp.log(jnp.sum(jnp.exp(values - top), axis=0, keepdims=True))


def merge(first, second):
    rows = first.shape[1] - SPARE
    far = 2 * rows - SPARE
    lse_s = logsumexp(first[:, :rows])
    lse_t = logsumexp(second[:, :rows])
    share_t = jnp.exp(second[:, :rows] - lse_t)
    cross = jnp.concatenate([first[:, rows:], second[:, rows:far]], axis=1)
    cross = jnp.sum(cross * share_t, axis=0, keepdims=True)
    picked = jnp.sum(second[:, far:], axis=0, keepdims=True)
    return lse_s, lse_t, cross, jnp.sum(picked, axis=1, keepdims=True)


def merge_kernel(in_ref, out_ref):
    pack_stats(out_ref, *merge(in_ref[:, 0, :], in_ref[:, 1, :]))


def merge_stats(stats):
    return pl.pallas_call(
        merge_kernel,
        out_shape=jax.ShapeDtypeStruct(stats.shape[1:], F32),
        in_specs=[WHOLE],
        out_specs=WHOLE,
        compiler_params=params(16),
        name="merge_stats",
    )(stats)


def stats_kernel(
    pos_ref, l_ref, own_ref, oth_ref, assign_ref, ids_ref, stats_ref, t_ref, both_ref
):
    rows, cols = l_ref.shape
    half = cols // 2
    total = own_ref.shape[0]
    first = pos_ref[0] == 0
    assign = in_row(assign_ref)
    assign = jnp.where(first, assign[:, :rows], assign[:, rows:])
    assign, ids = columns_of(assign, in_row(ids_ref))
    lanes = lax.broadcasted_iota(jnp.int32, (rows, total), 1).astype(F32)
    pick = (lanes == assign).astype(BF16)
    both_ref[:, pl.ds(pl.multiple_of(pos_ref[0] * half, half), half)] = own_ref[...]
    both_ref[:, pl.ds(pl.multiple_of((1 - pos_ref[0]) * half, half), half)] = oth_ref[...]
    teacher = jnp.dot(pick, both_ref[...], preferred_element_type=F32)
    t_ref[...] = teacher.astype(BF16)
    logits = l_ref[...]
    top_s = jnp.max(logits, axis=1, keepdims=True)
    sum_s = jnp.sum(jnp.exp(logits - top_s), axis=1, keepdims=True)
    top_t = jnp.max(teacher, axis=1, keepdims=True)
    exp_t = jnp.exp(teacher - top_t)
    sum_t = jnp.sum(exp_t, axis=1, keepdims=True)
    cross = jnp.sum(exp_t * (teacher - logits), axis=1, keepdims=True)
    columns = pos_ref[1] + lax.broadcasted_iota(jnp.int32, (rows, cols), 1)
    hot = columns.astype(F32) == ids
    picked = jnp.sum(jnp.where(hot, logits, 0.0), axis=1, keepdims=True)
    lane = lax.broadcasted_iota(jnp.int32, (rows, 128), 1)
    packed = jnp.zeros((rows, 128), F32)
    for at, value in enumerate((top_s, sum_s, top_t, sum_t, cross, picked)):
        packed = jnp.where(lane == at, value, packed)
    packed = packed.T
    top_s, sum_s, top_t, sum_t, cross, picked = (packed[at : at + 1] for at in range(6))
    cross = cross / sum_t
    picked = jnp.sum(picked, axis=1, keepdims=True)
    pack_stats(stats_ref, top_s + jnp.log(sum_s), top_t + jnp.log(sum_t), cross, picked)


def local_stats(pos, logits, own, oth, assign, ids):
    rows, cols = logits.shape
    return pl.pallas_call(
        stats_kernel,
        out_shape=(
            jax.ShapeDtypeStruct((2, rows + SPARE), F32),
            jax.ShapeDtypeStruct((rows, cols), BF16),
        ),
        in_specs=[pl.BlockSpec(memory_space=pltpu.SMEM)] + [WHOLE] * 5,
        out_specs=(WHOLE, WHOLE),
        scratch_shapes=[pltpu.VMEM((own.shape[0], cols), BF16)],
        compiler_params=params(16),
        cost_estimate=pl.CostEstimate(
            flops=2 * rows * cols * own.shape[0],
            bytes_accessed=4 * rows * cols + 4 * own.size + 2 * rows * cols,
            transcendentals=2 * rows * cols,
        ),
        name="local_stats",
    )(pos, logits, own, oth, assign, ids)


def chunk(far):
    return tuple((far, near) for near in range(4))


def hidden_product(groups, pos_ref, w_ref, g, outs):
    ny, nz, nx, sub, cols = w_ref.shape
    x_first, y, x = pos_ref[0] == 1, pos_ref[2], pos_ref[3]

    def block(far, near):
        dx = jnp.where(x_first, far, near)
        dy = jnp.where(x_first, near, far)
        w = w_ref[lax.rem(y + dy, ny), :, lax.rem(x + dx, nx)]
        return w.reshape(nz * sub, cols)

    for names, out in zip(groups, outs):
        w = jnp.concatenate([block(*name) for name in names], axis=0)
        product = lax.dot_general(w, g, (((1,), (1,)), ((), ())), preferred_element_type=F32)
        out[...] = product.reshape(out.shape)


def hidden_kernel(groups, pos_ref, w_ref, g_ref, *outs):
    hidden_product(groups, pos_ref, w_ref, g_ref[: outs[0].shape[-1], :], outs)


def hidden_part(pos, head5, g, groups):
    nz, sub = head5.shape[1], head5.shape[3]
    rows = g.shape[0] - LOSS_ROWS
    out_shape = [jax.ShapeDtypeStruct((len(names), nz, sub, rows), F32) for names in groups]
    return pl.pallas_call(
        functools.partial(hidden_kernel, groups),
        out_shape=out_shape,
        in_specs=[pl.BlockSpec(memory_space=pltpu.SMEM), WHOLE, WHOLE],
        out_specs=[WHOLE] * len(out_shape),
        compiler_params=params(16),
        cost_estimate=LIGHT,
        name="hidden_part",
    )(pos, head5, g)


def grad_kernel(pos_ref, l_ref, t_ref, ids_ref, scale_ref, stats_ref, w_ref, g_ref, far_ref):
    rows, cols = l_ref.shape
    norm_s, norm_t, cross, picked = merge(stats_ref[:, 0, :], stats_ref[:, 1, :])
    terms = cross - norm_t + (1.0 + CE_WEIGHT) * norm_s
    terms = jnp.sum(terms, axis=1, keepdims=True) - CE_WEIGHT * picked
    high = terms.astype(BF16).astype(F32)
    middle = (terms - high).astype(BF16).astype(F32)
    low = terms - high - middle
    at = lax.broadcasted_iota(jnp.int32, (LOSS_ROWS, cols), 0)
    tail = jnp.where(at == 0, high, jnp.where(at == 1, middle, jnp.where(at == 2, low, 0.0)))
    g_ref[rows:, :] = tail.astype(BF16)
    norm_s, norm_t, ids, scale = columns_of(norm_s, norm_t, in_row(ids_ref), in_row(scale_ref))
    columns = pos_ref[1] + lax.broadcasted_iota(jnp.int32, (rows, cols), 1)
    hot = jnp.where(columns.astype(F32) == ids, CE_WEIGHT, 0.0)
    prob_s = jnp.exp(l_ref[...] - norm_s)
    prob_t = jnp.exp(t_ref[...].astype(F32) - norm_t)
    g = (scale * ((1.0 + CE_WEIGHT) * prob_s - prob_t - hot)).astype(BF16)
    g_ref[:rows, :] = g
    hidden_product((chunk(2),), pos_ref, w_ref, g, (far_ref,))


def grad_logits(pos, logits, teacher, ids, scale, stats, head5):
    rows, cols = logits.shape
    _, nz, _, sub, _ = head5.shape
    return pl.pallas_call(
        grad_kernel,
        out_shape=(
            jax.ShapeDtypeStruct((rows + LOSS_ROWS, cols), BF16),
            jax.ShapeDtypeStruct((4, nz, sub, rows), F32),
        ),
        in_specs=[pl.BlockSpec(memory_space=pltpu.SMEM)] + [WHOLE] * 6,
        out_specs=(WHOLE, WHOLE),
        compiler_params=params(16),
        cost_estimate=pl.CostEstimate(
            flops=8 * rows * cols,
            bytes_accessed=8 * rows * cols,
            transcendentals=2 * rows * cols,
        ),
        name="grad_logits",
    )(pos, logits, teacher, ids, scale, stats, head5)


def head_kernel(pos_ref, own_ref, oth_ref, g_own_ref, g_oth_ref, out_ref, loss_ref, buf, sem):
    steps, block, _ = buf.shape
    rows = own_ref.shape[0]
    g = jnp.concatenate([g_own_ref[:rows, :], g_oth_ref[:rows, :]], axis=0)
    copies = []
    for i in range(steps):
        at = pl.ds(pl.multiple_of(pos_ref[0] * (steps * block) + i * block, block), block)
        h = jnp.concatenate([own_ref[:, at], oth_ref[:, at]], axis=0)
        total = lax.dot_general(h, g, (((0,), (0,)), ((), ())), preferred_element_type=F32)
        buf[i] = total.astype(BF16)
        copy = pltpu.make_async_copy(buf.at[i], out_ref.at[pl.ds(i * block, block)], sem.at[i])
        copy.start()
        copies.append(copy)

    def loss(ref):
        parts = ref[rows:, :128].astype(F32)
        return (parts[0:1] + parts[1:2]) + parts[2:3]

    loss_ref[...] = (loss(g_own_ref) + loss(g_oth_ref)) * (1.0 / (2 * rows))
    for copy in copies:
        copy.wait()


def head_grad(pos, hidden, hidden_oth, g, g_oth, steps=2):
    rows, depth = hidden.shape
    cols = g.shape[1]
    width = depth // 2
    return pl.pallas_call(
        head_kernel,
        out_shape=(
            jax.ShapeDtypeStruct((width, cols), BF16),
            jax.ShapeDtypeStruct((1, 128), F32),
        ),
        in_specs=[pl.BlockSpec(memory_space=pltpu.SMEM)] + [WHOLE] * 4,
        out_specs=(pl.BlockSpec(memory_space=pl.ANY), WHOLE),
        scratch_shapes=[
            pltpu.VMEM((steps, width // steps, cols), BF16),
            pltpu.SemaphoreType.DMA((steps,)),
        ],
        compiler_params=params(20),
        cost_estimate=LIGHT,
        name="head_grad",
    )(pos, hidden, hidden_oth, g, g_oth)


def body(teacher, hidden, head, ids, assignment, row_scale):
    c, x, y = (lax.axis_index(a) for a in ("c", "x", "y"))
    rows, depth = hidden.shape
    cols = head.shape[1]
    chips = ("y", "z", "x")
    ny, nz, nx = (lax.axis_size(a) for a in chips)
    pos = jnp.stack([c, lax.axis_index(chips) * cols, y, x]).astype(jnp.int32)
    assign = assignment.reshape(-1, 128)
    ids = ids.reshape(-1, 128)
    scale = row_scale.reshape(-1, 128)

    teacher_oth = shift(teacher, "c", 1)
    logits = student_logits(hidden, head)
    stats, teacher_rows = local_stats(pos, logits, teacher, teacher_oth, assign, ids)
    stats, scale = lax.optimization_barrier((stats, scale))

    def gathered(value, axes, n):
        value = jnp.broadcast_to(value[None], (n,) + value.shape)
        return lax.all_to_all(value, axes, 0, 0, tiled=True)

    stats = merge_stats(gathered(stats, "z", nz))
    stats, hidden_far = lax.optimization_barrier((stats, hidden))
    hidden_oth = shift(hidden_far, "c", 1)
    stats = gathered(stats, ("y", "x"), ny * nx)
    head5 = head.reshape(ny, nz, nx, depth // (ny * nz * nx), cols)
    g, far2 = grad_logits(pos, logits, teacher_rows, ids, scale, stats, head5)

    def coded(value):
        return (value * SEND_SCALE).astype(F16)

    def taken(value):
        return value.astype(F32) * (1.0 / SEND_SCALE)

    far2, g = lax.optimization_barrier((coded(far2), g))
    got2 = shift_by_core(far2, 2, True)
    far1, far3 = hidden_part(pos, head5, g, (chunk(1), chunk(3)))
    far1, far3, g = lax.optimization_barrier((coded(far1), coded(far3), g))
    got = [got2, shift_by_core(far1, 1, True), shift_by_core(far3, 3, True)]
    g_oth = shift(g, "c", 1)
    (own,) = hidden_part(pos, head5, g, (chunk(0),))
    head_out, loss = head_grad(pos, hidden, hidden_oth, g, g_oth)
    loss = loss[0, :1]
    *got, loss, head_out = lax.optimization_barrier((*got, loss, head_out))

    def summed(near):
        return own[near] + sum(taken(v[near]) for v in got)

    far2 = coded(summed(2))
    far2, own, *got = lax.optimization_barrier((far2, own, *got))
    far = [shift_by_core(coded(summed(d)), d, False) for d in (3, 1)]
    far += [shift_by_core(far2, 2, False)]
    both = coded(summed(0) + sum(taken(v) for v in far))
    both = lax.all_to_all(both, "z", 0, 0, tiled=True)
    hidden_grad = jnp.sum(taken(both), axis=0).T.astype(BF16)
    return loss, hidden_grad, head_out


def solution(mesh):
    ny, nzx, nc = mesh.devices.shape
    nx = 4
    fine = Mesh(mesh.devices.reshape(ny, nzx // nx, nx, nc), ("y", "z", "x", "c"))
    vocab = ("y", "z", "x")
    in_specs = (
        P(None, vocab + ("c",)),
        P("c", None),
        P(None, vocab),
        P("c"),
        P(),
        P("c"),
    )
    out_specs = (P(), P("c", vocab), P("c", vocab))
    return jax.shard_map(body, mesh=fine, in_specs=in_specs, out_specs=out_specs, check_vma=False)
```

```python
import functools

import jax
import jax.numpy as jnp
import numpy as np
from jax import lax
from jax.experimental import pallas as pl
from jax.experimental.pallas import tpu as pltpu
from jax.sharding import Mesh, PartitionSpec as P

CE_WEIGHT = 0.5
SEND_SCALE = 64.0
SPARE = 256
LOSS_ROWS = 16
F32 = jnp.float32
BF16 = jnp.bfloat16
F16 = jnp.float16


LIGHT = pl.CostEstimate(flops=1, bytes_accessed=1, transcendentals=0)
WHOLE = pl.BlockSpec(memory_space=pltpu.VMEM)


def params(mib, *semantics):
    return pltpu.CompilerParams(
        vmem_limit_bytes=mib * 1024 * 1024, dimension_semantics=semantics or None
    )


def shift(a, axis, by):
    n = lax.axis_size(axis)
    return lax.ppermute(a, axis, [(i, (i + by) % n) for i in range(n)])


def shift_by_core(a, by, first):
    axes = ("y", "z", "x", "c")
    shape = tuple(lax.axis_size(axis) for axis in axes)
    pairs = []
    for source in np.ndindex(shape):
        target = list(source)
        axis = 2 if (source[3] == 0) == first else 0
        target[axis] = (target[axis] + by) % shape[axis]
        pairs.append(tuple(int(np.ravel_multi_index(at, shape)) for at in (source, target)))
    return lax.ppermute(a, axes, pairs)


def logits_kernel(steps, h_ref, w_ref, out_ref, h_buf, w_buf, h_sem, w_sem):
    kb = w_buf.shape[1]

    def copies(k):
        at = pl.ds(k * kb, kb)
        return (
            pltpu.make_async_copy(h_ref.at[:, at], h_buf.at[k], h_sem.at[k]),
            pltpu.make_async_copy(w_ref.at[at], w_buf.at[k], w_sem.at[k]),
        )

    for k in range(steps):
        for copy in copies(k):
            copy.start()
    out_ref[...] = jnp.zeros_like(out_ref)

    def step(k, carry):
        for copy in copies(k):
            copy.wait()
        out_ref[...] += jnp.dot(h_buf[k], w_buf[k], preferred_element_type=F32)
        return carry

    lax.fori_loop(0, steps, step, 0)


def student_logits(hidden, head, steps=4):
    rows, depth = hidden.shape
    cols = head.shape[1]
    kb = depth // steps
    return pl.pallas_call(
        functools.partial(logits_kernel, steps),
        out_shape=jax.ShapeDtypeStruct((rows, cols), F32),
        in_specs=[pl.BlockSpec(memory_space=pl.ANY)] * 2,
        out_specs=WHOLE,
        scratch_shapes=[
            pltpu.VMEM((steps, rows, kb), BF16),
            pltpu.VMEM((steps, kb, cols), BF16),
            pltpu.SemaphoreType.DMA((steps,)),
            pltpu.SemaphoreType.DMA((steps,)),
        ],
        compiler_params=params(52),
        cost_estimate=pl.CostEstimate(
            flops=2 * rows * depth * cols,
            bytes_accessed=2 * (rows * depth + depth * cols) + 4 * rows * cols,
            transcendentals=0,
        ),
        name="student_logits",
    )(hidden, head)


def columns_of(*rows):
    n = rows[0].shape[1]
    sub = lax.broadcasted_iota(jnp.int32, (128, n), 0)
    packed = jnp.zeros((128, n), F32)
    for at, row in enumerate(rows):
        packed = jnp.where(sub == at, row.astype(F32), packed)
    turned = packed.T
    return [turned[:, at : at + 1] for at in range(len(rows))]


def in_row(ref):
    return jnp.concatenate([ref[i : i + 1, :] for i in range(ref.shape[0])], axis=1)


def pack_stats(out_ref, lse_s, lse_t, cross, picked):
    rows = lse_s.shape[1]
    spare = out_ref.shape[1] - rows
    far = 2 * rows - spare
    out_ref[0:1, :rows] = lse_s
    out_ref[1:2, :rows] = lse_t
    out_ref[0:1, rows:] = cross[:, :spare]
    out_ref[1:2, rows:far] = cross[:, spare:]
    lane = lax.broadcasted_iota(jnp.int32, (1, out_ref.shape[1] - far), 1)
    out_ref[1:2, far:] = jnp.where(lane == 0, picked, 0.0)


def logsumexp(values):
    top = jnp.max(values, axis=0, keepdims=True)
    return top + jnp.log(jnp.sum(jnp.exp(values - top), axis=0, keepdims=True))


def merge(first, second):
    rows = first.shape[1] - SPARE
    far = 2 * rows - SPARE
    lse_s = logsumexp(first[:, :rows])
    lse_t = logsumexp(second[:, :rows])
    share_t = jnp.exp(second[:, :rows] - lse_t)
    cross = jnp.concatenate([first[:, rows:], second[:, rows:far]], axis=1)
    cross = jnp.sum(cross * share_t, axis=0, keepdims=True)
    picked = jnp.sum(second[:, far:], axis=0, keepdims=True)
    return lse_s, lse_t, cross, jnp.sum(picked, axis=1, keepdims=True)


def merge_kernel(in_ref, out_ref):
    pack_stats(out_ref, *merge(in_ref[:, 0, :], in_ref[:, 1, :]))


def merge_stats(stats):
    return pl.pallas_call(
        merge_kernel,
        out_shape=jax.ShapeDtypeStruct(stats.shape[1:], F32),
        in_specs=[WHOLE],
        out_specs=WHOLE,
        compiler_params=params(16),
        name="merge_stats",
    )(stats)


def stats_kernel(
    pos_ref, l_ref, own_ref, oth_ref, assign_ref, ids_ref, stats_ref, t_ref, both_ref
):
    rows, cols = l_ref.shape
    half = cols // 2
    total = own_ref.shape[0]
    first = pos_ref[0] == 0
    assign = in_row(assign_ref)
    assign = jnp.where(first, assign[:, :rows], assign[:, rows:])
    assign, ids = columns_of(assign, in_row(ids_ref))
    lanes = lax.broadcasted_iota(jnp.int32, (rows, total), 1).astype(F32)
    pick = (lanes == assign).astype(BF16)
    both_ref[:, pl.ds(pl.multiple_of(pos_ref[0] * half, half), half)] = own_ref[...]
    both_ref[:, pl.ds(pl.multiple_of((1 - pos_ref[0]) * half, half), half)] = oth_ref[...]
    teacher = jnp.dot(pick, both_ref[...], preferred_element_type=F32)
    t_ref[...] = teacher.astype(BF16)
    logits = l_ref[...]
    top_s = jnp.max(logits, axis=1, keepdims=True)
    sum_s = jnp.sum(jnp.exp(logits - top_s), axis=1, keepdims=True)
    top_t = jnp.max(teacher, axis=1, keepdims=True)
    exp_t = jnp.exp(teacher - top_t)
    sum_t = jnp.sum(exp_t, axis=1, keepdims=True)
    cross = jnp.sum(exp_t * (teacher - logits), axis=1, keepdims=True)
    columns = pos_ref[1] + lax.broadcasted_iota(jnp.int32, (rows, cols), 1)
    hot = columns.astype(F32) == ids
    picked = jnp.sum(jnp.where(hot, logits, 0.0), axis=1, keepdims=True)
    lane = lax.broadcasted_iota(jnp.int32, (rows, 128), 1)
    packed = jnp.zeros((rows, 128), F32)
    for at, value in enumerate((top_s, sum_s, top_t, sum_t, cross, picked)):
        packed = jnp.where(lane == at, value, packed)
    packed = packed.T
    top_s, sum_s, top_t, sum_t, cross, picked = (packed[at : at + 1] for at in range(6))
    cross = cross / sum_t
    picked = jnp.sum(picked, axis=1, keepdims=True)
    pack_stats(stats_ref, top_s + jnp.log(sum_s), top_t + jnp.log(sum_t), cross, picked)


def local_stats(pos, logits, own, oth, assign, ids):
    rows, cols = logits.shape
    return pl.pallas_call(
        stats_kernel,
        out_shape=(
            jax.ShapeDtypeStruct((2, rows + SPARE), F32),
            jax.ShapeDtypeStruct((rows, cols), BF16),
        ),
        in_specs=[pl.BlockSpec(memory_space=pltpu.SMEM)] + [WHOLE] * 5,
        out_specs=(WHOLE, WHOLE),
        scratch_shapes=[pltpu.VMEM((own.shape[0], cols), BF16)],
        compiler_params=params(16),
        cost_estimate=pl.CostEstimate(
            flops=2 * rows * cols * own.shape[0],
            bytes_accessed=4 * rows * cols + 4 * own.size + 2 * rows * cols,
            transcendentals=2 * rows * cols,
        ),
        name="local_stats",
    )(pos, logits, own, oth, assign, ids)


def chunk(far):
    return tuple((far, near) for near in range(4))


def hidden_product(groups, pos_ref, w_ref, g, outs):
    ny, nz, nx, sub, cols = w_ref.shape
    x_first, y, x = pos_ref[0] == 0, pos_ref[2], pos_ref[3]

    def block(far, near):
        dx = jnp.where(x_first, far, near)
        dy = jnp.where(x_first, near, far)
        w = w_ref[lax.rem(y + dy, ny), :, lax.rem(x + dx, nx)]
        return w.reshape(nz * sub, cols)

    for names, out in zip(groups, outs):
        w = jnp.concatenate([block(*name) for name in names], axis=0)
        product = lax.dot_general(w, g, (((1,), (1,)), ((), ())), preferred_element_type=F32)
        out[...] = product.reshape(out.shape)


def hidden_kernel(groups, pos_ref, w_ref, g_ref, *outs):
    hidden_product(groups, pos_ref, w_ref, g_ref[: outs[0].shape[-1], :], outs)


def hidden_part(pos, head5, g, groups):
    nz, sub = head5.shape[1], head5.shape[3]
    rows = g.shape[0] - LOSS_ROWS
    out_shape = [jax.ShapeDtypeStruct((len(names), nz, sub, rows), F32) for names in groups]
    return pl.pallas_call(
        functools.partial(hidden_kernel, groups),
        out_shape=out_shape,
        in_specs=[pl.BlockSpec(memory_space=pltpu.SMEM), WHOLE, WHOLE],
        out_specs=[WHOLE] * len(out_shape),
        compiler_params=params(16),
        cost_estimate=LIGHT,
        name="hidden_part",
    )(pos, head5, g)


def grad_kernel(pos_ref, l_ref, t_ref, ids_ref, scale_ref, stats_ref, w_ref, g_ref, far_ref):
    rows, cols = l_ref.shape
    norm_s, norm_t, cross, picked = merge(stats_ref[:, 0, :], stats_ref[:, 1, :])
    terms = cross - norm_t + (1.0 + CE_WEIGHT) * norm_s
    terms = jnp.sum(terms, axis=1, keepdims=True) - CE_WEIGHT * picked
    high = terms.astype(BF16).astype(F32)
    middle = (terms - high).astype(BF16).astype(F32)
    low = terms - high - middle
    at = lax.broadcasted_iota(jnp.int32, (LOSS_ROWS, cols), 0)
    tail = jnp.where(at == 0, high, jnp.where(at == 1, middle, jnp.where(at == 2, low, 0.0)))
    g_ref[rows:, :] = tail.astype(BF16)
    norm_s, norm_t, ids, scale = columns_of(norm_s, norm_t, in_row(ids_ref), in_row(scale_ref))
    columns = pos_ref[1] + lax.broadcasted_iota(jnp.int32, (rows, cols), 1)
    hot = jnp.where(columns.astype(F32) == ids, CE_WEIGHT, 0.0)
    prob_s = jnp.exp(l_ref[...] - norm_s)
    prob_t = jnp.exp(t_ref[...].astype(F32) - norm_t)
    g = (scale * ((1.0 + CE_WEIGHT) * prob_s - prob_t - hot)).astype(BF16)
    g_ref[:rows, :] = g
    hidden_product((chunk(2),), pos_ref, w_ref, g, (far_ref,))


def grad_logits(pos, logits, teacher, ids, scale, stats, head5):
    rows, cols = logits.shape
    _, nz, _, sub, _ = head5.shape
    return pl.pallas_call(
        grad_kernel,
        out_shape=(
            jax.ShapeDtypeStruct((rows + LOSS_ROWS, cols), BF16),
            jax.ShapeDtypeStruct((4, nz, sub, rows), F32),
        ),
        in_specs=[pl.BlockSpec(memory_space=pltpu.SMEM)] + [WHOLE] * 6,
        out_specs=(WHOLE, WHOLE),
        compiler_params=params(16),
        cost_estimate=pl.CostEstimate(
            flops=8 * rows * cols,
            bytes_accessed=8 * rows * cols,
            transcendentals=2 * rows * cols,
        ),
        name="grad_logits",
    )(pos, logits, teacher, ids, scale, stats, head5)


def head_kernel(pos_ref, own_ref, oth_ref, g_own_ref, g_oth_ref, out_ref, loss_ref, buf, sem):
    steps, block, _ = buf.shape
    rows = own_ref.shape[0]
    g = jnp.concatenate([g_own_ref[:rows, :], g_oth_ref[:rows, :]], axis=0)
    copies = []
    for i in range(steps):
        at = pl.ds(pl.multiple_of(pos_ref[0] * (steps * block) + i * block, block), block)
        h = jnp.concatenate([own_ref[:, at], oth_ref[:, at]], axis=0)
        total = lax.dot_general(h, g, (((0,), (0,)), ((), ())), preferred_element_type=F32)
        buf[i] = total.astype(BF16)
        copy = pltpu.make_async_copy(buf.at[i], out_ref.at[pl.ds(i * block, block)], sem.at[i])
        copy.start()
        copies.append(copy)

    def loss(ref):
        parts = ref[rows:, :128].astype(F32)
        return (parts[0:1] + parts[1:2]) + parts[2:3]

    loss_ref[...] = (loss(g_own_ref) + loss(g_oth_ref)) * (1.0 / (2 * rows))
    for copy in copies:
        copy.wait()


def head_grad(pos, hidden, hidden_oth, g, g_oth, steps=2):
    rows, depth = hidden.shape
    cols = g.shape[1]
    width = depth // 2
    return pl.pallas_call(
        head_kernel,
        out_shape=(
            jax.ShapeDtypeStruct((width, cols), BF16),
            jax.ShapeDtypeStruct((1, 128), F32),
        ),
        in_specs=[pl.BlockSpec(memory_space=pltpu.SMEM)] + [WHOLE] * 4,
        out_specs=(pl.BlockSpec(memory_space=pl.ANY), WHOLE),
        scratch_shapes=[
            pltpu.VMEM((steps, width // steps, cols), BF16),
            pltpu.SemaphoreType.DMA((steps,)),
        ],
        compiler_params=params(20),
        cost_estimate=LIGHT,
        name="head_grad",
    )(pos, hidden, hidden_oth, g, g_oth)


def body(teacher, hidden, head, ids, assignment, row_scale):
    c, x, y = (lax.axis_index(a) for a in ("c", "x", "y"))
    rows, depth = hidden.shape
    cols = head.shape[1]
    chips = ("y", "z", "x")
    ny, nz, nx = (lax.axis_size(a) for a in chips)
    pos = jnp.stack([c, lax.axis_index(chips) * cols, y, x]).astype(jnp.int32)
    assign = assignment.reshape(-1, 128)
    ids = ids.reshape(-1, 128)
    scale = row_scale.reshape(-1, 128)

    teacher_oth = shift(teacher, "c", 1)
    logits = student_logits(hidden, head)
    stats, teacher_rows = local_stats(pos, logits, teacher, teacher_oth, assign, ids)
    stats, scale = lax.optimization_barrier((stats, scale))

    def gathered(value, axes, n):
        value = jnp.broadcast_to(value[None], (n,) + value.shape)
        return lax.all_to_all(value, axes, 0, 0, tiled=True)

    stats = merge_stats(gathered(stats, "z", nz))
    stats, hidden_far = lax.optimization_barrier((stats, hidden))
    hidden_oth = shift(hidden_far, "c", 1)
    stats = gathered(stats, ("y", "x"), ny * nx)
    head5 = head.reshape(ny, nz, nx, depth // (ny * nz * nx), cols)
    g, far2 = grad_logits(pos, logits, teacher_rows, ids, scale, stats, head5)

    def coded(value):
        return (value * SEND_SCALE).astype(F16)

    def taken(value):
        return value.astype(F32) * (1.0 / SEND_SCALE)

    far2, g = lax.optimization_barrier((coded(far2), g))
    got2 = shift_by_core(far2, 2, True)
    far1, far3 = hidden_part(pos, head5, g, (chunk(1), chunk(3)))
    far1, far3, g = lax.optimization_barrier((coded(far1), coded(far3), g))
    got = [got2, shift_by_core(far1, 1, True), shift_by_core(far3, 3, True)]
    g_oth = shift(g, "c", 1)
    (own,) = hidden_part(pos, head5, g, (chunk(0),))
    head_out, loss = head_grad(pos, hidden, hidden_oth, g, g_oth)
    loss = loss[0, :1]
    *got, loss, head_out = lax.optimization_barrier((*got, loss, head_out))

    def summed(near):
        return own[near] + sum(taken(v[near]) for v in got)

    far2 = coded(summed(2))
    far2, own, *got = lax.optimization_barrier((far2, own, *got))
    far = [shift_by_core(coded(summed(d)), d, False) for d in (3, 1)]
    far += [shift_by_core(far2, 2, False)]
    both = coded(summed(0) + sum(taken(v) for v in far))
    both = lax.all_to_all(both, "z", 0, 0, tiled=True)
    hidden_grad = jnp.sum(taken(both), axis=0).T.astype(BF16)
    return loss, hidden_grad, head_out


def solution(mesh):
    ny, nzx, nc = mesh.devices.shape
    nx = 4
    fine = Mesh(mesh.devices.reshape(ny, nzx // nx, nx, nc), ("y", "z", "x", "c"))
    vocab = ("y", "z", "x")
    in_specs = (
        P(None, vocab + ("c",)),
        P("c", None),
        P(None, vocab),
        P("c"),
        P(),
        P("c"),
    )
    out_specs = (P(), P("c", vocab), P("c", vocab))
    return jax.shard_map(body, mesh=fine, in_specs=in_specs, out_specs=out_specs, check_vma=False)
```
